32 devices in a mesh: out: 4 (over y, x), blk: 8 (over z, core).
Axes of the slice: x: 2, y: 2, z: 4, core: 2. Of those that a mesh axis runs over, the one named last changes fastest.
Arguments:
- checkpoints: bfloat16 [4, 5, 128, 1024], P('out', None, None, 'blk'), may hold values from -4 to 4
- owner: int32 [4], replicated, may hold values from 0 to 3, each once
- flux_matrix: float32 [5, 5], replicated, may hold values from -2.5 to 2.5
- row_link: int32 [8, 128], P('blk'), may hold values from 0 to 127, each once within a row
- blade_group: int32 [96], replicated, may hold values from 0 to 7
- forcing: float32 [5, 128, 1024], P(None, None, 'blk'), may hold values from -6 to 6
Outputs:
- adjoint: float32 [8, 4, 5, 128, 1024], P('out', None, None, None, 'blk')
- sensitivity: float32 [8, 4], P('out')
The draws below stay inside these ranges and needn't reach their ends.
Inputs may be any that keep to these rules, and one draw needn't show every extreme that they name: Each tile's row_link is a permutation of its rows.
All inputs are finite; a program needn't handle non-finite values.
Results may differ from the reference program's by a relative error of at most 0.0003.
Values may be sent and summed in bfloat16 or wider, within the bound.
No kernel may reach another device: no remote copies, remote signals or barrier semaphores. Data moves between devices by JAX's collectives and lax.ppermute only.
A program may use at most 128 MiB of HBM per device.

```python
import math
import jax
import jax.numpy as jnp
from jax import lax

FIELDS = 5
BLADES = 96
AMP = 4
STEPS = 3
R = 128
CW = 128
GROUPS = 8
TILES = 8
NC = 1024
N_OUT = 4


def plant(values, key, smallest, top_value):
    index_at = [jax.random.randint(jax.random.fold_in(key, axis), (), 0, length) for axis, length in enumerate(values.shape)]
    main_axis = values.shape.index(max(values.shape))
    beside = index_at[:main_axis] + [(index_at[main_axis] + 1) % values.shape[main_axis]] + index_at[main_axis + 1:]
    return values.at[tuple(index_at)].set(smallest).at[tuple(beside)].set(top_value)


def block_scale(stream_key, shape, split, low, high):
    factor_of = 1.0
    for dim, parts in split:
        draws = jax.random.uniform(jax.random.fold_in(jax.random.fold_in(stream_key, 6), dim), (parts,), jnp.float32, low / len(split), high / len(split))
        factor_of = factor_of * jnp.repeat(jnp.exp(draws), shape[dim] // parts).reshape((-1,) + (1,) * (len(shape) - 1 - dim))
    return factor_of


def centred(rng, shape, spread, bound, split=(), kind=jnp.bfloat16):
    drawn = spread * jax.random.normal(rng, shape, jnp.float32)
    if split:
        drawn = drawn * block_scale(rng, shape, split, -0.22, 0.18)
    return jnp.clip(drawn, -bound, bound).astype(kind)


def setup_inputs(seed: int = 0) -> dict:
    arg_keys = jax.random.split(jax.random.key(seed), 7)
    return {
        "checkpoints": centred(arg_keys[0], (N_OUT, FIELDS, R, NC), 1.0, 4.0, ((0, 4), (3, 8))),
        "owner": jax.random.permutation(arg_keys[1], N_OUT).astype(jnp.int32),
        "flux_matrix": centred(arg_keys[2], (FIELDS, FIELDS), FIELDS ** -0.5, 2.5, (), jnp.float32),
        "row_link": jax.vmap(lambda own: jax.random.permutation(own, R))(jax.random.split(arg_keys[3], TILES)).reshape((TILES, R)).astype(jnp.int32),
        "blade_group": plant(jax.random.randint(arg_keys[4], (BLADES,), 0, GROUPS), jax.random.fold_in(arg_keys[4], 1), 0, GROUPS - 1).astype(jnp.int32),
        "forcing": centred(arg_keys[5], (FIELDS, R, NC), 1.0, 6.0, ((2, 8),), jnp.float32),
    }


time_step = 0.25
second_diff = 0.1
fourth_diff = 0.02
link_weight = 0.5
two_pi = 2.0 * math.pi

def transposed(mu, state, flux_matrix, inverse):
    plus_one = jnp.roll(mu, -1, axis=-1)
    minus_one = jnp.roll(mu, 1, axis=-1)
    plus_two = jnp.roll(mu, -2, axis=-1)
    minus_two = jnp.roll(mu, 2, axis=-1)
    diff = (minus_one - plus_one) * 0.5
    velocity = state[1]
    flux_part = jnp.einsum('fe,afrc->aerc', flux_matrix, diff, precision=lax.Precision.HIGHEST)
    inner = lax.optimization_barrier(jnp.sum(state[None] * diff, axis=1, keepdims=True))
    is_velocity = (jnp.arange(FIELDS) == 1).astype(jnp.float32)[None, :, None, None]
    jac = flux_part + 0.5 * velocity[None, None] * diff + 0.5 * is_velocity * inner
    lapl = plus_one - 2.0 * mu + minus_one
    quart = plus_two - 4.0 * plus_one + 6.0 * mu - 4.0 * minus_one + minus_two
    tiled = mu.reshape(AMP, FIELDS, R, TILES, CW)
    index = inverse.T.astype(jnp.int32)[None, None, :, :, None]
    linked = jnp.take_along_axis(tiled, index, axis=2).reshape(mu.shape)
    rows_part = mu - linked
    return mu - time_step * (jac - second_diff * lapl + fourth_diff * quart + link_weight * rows_part)

def reference(checkpoints, owner, flux_matrix, row_link, blade_group, forcing):
    total = NC
    column = jnp.arange(total, dtype=jnp.int32)
    scaled = column * BLADES
    blade_of = scaled // total
    phase = (scaled % total).astype(jnp.float32) / total
    group_of = blade_group[blade_of]
    amp_index = jnp.arange(AMP, dtype=jnp.int32)
    order = (amp_index // 2 + 1).astype(jnp.float32)
    angle = two_pi * order[:, None] * phase[None, :]
    harmonic = jnp.where((amp_index % 2 == 0)[:, None], jnp.cos(angle), jnp.sin(angle))
    weight_col = 1.0 + 2.0 * column.astype(jnp.float32) / total
    norm_scale = 1.0 / math.sqrt(FIELDS * R * total)
    inverse = jnp.argsort(row_link, axis=1).astype(jnp.int32)
    states = [checkpoints[owner[step]].astype(jnp.float32) for step in range(STEPS)]
    weighted = forcing * weight_col[None, None, :]

    def one_group(group):
        member = (group_of == group).astype(jnp.float32)
        source_term = forcing[None] * (member[None, :] * harmonic)[:, None, None, :]
        adjoint = jnp.zeros((AMP, FIELDS, R, total), jnp.float32)
        sens = jnp.zeros((AMP,), jnp.float32)
        for step in reversed(range(STEPS)):
            adjoint = transposed(adjoint + source_term, states[step], flux_matrix, inverse)
            sens = sens + lax.optimization_barrier(jnp.sum(adjoint * weighted[None], axis=(1, 2, 3))) * norm_scale
        return (adjoint, sens)
    adjoints, sensitivity = lax.map(one_group, jnp.arange(GROUPS, dtype=jnp.int32))
    return (adjoints, sensitivity)
```

```python
import functools
import math

import jax
import jax.numpy as jnp
import numpy as np
from jax import lax
from jax.experimental import pallas as pl
from jax.experimental.pallas import tpu as pltpu
from jax.sharding import PartitionSpec as P

FIELDS = 5
BLADES = 96
AMP = 4
GRP_DEV = 2
STEPS = 3
PAIRS = GRP_DEV * AMP

time_step = 0.25
second_diff = 0.1
fourth_diff = 0.02
link_weight = 0.5
two_pi = 2.0 * math.pi

C0 = 1.0 - time_step * (2.0 * second_diff + 6.0 * fourth_diff + link_weight)
C1 = time_step * (second_diff + 4.0 * fourth_diff)
C2 = -time_step * fourth_diff
CP = time_step * link_weight
CM = 0.5 * time_step
CU = 0.25 * time_step

FW = 6
QW = 4
PARTS = 3
SLOT = 32
QROW = PARTS * FW
LINK_ROW = QROW + STEPS * QW
QS_ROWS = 48
SEG = 16
HALF = SEG // 2

VMEM = pl.BlockSpec(memory_space=pltpu.VMEM)
SMEM = pl.BlockSpec(memory_space=pltpu.SMEM)
HBM = pl.BlockSpec(memory_space=pl.ANY)
F32 = jnp.float32
BF16 = jnp.bfloat16
NT = (((1,), (1,)), ((), ()))
TN = (((0,), (0,)), ((), ()))
NN = (((1,), (0,)), ((), ()))


def mm(a, b, dims=NN):
    return lax.dot_general(a, b, dims, preferred_element_type=F32)


def split3(x):
    hi = x.astype(BF16)
    rest = x - hi.astype(F32)
    mid = rest.astype(BF16)
    return hi, mid, (rest - mid.astype(F32)).astype(BF16)


def exact_mm(a, x):
    hi, mid, lo = split3(x)
    return mm(a, hi) + mm(a, mid) + mm(a, lo)


def q_select(width):
    out = np.zeros((FIELDS, QS_ROWS, width), np.float32)
    for f in range(FIELDS):
        for j in range(QW):
            out[f, f * 8 + j, j] = 1.0
            out[f, f * 8 + QW + j, width - QW + j] = 1.0
    return out.astype(jnp.bfloat16)


def q_edges_kernel(ck_ref, sel_ref, out_ref):
    total = None
    for f in range(FIELDS):
        part = mm(sel_ref[f], ck_ref[f], NT)
        total = part if total is None else total + part
    out_ref[...] = total.astype(BF16)


def strip_selects(width):
    forcing_sel = np.zeros((PARTS, 2 * SLOT, width), np.float32)
    for part in range(PARTS):
        for j in range(FW):
            forcing_sel[part, part * FW + j, j] = 1.0
            forcing_sel[part, SLOT + part * FW + j, width - FW + j] = 1.0
    place = np.zeros((FIELDS, 2 * SLOT, STEPS * QS_ROWS), np.float32)
    for f in range(FIELDS):
        for n in range(STEPS):
            for j in range(QW):
                place[f, QROW + n * QW + j, n * QS_ROWS + f * 8 + j] = 1.0
                place[f, SLOT + QROW + n * QW + j, n * QS_ROWS + f * 8 + QW + j] = 1.0
    return forcing_sel.astype(jnp.bfloat16), place.astype(jnp.bfloat16)


def pick(values, index):
    out = values[0]
    for k in range(1, len(values)):
        out = jnp.where(index == k, values[k], out)
    return out


def strips_kernel(n_out, *refs):
    pos, owner, *qs = refs[: 2 + n_out]
    forcing, link, fsel, place, send_a, send_b = refs[2 + n_out :]
    me = pos[0]
    even = pos[1] % 2 == 0
    edges = [q[...].astype(F32) for q in qs]
    chosen = jnp.concatenate(
        [pick(edges, (me - owner[n] + n_out) % n_out) for n in range(STEPS)], axis=0
    ).astype(BF16)
    row = lax.broadcasted_iota(jnp.int32, (2 * SLOT, link.shape[1]), 0)
    links = jnp.broadcast_to(link[...].astype(F32), row.shape)
    for f in range(FIELDS):
        both = mm(place[f], chosen)
        for sel, part in zip(range(PARTS), split3(forcing[f])):
            both = both + mm(fsel[sel], part, NT)
        if f == 0:
            both = jnp.where(row % SLOT == LINK_ROW, links, both)
        left, right = both[:SLOT], both[SLOT:]
        send_a[f * SLOT : (f + 1) * SLOT] = jnp.where(even, right, left).astype(BF16)
        send_b[f * SLOT : (f + 1) * SLOT] = jnp.where(even, left, right).astype(BF16)


def halo_select(width):
    shifts = (-2, -1, 0, 1, 2)
    out = np.zeros((4 * SLOT, 8, width), np.float32)

    def forcing_rows(column):
        if column < 0:
            source, j = 0, column + FW
        elif column < FW:
            source, j = 1, column
        elif column < width:
            source, j = 2, column - (width - FW)
        else:
            source, j = 3, column - width
        return [source * SLOT + part * FW + j for part in range(PARTS)] if 0 <= j < FW else []

    def q_row(column, n):
        if column < 0:
            source, j = 0, column + QW
        elif column < QW:
            source, j = 1, column
        elif column < width:
            source, j = 2, column - (width - QW)
        else:
            source, j = 3, column - width
        return source * SLOT + QROW + n * QW + j

    for pair in range(PAIRS):
        for p in range(SEG):
            lane = pair * SEG + p
            column = p - QW if p < HALF else width - QW + p - HALF
            for i, d in enumerate(shifts):
                for row in forcing_rows(column + d):
                    out[row, i, lane] = 1.0
            out[q_row(column, STEPS - 1), 5, lane] = 1.0
            out[q_row(column, STEPS - 2), 6, lane] = 1.0
    for lane, column in ((width - 2, -2), (width - 1, -1), (0, width), (1, width + 1)):
        for row in forcing_rows(column):
            out[row, 7, lane] = 1.0
    return out.reshape(4 * SLOT, 8 * width).astype(jnp.bfloat16)


def column_factor(columns, pair, start, total, group_base, blade_group):
    scaled = columns * BLADES
    first = ((start + total - HALF) * BLADES) // total - BLADES
    group = jnp.full(columns.shape, -1, jnp.int32)
    numerator = jnp.zeros(columns.shape, jnp.int32)
    width = columns.shape[-1]
    for j in range((width + SEG) * BLADES // total + 2):
        blade = first + j
        inside = (scaled >= blade * total) & (scaled < (blade + 1) * total)
        group = jnp.where(inside, blade_group[(blade + BLADES) % BLADES], group)
        numerator = jnp.where(inside, scaled - blade * total, numerator)
    phase = numerator.astype(F32) / total
    amp = pair & (AMP - 1)
    order = ((amp >> 1) + 1).astype(F32)
    angle = two_pi * order * phase
    harmonic = jnp.where((amp & 1) == 0, jnp.cos(angle), jnp.sin(angle))
    return jnp.where(group == group_base + pair // AMP, harmonic, 0.0)


def flux(fm, q, d):
    inner = q[0] * d[0]
    for f in range(1, FIELDS):
        inner = inner + q[f] * d[f]
    u = q[1] * CU
    out = []
    for e in range(FIELDS):
        value = u * d[e]
        for f in range(FIELDS):
            value = value + fm[f, e] * d[f]
        if e == 1:
            value = value + CU * inner
        out.append(value)
    return out


def halo_kernel(
    cycle, pos, fm, blade_group, link_s, send_a, send_b, recv_a, recv_b, forcing, link_v, sel,
    h1_ref, h2_ref, b0_ref, fe_ref, k_ref, inv_ref, fmc,
):
    width, rows = forcing.shape[2], forcing.shape[1]
    even = pos[1] % 2 == 0
    start = pos[1] * width
    total = cycle * width

    def invert(r, c):
        inv_ref[link_s[r]] = r
        return c

    lax.fori_loop(0, rows, invert, 0, unroll=8)

    for f in range(FIELDS):
        for e in range(FIELDS):
            fmc[f, e] = fm[f, e] * CM

    lane = lax.broadcasted_iota(jnp.int32, (8, width), 1)
    sub = lax.broadcasted_iota(jnp.int32, (8, width), 0)
    pair = PAIRS - 1 - lane // SEG
    p = lane & (SEG - 1)
    packed = jnp.where(p < HALF, p - QW, width - QW + p - HALF) + start
    args = (start, total, pos[0] * GRP_DEV, blade_group)
    kp = column_factor(packed + sub - 2, pair, *args)
    for i in range(5):
        k_ref[i] = column_factor(lane + start + (i - 2), sub, *args)

    sa, sb = send_a[...].astype(F32), send_b[...].astype(F32)
    ra, rb = recv_a[...].astype(F32), recv_b[...].astype(F32)
    own_left, own_right = jnp.where(even, sb, sa), jnp.where(even, sa, sb)
    left, right = jnp.where(even, rb, ra), jnp.where(even, ra, rb)
    row = lax.broadcasted_iota(jnp.int32, (rows, rows), 0).astype(F32)

    def hot(links):
        return jnp.where(links == row, 1.0, 0.0).astype(BF16)

    hot_own = hot(link_v[...].astype(F32))
    hot_left = hot(left[LINK_ROW : LINK_ROW + 1])
    hot_right = hot(right[LINK_ROW : LINK_ROW + 1])
    picked = []
    for f in range(FIELDS):
        s = slice(f * SLOT, (f + 1) * SLOT)
        g = jnp.concatenate([left[s], own_left[s], own_right[s], right[s]], axis=0)
        g = g.T.astype(BF16)
        x = mm(g, sel[...])
        picked.append([x[:, i * width : (i + 1) * width] for i in range(8)])
        fe_ref[f] = picked[f][7]
        b0_ref[f] = (C0 + 1.0) * forcing[f] + CP * exact_mm(hot_own, forcing[f])

    big_lane = lax.broadcasted_iota(jnp.int32, (rows, width), 1) & (SEG - 1)
    is_left = big_lane < HALF
    is_own = (big_lane >= QW) & (big_lane < SEG - QW)

    def permuted(x):
        outer = jnp.where(is_left, exact_mm(hot_left, x), exact_mm(hot_right, x))
        return jnp.where(is_own, exact_mm(hot_own, x), outer)

    def finish(x):
        return jnp.where(big_lane < QW, x, pltpu.roll(x, width - HALF, 1))

    shifted = [[picked[f][i] for f in range(FIELDS)] for i in range(5)]
    q2 = [picked[f][5] for f in range(FIELDS)]
    plus = flux(fmc, q2, shifted[3])
    minus = flux(fmc, q2, shifted[1])
    mu1 = []
    for f in range(FIELDS):
        b = [
            C2 * shifted[0][f],
            C1 * shifted[1][f] - minus[f],
            (C0 + 1.0) * shifted[2][f] + CP * permuted(shifted[2][f]),
            C1 * shifted[3][f] + plus[f],
            C2 * shifted[4][f],
        ]
        value = b[0] * kp[0:1]
        for i in range(1, 5):
            value = value + b[i] * kp[i : i + 1]
        mu1.append(value)
    q1 = [picked[f][6] for f in range(FIELDS)]
    m1 = [pltpu.roll(x, 1, 1) for x in mu1]
    p1 = [pltpu.roll(x, width - 1, 1) for x in mu1]
    m2 = [pltpu.roll(x, 2, 1) for x in mu1]
    p2 = [pltpu.roll(x, width - 2, 1) for x in mu1]
    part = flux(fmc, q1, [a - b for a, b in zip(m1, p1)])
    for f in range(FIELDS):
        value = C0 * mu1[f] + C1 * (m1[f] + p1[f]) + C2 * (m2[f] + p2[f])
        value = value + CP * permuted(mu1[f]) - part[f]
        value = value + shifted[2][f] * kp[2:3]
        h1_ref[f] = finish(mu1[f])
        h2_ref[f] = finish(value)


def main_kernel(n_out, cycle, *refs):
    pos, owner, fm, inv = refs[:4]
    slots = refs[4 : 4 + n_out]
    forcing, b0, fe, h1, h2, k_ref = refs[4 + n_out : 10 + n_out]
    out_hbm, sens_ref = refs[10 + n_out : 12 + n_out]
    bs, coef, mu1, mu2, stage, weighted, fmc, sem = refs[12 + n_out :]
    rows, width = forcing.shape[1], forcing.shape[2]
    me = pos[0]
    total = cycle * width

    for f in range(FIELDS):
        for e in range(FIELDS):
            fmc[f, e] = fm[f, e] * CM
    which = [(me - owner[n] + n_out) % n_out for n in range(STEPS)]
    lane = lax.broadcasted_iota(jnp.int32, (8, width), 1)
    weight = 1.0 + 2.0 * (lane + pos[1] * width).astype(F32) / total
    norm = 1.0 / math.sqrt(FIELDS * rows * total)

    def states(n, rs):
        return [pick([s[f, rs, :].astype(F32) for s in slots], which[n]) for f in range(FIELDS)]

    def around(x, edge):
        return (
            pltpu.roll(jnp.where(lane == width - 1, edge, x), 1, 1),
            pltpu.roll(jnp.where(lane == 0, edge, x), width - 1, 1),
            pltpu.roll(jnp.where(lane >= width - 2, edge, x), 2, 1),
            pltpu.roll(jnp.where(lane < 2, edge, x), width - 2, 1),
        )

    def dense(i, z):
        rs = pl.ds(pl.multiple_of(i * 16, 16), 16)
        for n in range(STEPS - 1):
            q = states(n, rs)
            u = CU * q[1]
            for e in range(FIELDS):
                coef[n, e, rs, :] = (u if e != 1 else u + u) + fmc[e, e]
            for j, f in enumerate((0, 2, 3, 4)):
                coef[n, FIELDS + j, rs, :] = CU * q[f] + fmc[f, 1]
        for half in range(2):
            r8 = pl.ds(pl.multiple_of(i * 16 + half * 8, 8), 8)
            q = [pick([s[f, rs, :].astype(F32) for s in slots], which[STEPS - 1])[half * 8 : half * 8 + 8] for f in range(FIELDS)]
            near = [around(forcing[f, r8, :], fe[f, r8, :]) for f in range(FIELDS)]
            minus = flux(fmc, q, [a[0] for a in near])
            plus = flux(fmc, q, [a[1] for a in near])
            for f in range(FIELDS):
                m1, p1, m2, p2 = near[f]
                bs[0, f, r8, :] = C2 * m2
                bs[1, f, r8, :] = C1 * m1 - minus[f]
                bs[2, f, r8, :] = C1 * p1 + plus[f]
                bs[3, f, r8, :] = C2 * p2
                w = forcing[f, r8, :] * weight
                weighted[f, r8, :] = w
                z = z + w * forcing[f, r8, :]
        return z

    zero = jnp.zeros((8, width), F32)
    z = lax.fori_loop(0, rows // 16, dense, zero)
    k = [k_ref[i] for i in range(5)]

    def spread(ref, index, r):
        return jnp.broadcast_to(ref[(*index, pl.ds(r, 1), slice(None))], (8, width))

    def first(r, acc):
        for f in range(FIELDS):
            value = spread(bs, (0, f), r) * k[0] + spread(bs, (1, f), r) * k[1]
            value = value + spread(b0, (f,), r) * k[2] + spread(bs, (2, f), r) * k[3]
            value = value + spread(bs, (3, f), r) * k[4]
            mu1[r, f] = value
            acc = acc + value * spread(weighted, (f,), r)
        return acc

    acc = lax.fori_loop(0, rows, first, zero, unroll=4)

    def step(n, source, edges, r):
        linked = inv[r]
        center = [source[r, f] for f in range(FIELDS)]
        d, base = [], []
        for f in range(FIELDS):
            seg = spread(edges, (f,), r)
            edge = pltpu.roll(seg, SEG - 4, 1, stride=SEG, stride_axis=0)
            m1, p1, m2, p2 = around(center[f], edge)
            d.append(m1 - p1)
            base.append(
                C0 * center[f] + C1 * (m1 + p1) + C2 * (m2 + p2) + CP * source[linked, f]
            )
        result = []
        for e in range(FIELDS):
            value = base[e] - spread(coef, (n, e), r) * d[e]
            for f in range(FIELDS):
                if f == e:
                    continue
                if e == 1:
                    m = spread(coef, (n, FIELDS + (0, 2, 3, 4).index(f)), r)
                else:
                    m = fmc[f, e]
                value = value - m * d[f]
            result.append(value)
        return result

    def second(r, acc):
        for f, value in enumerate(step(1, mu1, h1, r)):
            value = value + spread(forcing, (f,), r) * k[2]
            mu2[r, f] = value
            acc = acc + value * spread(weighted, (f,), r)
        return acc

    acc = lax.fori_loop(0, rows, second, acc, unroll=2)

    def third(r, acc):
        for f, value in enumerate(step(0, mu2, h2, r)):
            stage[pl.ds(f * rows + r, PAIRS, stride=FIELDS * rows), :] = value
            acc = acc + value * spread(weighted, (f,), r)
        return acc

    acc = lax.fori_loop(0, rows, third, acc, unroll=2)
    copy = pltpu.make_async_copy(stage, out_hbm, sem)
    copy.start()
    source_part = jnp.sum(z, axis=0, keepdims=True) * k[2]
    acc = (acc - 2.0 * source_part) * norm
    sens_ref[...] = jnp.broadcast_to(jnp.sum(acc, axis=1, keepdims=True), (8, width))
    copy.wait()


def shift_pairs(devices, k):
    return [(i, (i + k) % devices) for i in range(devices)]


def on_device(checkpoints, owner, flux_matrix, row_link, blade_group, forcing):
    n_out = lax.axis_size("out")
    cycle = lax.axis_size("blk")
    rows, width = forcing.shape[1], forcing.shape[2]
    pos = jnp.stack([lax.axis_index("out"), lax.axis_index("blk")]).astype(jnp.int32)
    slot = checkpoints[0]

    own_edges = pl.pallas_call(
        q_edges_kernel,
        out_shape=jax.ShapeDtypeStruct((QS_ROWS, rows), BF16),
        in_specs=[VMEM, VMEM],
        out_specs=VMEM,
        name="edges",
    )(slot, q_select(width))
    edges = [own_edges] + [
        lax.ppermute(own_edges, "out", shift_pairs(n_out, k)) for k in range(1, n_out)
    ]
    slots = [slot] + [lax.ppermute(slot, "out", shift_pairs(n_out, k)) for k in range(1, n_out)]

    fsel, place = strip_selects(width)
    strip = jax.ShapeDtypeStruct((FIELDS * SLOT, rows), BF16)


    send_a, send_b = pl.pallas_call(
        functools.partial(strips_kernel, n_out),
        out_shape=(strip, strip),
        in_specs=[SMEM, SMEM] + [VMEM] * (n_out + 4),
        out_specs=(VMEM, VMEM),
        name="strips",
    )(pos, owner, *edges, forcing, row_link, fsel, place)
    recv_a = lax.ppermute(send_a, "blk", [(i, i ^ 1) for i in range(cycle)])
    recv_b = lax.ppermute(
        send_b, "blk", [(i, (i + 1) % cycle if i % 2 else (i - 1) % cycle) for i in range(cycle)]
    )

    field = jax.ShapeDtypeStruct((FIELDS, rows, width), F32)
    h1, h2, b0, fe, k, inv = pl.pallas_call(
        functools.partial(halo_kernel, cycle),
        out_shape=(
            field,
            field,
            field,
            field,
            jax.ShapeDtypeStruct((5, PAIRS, width), F32),
            jax.ShapeDtypeStruct((rows,), jnp.int32),
        ),
        in_specs=[SMEM] * 4 + [VMEM] * 7,
        out_specs=(VMEM,) * 5 + (SMEM,),
        scratch_shapes=[pltpu.SMEM((FIELDS, FIELDS), F32)],
        compiler_params=pltpu.CompilerParams(vmem_limit_bytes=40 * 2**20),
        name="halo",
    )(
        pos, flux_matrix, blade_group, row_link[0], send_a, send_b, recv_a, recv_b,
        forcing, row_link, halo_select(width),
    )

    pairs_fields = PAIRS * FIELDS
    adjoint, sens = pl.pallas_call(
        functools.partial(main_kernel, n_out, cycle),
        out_shape=(
            jax.ShapeDtypeStruct((pairs_fields * rows, width), F32),
            jax.ShapeDtypeStruct((PAIRS, width), F32),
        ),
        in_specs=[SMEM] * 4 + [VMEM] * (n_out + 6),
        out_specs=(HBM, VMEM),
        scratch_shapes=[
            pltpu.VMEM((4, FIELDS, rows, width), F32),
            pltpu.VMEM((STEPS - 1, 2 * FIELDS - 1, rows, width), F32),
            pltpu.VMEM((rows, FIELDS, PAIRS, width), F32),
            pltpu.VMEM((rows, FIELDS, PAIRS, width), F32),
            pltpu.VMEM((pairs_fields * rows, width), F32),
            pltpu.VMEM((FIELDS, rows, width), F32),
            pltpu.SMEM((FIELDS, FIELDS), F32),
            pltpu.SemaphoreType.DMA(()),
        ],
        compiler_params=pltpu.CompilerParams(vmem_limit_bytes=50 * 2**20),
        name="steps",
    )(pos, owner, flux_matrix, inv, *slots, forcing, b0, fe, h1, h2, k)

    sens = lax.psum(sens[:, 0].reshape(GRP_DEV, AMP), "blk")
    return adjoint.reshape(GRP_DEV, AMP, FIELDS, rows, width), sens


def solution(mesh):
    return jax.shard_map(
        on_device,
        mesh=mesh,
        in_specs=(P("out", None, None, "blk"), P(), P(), P("blk", None), P(), P(None, None, "blk")),
        out_specs=(P("out", None, None, None, "blk"), P("out", None)),
        check_vma=False,
    )
```

```python
import functools
import math

import jax
import jax.numpy as jnp
import numpy as np
from jax import lax
from jax.experimental import pallas as pl
from jax.experimental.pallas import tpu as pltpu
from jax.sharding import PartitionSpec as P

FIELDS = 5
BLADES = 96
AMP = 4
GRP_DEV = 2
STEPS = 3
PAIRS = GRP_DEV * AMP

time_step = 0.25
second_diff = 0.1
fourth_diff = 0.02
link_weight = 0.5
two_pi = 2.0 * math.pi

C0 = 1.0 - time_step * (2.0 * second_diff + 6.0 * fourth_diff + link_weight)
C1 = time_step * (second_diff + 4.0 * fourth_diff)
C2 = -time_step * fourth_diff
CP = time_step * link_weight
CM = 0.5 * time_step
CU = 0.25 * time_step

FW = 6
QW = 4
PARTS = 3
SLOT = 32
QROW = PARTS * FW
LINK_ROW = QROW + STEPS * QW
QS_ROWS = 48
SEG = 16
HALF = SEG // 2
VMEM_LIMIT = 60 * 2**20

VMEM = pl.BlockSpec(memory_space=pltpu.VMEM)
SMEM = pl.BlockSpec(memory_space=pltpu.SMEM)
HBM = pl.BlockSpec(memory_space=pl.ANY)
UNIT = time_step * fourth_diff
CENTRE = round(C0 / UNIT)
NEAR = round(C1 / UNIT)
F32 = jnp.float32
BF16 = jnp.bfloat16
NT = (((1,), (1,)), ((), ()))
TN = (((0,), (0,)), ((), ()))
NN = (((1,), (0,)), ((), ()))


def mm(a, b, dims=NN):
    return lax.dot_general(a, b, dims, preferred_element_type=F32)


def split3(x):
    hi = x.astype(BF16)
    rest = x - hi.astype(F32)
    mid = rest.astype(BF16)
    return hi, mid, (rest - mid.astype(F32)).astype(BF16)


def exact_mm(a, x):
    hi, mid, lo = split3(x)
    return mm(a, hi) + mm(a, mid) + mm(a, lo)


def fetch(moves, sems):
    copies = [pltpu.make_async_copy(src, dst, sems.at[i]) for i, (src, dst) in enumerate(moves)]
    for copy in copies:
        copy.start()
    return copies


def arrive(copies):
    for copy in copies:
        copy.wait()


def like(x):
    return pltpu.VMEM(x.shape, x.dtype)


def cost(flops, moved):
    return pl.CostEstimate(flops=flops, bytes_accessed=moved, transcendentals=0)


def q_select(width):
    out = np.zeros((FIELDS, QS_ROWS, width), np.float32)
    for f in range(FIELDS):
        for j in range(QW):
            out[f, f * 8 + j, j] = 1.0
            out[f, f * 8 + QW + j, width - QW + j] = 1.0
    return out.astype(jnp.bfloat16)


def q_edges_kernel(ck_hbm, sel_hbm, out_ref, ck_ref, sel_ref, sems):
    arrive(fetch(((ck_hbm, ck_ref), (sel_hbm, sel_ref)), sems))
    total = None
    for f in range(FIELDS):
        part = mm(sel_ref[f], ck_ref[f], NT)
        total = part if total is None else total + part
    out_ref[...] = total.astype(BF16)


def strip_selects(width):
    forcing_sel = np.zeros((PARTS, 2 * SLOT, width), np.float32)
    for part in range(PARTS):
        for j in range(FW):
            forcing_sel[part, part * FW + j, j] = 1.0
            forcing_sel[part, SLOT + part * FW + j, width - FW + j] = 1.0
    place = np.zeros((FIELDS, 2 * SLOT, STEPS * QS_ROWS), np.float32)
    for f in range(FIELDS):
        for n in range(STEPS):
            for j in range(QW):
                place[f, QROW + n * QW + j, n * QS_ROWS + f * 8 + j] = 1.0
                place[f, SLOT + QROW + n * QW + j, n * QS_ROWS + f * 8 + QW + j] = 1.0
    return forcing_sel.astype(jnp.bfloat16), place.astype(jnp.bfloat16)


def pick(values, index):
    out = values[0]
    for k in range(1, len(values)):
        out = jnp.where(index == k, values[k], out)
    return out


def strips_kernel(n_out, *refs):
    owner, *qs = refs[: 1 + n_out]
    hbm = refs[1 + n_out : 5 + n_out]
    send_a, send_b = refs[5 + n_out : 7 + n_out]
    scratch = refs[7 + n_out : -1]
    arrive(fetch(zip((*qs, *hbm), scratch), refs[-1]))
    edges = [q[...].astype(F32) for q in scratch[:n_out]]
    forcing, link, fsel, place = scratch[n_out:]
    me = lax.axis_index("out")
    even = lax.axis_index("blk") % 2 == 0
    chosen = jnp.concatenate(
        [pick(edges, (me - owner[n] + n_out) % n_out) for n in range(STEPS)], axis=0
    ).astype(BF16)
    row = lax.broadcasted_iota(jnp.int32, (2 * SLOT, link.shape[1]), 0)
    links = jnp.broadcast_to(link[...].astype(F32), row.shape)
    for f in range(FIELDS):
        both = mm(place[f], chosen)
        for sel, part in zip(range(PARTS), split3(forcing[f])):
            both = both + mm(fsel[sel], part, NT)
        if f == 0:
            both = jnp.where(row % SLOT == LINK_ROW, links, both)
        left, right = both[:SLOT], both[SLOT:]
        send_a[f * SLOT : (f + 1) * SLOT] = jnp.where(even, right, left).astype(BF16)
        send_b[f * SLOT : (f + 1) * SLOT] = jnp.where(even, left, right).astype(BF16)


def column_factor(columns, pair, start, total, group_base, blade_group):
    scaled = columns * BLADES
    first = ((start + total - HALF) * BLADES) // total - BLADES
    group = jnp.full(columns.shape, -1, jnp.int32)
    numerator = jnp.zeros(columns.shape, jnp.int32)
    width = columns.shape[-1]
    for j in range((width + SEG) * BLADES // total + 2):
        blade = first + j
        inside = (scaled >= blade * total) & (scaled < (blade + 1) * total)
        group = jnp.where(inside, blade_group[(blade + BLADES) % BLADES], group)
        numerator = jnp.where(inside, scaled - blade * total, numerator)
    phase = numerator.astype(F32) / total
    amp = pair & (AMP - 1)
    order = ((amp >> 1) + 1).astype(F32)
    angle = two_pi * order * phase
    harmonic = jnp.where((amp & 1) == 0, jnp.cos(angle), jnp.sin(angle))
    return jnp.where(group == group_base + pair // AMP, harmonic, 0.0)


def flux(fm, q, d):
    inner = q[0] * d[0]
    for f in range(1, FIELDS):
        inner = inner + q[f] * d[f]
    u = q[1] * CU
    out = []
    for e in range(FIELDS):
        value = u * d[e]
        for f in range(FIELDS):
            value = value + fm[f, e] * d[f]
        if e == 1:
            value = value + CU * inner
        out.append(value)
    return out


def prepare_kernel(cycle, blade_group, link_s, forcing_hbm, link_hbm, k_ref, kp_ref, b0_ref, inv_ref, forcing, link, sems):
    copies = fetch(((forcing_hbm, forcing), (link_hbm, link)), sems)
    rows, width = forcing.shape[1:]
    total = cycle * width
    start = lax.axis_index("blk") * width

    def invert(r, c):
        inv_ref[link_s[r]] = r
        return c

    lax.fori_loop(0, rows, invert, 0, unroll=8)
    lane = lax.broadcasted_iota(jnp.int32, (8, width), 1)
    sub = lax.broadcasted_iota(jnp.int32, (8, width), 0)
    p = lane & (SEG - 1)
    packed = jnp.where(p < HALF, p - QW, width - QW + p - HALF) + start
    args = (start, total, lax.axis_index("out") * GRP_DEV, blade_group)
    for i in range(5):
        k_ref[i] = column_factor(lane + start + (i - 2), sub, *args)
        kp_ref[i] = column_factor(packed + (i - 2), sub, *args)
    arrive(copies)
    hot = one_hot(link[...].astype(F32), rows)
    for f in range(FIELDS):
        b0_ref[f] = (C0 + 1.0) * forcing[f] + CP * exact_mm(hot, forcing[f])


def one_hot(links, rows):
    row = lax.broadcasted_iota(jnp.int32, (rows, rows), 0).astype(F32)
    return jnp.where(links == row, 1.0, 0.0).astype(BF16)


def halo_selects(width, rows):
    blocks = width // SEG
    step = rows // blocks
    sel = np.zeros((4 * SLOT, 7, SEG), np.float32)
    edge = np.zeros((4 * SLOT, width), np.float32)

    def place(column, size):
        if column < 0:
            return 0, column + size
        if column < size:
            return 1, column
        if column < width:
            return 2, column - (width - size)
        return 3, column - width

    def forcing_rows(column):
        source, j = place(column, FW)
        return [source * SLOT + part * FW + j for part in range(PARTS)] if 0 <= j < FW else []

    for p in range(SEG):
        column = p - QW if p < HALF else width - QW + p - HALF
        for i in range(5):
            for row in forcing_rows(column + i - 2):
                sel[row, i, p] = 1.0
        source, j = place(column, QW)
        for i, n in ((5, STEPS - 1), (6, STEPS - 2)):
            sel[source * SLOT + QROW + n * QW + j, i, p] = 1.0
    for lane, column in ((width - 2, -2), (width - 1, -1), (0, width), (1, width + 1)):
        for row in forcing_rows(column):
            edge[row, lane] = 1.0
    big = np.zeros((blocks, 4 * SLOT, 7, blocks, SEG), np.float32)
    for j in range(blocks):
        big[j, :, :, j, :] = sel
    big = big.reshape(blocks * 4 * SLOT, 7 * width)
    return big.astype(jnp.bfloat16), edge.astype(jnp.bfloat16)


def stencil_selects(width):
    blocks = width // SEG
    inner = np.zeros((2, width, 2 * width), np.float32)
    outer = np.zeros((blocks, 2, width, 2 * width), np.float32)

    def spread(column):
        out = []
        for c, w in ((column + 1, 1.0), (column - 1, -1.0)):
            if 0 <= c < width:
                out.append((c, w))
        for c, w in (
            (column, CENTRE),
            (column - 1, NEAR),
            (column + 1, NEAR),
            (column - 2, -1.0),
            (column + 2, -1.0),
        ):
            if 0 <= c < width:
                out.append((width + c, w))
        return out

    for column in range(width):
        for lane, w in spread(column):
            inner[:, column, lane] = w
    for j in range(blocks):
        for p, column in ((2, -2), (3, -1), (HALF + QW, width), (HALF + QW + 1, width + 1)):
            for lane, w in spread(column):
                outer[j, :, j * SEG + p, lane] = w
    return (
        inner.reshape(2 * width, 2 * width).astype(jnp.bfloat16),
        outer.reshape(blocks, 2 * width, 2 * width).astype(jnp.bfloat16),
    )


def halves(x):
    hi = x.astype(BF16)
    return jnp.concatenate([hi, (x - hi.astype(F32)).astype(BF16)], axis=1)


def halo_kernel(
    fm, link_hbm, send_a, send_b, recv_a, recv_b, big_hbm, edge_hbm, kp_hbm,
    e1_ref, e2_ref, fe_ref,
    link, sa_v, sb_v, ra_v, rb_v, big, edge, kp_ref, y_ref, fmc, sems,
):
    copies = fetch(
        (
            (link_hbm, link), (send_a, sa_v), (send_b, sb_v), (recv_a, ra_v), (recv_b, rb_v),
            (edge_hbm, edge), (kp_hbm, kp_ref), (big_hbm, big),
        ),
        sems,
    )
    rows, width = link.shape[1], kp_ref.shape[2]
    blocks = width // SEG
    step = rows // blocks
    even = lax.axis_index("blk") % 2 == 0
    for f in range(FIELDS):
        for e in range(FIELDS):
            fmc[f, e] = fm[f, e] * CM
    arrive(copies[:-1])
    sa, sb = sa_v[...].astype(F32), sb_v[...].astype(F32)
    ra, rb = ra_v[...].astype(F32), rb_v[...].astype(F32)
    own_left, own_right = jnp.where(even, sb, sa), jnp.where(even, sa, sb)
    left, right = jnp.where(even, rb, ra), jnp.where(even, ra, rb)
    hot_own = one_hot(link[...].astype(F32), rows)
    hot_left = one_hot(left[LINK_ROW : LINK_ROW + 1], rows)
    hot_right = one_hot(right[LINK_ROW : LINK_ROW + 1], rows)
    source = lax.broadcasted_iota(jnp.int32, (rows, 4 * SLOT), 1) // SLOT

    def permuted(x):
        by_left, by_right = mm(hot_left, x), mm(hot_right, x)
        outer = jnp.where(source == 0, by_left, by_right)
        by_tile = jnp.where((source == 1) | (source == 2), mm(hot_own, x), outer)
        return by_left.astype(BF16), by_right.astype(BF16), by_tile.astype(BF16)

    def rowed(x):
        return jnp.concatenate([x[j * step : (j + 1) * step] for j in range(blocks)], axis=1)

    sets = [[] for _ in range(5)]
    for f in range(FIELDS):
        s = slice(f * SLOT, (f + 1) * SLOT)
        g = jnp.concatenate([left[s], own_left[s], own_right[s], right[s]], axis=0)
        g = g.T.astype(BF16)
        fe_ref[f] = mm(g, edge[...])
        by_left, by_right, by_tile = permuted(g)
        for rows_of, x in zip(sets, (g, by_tile, permuted(by_tile)[2], by_left, by_right)):
            rows_of.append(rowed(x))
    copies[-1].wait()
    group = FIELDS * step
    y = mm(jnp.concatenate(sum(sets, []), axis=0), big[...])
    is_left = lax.broadcasted_iota(jnp.int32, (step, width), 1) & (SEG - 1) < HALF

    def part(i, f, which):
        return y[i * group + f * step : i * group + (f + 1) * step, which * width : (which + 1) * width]

    def at(linked, f, which):
        if linked:
            return jnp.where(is_left, part(3, f, which), part(4, f, which))
        return part(0, f, which)

    for i in range(2):
        shifted = [[at(i, f, d) for f in range(FIELDS)] for d in range(5)]
        q2 = [at(i, f, 5) for f in range(FIELDS)]
        plus = flux(fmc, q2, shifted[3])
        minus = flux(fmc, q2, shifted[1])
        for f in range(FIELDS):
            b = (
                C2 * shifted[0][f],
                C1 * shifted[1][f] - minus[f],
                (C0 + 1.0) * shifted[2][f] + CP * part(i + 1, f, 2),
                C1 * shifted[3][f] + plus[f],
                C2 * shifted[4][f],
            )
            for d in range(5):
                y_ref[i * 5 + d, f] = b[d]
    for f in range(FIELDS):
        y_ref[10, f] = part(0, f, 2)
        y_ref[11, f] = part(0, f, 6)
    kp = [kp_ref[i] for i in range(5)]

    def body(r, c):
        def row(i, f):
            return jnp.broadcast_to(y_ref[i, f, pl.ds(r, 1), :], (8, width))

        mu, linked, d, base = [], [], [], []
        for f in range(FIELDS):
            for i, out in ((0, mu), (5, linked)):
                value = row(i, f) * kp[0]
                for n in range(1, 5):
                    value = value + row(i + n, f) * kp[n]
                out.append(value)
            x = mu[f]
            m1, p1 = pltpu.roll(x, 1, 1), pltpu.roll(x, width - 1, 1)
            m2, p2 = pltpu.roll(x, 2, 1), pltpu.roll(x, width - 2, 1)
            d.append(m1 - p1)
            base.append(
                C0 * x + C1 * (m1 + p1) + C2 * (m2 + p2) + CP * linked[f] + row(10, f) * kp[2]
            )
        moved = flux(fmc, [row(11, f) for f in range(FIELDS)], d)
        at = pl.ds(pl.multiple_of(r * (FIELDS * 8), 8), FIELDS * 8)
        e1_ref[at, :] = halves(jnp.concatenate(mu, axis=0))
        e2_ref[at, :] = halves(
            jnp.concatenate([b - m for b, m in zip(base, moved)], axis=0)
        )
        return c

    lax.fori_loop(0, step, body, 0, unroll=4)


def main_kernel(n_out, cycle, *refs):
    owner, fm, inv = refs[:3]
    slots = refs[3 : 3 + n_out]
    hbm = refs[3 + n_out : 11 + n_out]
    out_hbm, sens_ref = refs[11 + n_out : 13 + n_out]
    (
        forcing, fe, b0, k_ref, inner, outer, e1, e2,
        q0, q1, q2, bs, coef, mu1, mu2, dz, stage, weighted, fmc, sems, out_sems,
    ) = refs[13 + n_out :]
    copies = fetch(zip(hbm, (forcing, fe, b0, k_ref, inner, outer, e1, e2)), sems)
    rows, width = forcing.shape[1], forcing.shape[2]
    me = lax.axis_index("out")
    total = cycle * width
    q_copies = []
    for n, q in reversed(tuple(enumerate((q0, q1, q2)))):
        which = (me - owner[n] + n_out) % n_out
        for s, slot in enumerate(slots):

            @pl.when(which == s)
            def _():
                pltpu.make_async_copy(slot, q, sems.at[8 + n]).start()

        q_copies.append(pltpu.make_async_copy(slots[0], q, sems.at[8 + n]))

    for f in range(FIELDS):
        for e in range(FIELDS):
            fmc[f, e] = fm[f, e] * CM
    lane = lax.broadcasted_iota(jnp.int32, (8, width), 1)
    start = lax.axis_index("blk") * width
    weight = 1.0 + 2.0 * (lane + start).astype(F32) / total
    norm = 1.0 / math.sqrt(FIELDS * rows * total)

    def around(x, edge):
        return (
            pltpu.roll(jnp.where(lane == width - 1, edge, x), 1, 1),
            pltpu.roll(jnp.where(lane == 0, edge, x), width - 1, 1),
            pltpu.roll(jnp.where(lane >= width - 2, edge, x), 2, 1),
            pltpu.roll(jnp.where(lane < 2, edge, x), width - 2, 1),
        )

    def dense(i, z):
        rs = pl.ds(pl.multiple_of(i * 16, 16), 16)
        for n, q_ref in enumerate((q0, q1)):
            q = [q_ref[f, rs, :].astype(F32) for f in range(FIELDS)]
            u = CU * q[1]
            for e in range(FIELDS):
                coef[n, e, rs, :] = (u if e != 1 else u + u) + fmc[e, e]
            for j, f in enumerate((0, 2, 3, 4)):
                coef[n, FIELDS + j, rs, :] = CU * q[f] + fmc[f, 1]
        q = [q2[f, rs, :].astype(F32) for f in range(FIELDS)]
        for half in range(2):
            r8 = pl.ds(pl.multiple_of(i * 16 + half * 8, 8), 8)
            near = [around(forcing[f, r8, :], fe[f, r8, :]) for f in range(FIELDS)]
            mine = [x[half * 8 : half * 8 + 8] for x in q]
            minus = flux(fmc, mine, [a[0] for a in near])
            plus = flux(fmc, mine, [a[1] for a in near])
            for f in range(FIELDS):
                m1, p1, m2, p2 = near[f]
                bs[0, f, r8, :] = C2 * m2
                bs[1, f, r8, :] = C1 * m1 - minus[f]
                bs[2, f, r8, :] = C1 * p1 + plus[f]
                bs[3, f, r8, :] = C2 * p2
                w = forcing[f, r8, :] * weight
                weighted[f, r8, :] = w
                z = z + w * forcing[f, r8, :]
        return z

    zero = jnp.zeros((8, width), F32)
    arrive(copies + q_copies)
    z = lax.fori_loop(0, rows // 16, dense, zero)
    k = [k_ref[i] for i in range(5)]

    def spread(ref, index, r):
        return jnp.broadcast_to(ref[(*index, pl.ds(r, 1), slice(None))], (8, width))

    def first(i, acc):
        for j in range(8):
            r = i * 8 + j
            for f in range(FIELDS):
                value = spread(bs, (0, f), r) * k[0] + spread(bs, (1, f), r) * k[1]
                value = value + spread(b0, (f,), r) * k[2] + spread(bs, (2, f), r) * k[3]
                value = value + spread(bs, (3, f), r) * k[4]
                mu1[r, f] = value
                acc = acc + value * spread(weighted, (f,), r)
        return acc

    acc = lax.fori_loop(0, rows // 8, first, zero)

    blocks = width // SEG
    size = rows // blocks
    group = size * FIELDS * 8

    def step(n, source, edges, j, keep, acc):
        r0 = pl.multiple_of(j * size, size)
        x = source[pl.ds(r0, size)].reshape(group, width)
        dz[...] = mm(halves(x), inner[...]) + mm(edges[...], outer[j])
        for i in range(size):
            r = r0 + i
            linked = inv[r]
            at = [slice((i * FIELDS + f) * 8, (i * FIELDS + f + 1) * 8) for f in range(FIELDS)]
            d = [dz[at[f], :width] for f in range(FIELDS)]
            for e in range(FIELDS):
                value = UNIT * dz[at[e], width:] + CP * source[linked, e]
                for f in range(FIELDS):
                    if f == e:
                        m = spread(coef, (n, e), r)
                    elif e == 1:
                        m = spread(coef, (n, FIELDS + (0, 2, 3, 4).index(f)), r)
                    else:
                        m = fmc[f, e]
                    value = value - m * d[f]
                value = keep(r, e, value)
                acc = acc + value * spread(weighted, (e,), r)
        return acc

    def second(j, acc):
        def keep(r, e, value):
            value = value + spread(forcing, (e,), r) * k[2]
            mu2[r, e] = value
            return value

        return step(1, mu1, e1, j, keep, acc)

    acc = lax.fori_loop(0, blocks, second, acc)
    shaped = stage.reshape(PAIRS * FIELDS, rows, width)

    def send(j):
        at = pl.ds(pl.multiple_of(j * size, size), size)
        return pltpu.make_async_copy(shaped.at[:, at, :], out_hbm.at[:, at, :], out_sems.at[j])

    def third(j, acc):
        def keep(r, e, value):
            stage[pl.ds(e * rows + r, PAIRS, stride=FIELDS * rows), :] = value
            return value

        acc = step(0, mu2, e2, j, keep, acc)
        send(j).start()
        return acc

    acc = lax.fori_loop(0, blocks, third, acc)
    source_part = jnp.sum(z, axis=0, keepdims=True) * k[2]
    acc = (acc - 2.0 * source_part) * norm
    sens_ref[...] = jnp.broadcast_to(jnp.sum(acc, axis=1, keepdims=True), (8, width))
    for j in range(blocks):
        send(j).wait()


def shift_pairs(devices, k):
    return [(i, (i + k) % devices) for i in range(devices)]


def total_over(x, axis):
    devices = lax.axis_size(axis)
    if devices & (devices - 1):
        return lax.psum(x, axis)
    bit = 1
    while bit < devices:
        x = x + lax.ppermute(x, axis, [(i, i ^ bit) for i in range(devices)])
        bit *= 2
    return x


def on_device(checkpoints, owner, flux_matrix, row_link, blade_group, forcing):
    n_out = lax.axis_size("out")
    cycle = lax.axis_size("blk")
    rows, width = forcing.shape[1], forcing.shape[2]
    blocks = width // SEG
    slot = checkpoints[0]

    def struct(shape, kind=F32):
        return jax.ShapeDtypeStruct(shape, kind)

    sems = pltpu.SemaphoreType.DMA
    edge_sel = q_select(width)
    own_edges = pl.pallas_call(
        q_edges_kernel,
        out_shape=struct((QS_ROWS, rows), BF16),
        in_specs=[HBM, HBM],
        out_specs=VMEM,
        scratch_shapes=[like(slot), like(edge_sel), sems((2,))],
        cost_estimate=cost(2 * 240 * 128 * 128, 200000),
        name="edges",
    )(slot, edge_sel)
    edges = [own_edges] + [
        lax.ppermute(own_edges, "out", shift_pairs(n_out, k)) for k in range(1, n_out)
    ]
    sent = lax.optimization_barrier((slot, *edges[1:]))[0]
    slots = [slot] + [lax.ppermute(sent, "out", shift_pairs(n_out, k)) for k in range(1, n_out)]

    fsel, place = strip_selects(width)
    strip = struct((FIELDS * SLOT, rows), BF16)
    operands = (*edges, forcing, row_link, fsel, place)
    send_a, send_b = pl.pallas_call(
        functools.partial(strips_kernel, n_out),
        out_shape=(strip, strip),
        in_specs=[SMEM] + [HBM] * len(operands),
        out_specs=(VMEM, VMEM),
        scratch_shapes=[*map(like, operands), sems((len(operands),))],
        cost_estimate=cost(10**7, 600000),
        name="strips",
    )(owner, *operands)
    recv_a = lax.ppermute(send_a, "blk", [(i, i ^ 1) for i in range(cycle)])
    recv_b = lax.ppermute(
        send_b, "blk", [(i, (i + 1) % cycle if i % 2 else (i - 1) % cycle) for i in range(cycle)]
    )

    k, kp, b0, inv = pl.pallas_call(
        functools.partial(prepare_kernel, cycle),
        out_shape=(
            struct((5, PAIRS, width)),
            struct((5, PAIRS, width)),
            struct((FIELDS, rows, width)),
            struct((rows,), jnp.int32),
        ),
        in_specs=[SMEM, SMEM, HBM, HBM],
        out_specs=(VMEM, VMEM, VMEM, SMEM),
        scratch_shapes=[like(forcing), like(row_link), sems((2,))],
        cost_estimate=cost(10**8, 10**6),
        name="prepare",
    )(blade_group, row_link[0], forcing, row_link)

    big, edge = halo_selects(width, rows)
    step_rows = rows // blocks
    edge_shape = (step_rows * FIELDS * 8, 2 * width)
    operands = (row_link, send_a, send_b, recv_a, recv_b, big, edge, kp)
    loaded = (row_link, send_a, send_b, recv_a, recv_b, big, edge, kp)
    e1, e2, fe = pl.pallas_call(
        halo_kernel,
        out_shape=(struct(edge_shape, BF16), struct(edge_shape, BF16), struct((FIELDS, rows, width))),
        in_specs=[SMEM] + [HBM] * len(operands),
        out_specs=(VMEM,) * 3,
        scratch_shapes=[
            *map(like, loaded),
            pltpu.VMEM((12, FIELDS, step_rows, width), F32),
            pltpu.SMEM((FIELDS, FIELDS), F32),
            sems((len(operands),)),
        ],
        compiler_params=pltpu.CompilerParams(vmem_limit_bytes=VMEM_LIMIT),
        cost_estimate=cost(10**8, 4 * 10**6),
        name="halo",
    )(flux_matrix, *operands)

    pairs_fields = PAIRS * FIELDS
    inner, outer = stencil_selects(width)
    operands = (forcing, fe, b0, k, inner, outer, e1, e2)
    adjoint, sens = pl.pallas_call(
        functools.partial(main_kernel, n_out, cycle),
        out_shape=(struct((pairs_fields, rows, width)), struct((PAIRS, width))),
        in_specs=[SMEM] * 3 + [HBM] * (n_out + len(operands)),
        out_specs=(HBM, VMEM),
        scratch_shapes=[
            *map(like, operands),
            like(slot),
            like(slot),
            like(slot),
            pltpu.VMEM((4, FIELDS, rows, width), F32),
            pltpu.VMEM((STEPS - 1, 2 * FIELDS - 1, rows, width), F32),
            pltpu.VMEM((rows, FIELDS, PAIRS, width), F32),
            pltpu.VMEM((rows, FIELDS, PAIRS, width), F32),
            pltpu.VMEM((step_rows * FIELDS * PAIRS, 2 * width), F32),
            pltpu.VMEM((pairs_fields * rows, width), F32),
            pltpu.VMEM((FIELDS, rows, width), F32),
            pltpu.SMEM((FIELDS, FIELDS), F32),
            sems((len(operands) + STEPS,)),
            sems((blocks,)),
        ],
        compiler_params=pltpu.CompilerParams(vmem_limit_bytes=VMEM_LIMIT),
        cost_estimate=cost(10**9, 10**7),
        name="steps",
    )(owner, flux_matrix, inv, *slots, *operands)

    sens = total_over(sens, "blk")[:, 0].reshape(GRP_DEV, AMP)
    return adjoint.reshape(GRP_DEV, AMP, FIELDS, rows, width), sens


def solution(mesh):
    return jax.shard_map(
        on_device,
        mesh=mesh,
        in_specs=(P("out", None, None, "blk"), P(), P(), P("blk", None), P(), P(None, None, "blk")),
        out_specs=(P("out", None, None, None, "blk"), P("out", None)),
        check_vma=False,
    )
```

```python
import functools
import math

import jax
import jax.numpy as jnp
import numpy as np
from jax import lax
from jax.experimental import pallas as pl
from jax.experimental.pallas import tpu as pltpu
from jax.sharding import PartitionSpec as P

FIELDS = 5
BLADES = 96
AMP = 4
GRP_DEV = 2
STEPS = 3
PAIRS = GRP_DEV * AMP

time_step = 0.25
second_diff = 0.1
fourth_diff = 0.02
link_weight = 0.5
two_pi = 2.0 * math.pi

C0 = 1.0 - time_step * (2.0 * second_diff + 6.0 * fourth_diff + link_weight)
C1 = time_step * (second_diff + 4.0 * fourth_diff)
C2 = -time_step * fourth_diff
CP = time_step * link_weight
CM = 0.5 * time_step
CU = 0.25 * time_step

FW = 6
QW = 4
PARTS = 3
SLOT = 32
LINK_ROW = PARTS * FW
SEG = 16
HALF = SEG // 2
VMEM_LIMIT = 40 * 2**20
SMALL_LIMIT = 16 * 2**20

VMEM = pl.BlockSpec(memory_space=pltpu.VMEM)
SMEM = pl.BlockSpec(memory_space=pltpu.SMEM)
HBM = pl.BlockSpec(memory_space=pltpu.HBM)
UNIT = time_step * fourth_diff
CENTRE = round(C0 / UNIT)
NEAR = round(C1 / UNIT)
F32 = jnp.float32
BF16 = jnp.bfloat16
NT = (((1,), (1,)), ((), ()))
TN = (((0,), (0,)), ((), ()))
NN = (((1,), (0,)), ((), ()))


def mm(a, b, dims=NN):
    return lax.dot_general(a, b, dims, preferred_element_type=F32)


def split3(x):
    hi = x.astype(BF16)
    rest = x - hi.astype(F32)
    mid = rest.astype(BF16)
    return hi, mid, (rest - mid.astype(F32)).astype(BF16)


def exact_mm(a, x):
    hi, mid, lo = split3(x)
    return mm(a, hi) + mm(a, mid) + mm(a, lo)


def fetch(moves, sems):
    copies = [pltpu.make_async_copy(src, dst, sems.at[i]) for i, (src, dst) in enumerate(moves)]
    for copy in copies:
        copy.start()
    return copies


def arrive(copies):
    for copy in copies:
        copy.wait()


def like(x):
    return pltpu.VMEM(x.shape, x.dtype)


def cost(flops, moved):
    return pl.CostEstimate(flops=flops, bytes_accessed=moved, transcendentals=0)


def forcing_select(width):
    out = np.zeros((PARTS, width, width), np.float32)
    for part in range(PARTS):
        for j in range(FW):
            out[part, j, part * FW + j] = 1.0
            out[part, width - FW + j, SLOT + part * FW + j] = 1.0
    return out.reshape(PARTS * width, width).astype(jnp.bfloat16)


def state_select(width):
    out = np.zeros((2 * SLOT, STEPS, width), np.float32)
    for n in range(STEPS):
        for j in range(QW):
            out[n * QW + j, n, j] = 1.0
            out[SLOT + n * QW + j, n, width - QW + j] = 1.0
    return out.reshape(2 * SLOT, STEPS * width).astype(jnp.bfloat16)


def give(send_a, send_b, f, both):
    even = lax.axis_index("blk") % 2 == 0
    left, right = both[:SLOT], both[SLOT:]
    send_a[f * SLOT : (f + 1) * SLOT] = jnp.where(even, right, left).astype(BF16)
    send_b[f * SLOT : (f + 1) * SLOT] = jnp.where(even, left, right).astype(BF16)


def strips_kernel(n_out, *refs):
    owner = refs[0]
    slots = refs[1 : 1 + n_out]
    sel, send_a, send_b, *chosen = refs[1 + n_out :]
    me = lax.axis_index("out")
    for n, target in enumerate(chosen):
        which = (me - owner[n] + n_out) % n_out
        for s, slot in enumerate(slots):

            @pl.when(which == s)
            def _():
                target[...] = slot[...]

    for f in range(FIELDS):
        give(send_a, send_b, f, mm(sel[...], jnp.concatenate([q[f] for q in chosen], axis=1), NT))


def column_factor(columns, pair, start, total, group_base, blade_group):
    scaled = columns * BLADES
    first = ((start + total - HALF) * BLADES) // total - BLADES
    group = jnp.full(columns.shape, -1, jnp.int32)
    numerator = jnp.zeros(columns.shape, jnp.int32)
    width = columns.shape[-1]
    for j in range((width + SEG) * BLADES // total + 2):
        blade = first + j
        inside = (scaled >= blade * total) & (scaled < (blade + 1) * total)
        group = jnp.where(inside, blade_group[(blade + BLADES) % BLADES], group)
        numerator = jnp.where(inside, scaled - blade * total, numerator)
    phase = numerator.astype(F32) / total
    amp = pair & (AMP - 1)
    order = ((amp >> 1) + 1).astype(F32)
    angle = two_pi * order * phase
    harmonic = jnp.where((amp & 1) == 0, jnp.cos(angle), jnp.sin(angle))
    return jnp.where(group == group_base + pair // AMP, harmonic, 0.0)


def flux(fm, q, d):
    inner = q[0] * d[0]
    for f in range(1, FIELDS):
        inner = inner + q[f] * d[f]
    u = q[1] * CU
    out = []
    for e in range(FIELDS):
        value = u * d[e]
        for f in range(FIELDS):
            value = value + fm[f, e] * d[f]
        if e == 1:
            value = value + CU * inner
        out.append(value)
    return out


def prepare_kernel(cycle, blade_group, link_s, *refs):
    owner, fm = refs[:2]
    kept = refs[2 : (len(refs) - 11) // 2 + 2]
    k_ref, kp_ref, b0_ref, send_a, send_b, inv_ref, owner_out, fm_out, *held, sems = refs[
        2 + len(kept) :
    ]
    copies = fetch(zip(kept, held), sems)
    for i in range(owner.shape[0]):
        owner_out[i] = owner[i]
    for f in range(FIELDS):
        for e in range(FIELDS):
            fm_out[f, e] = fm[f, e]
    forcing, link, sel = held[:3]
    rows, width = forcing.shape[1:]
    total = cycle * width
    start = lax.axis_index("blk") * width

    def invert(r, c):
        inv_ref[link_s[r]] = r
        return c

    lax.fori_loop(0, rows, invert, 0, unroll=8)
    lane = lax.broadcasted_iota(jnp.int32, (8, width), 1)
    sub = lax.broadcasted_iota(jnp.int32, (8, width), 0)
    p = lane & (SEG - 1)
    packed = jnp.where(p < HALF, p - QW, width - QW + p - HALF) + start
    args = (start, total, lax.axis_index("out") * GRP_DEV, blade_group)
    for i in range(5):
        k_ref[i] = column_factor(lane + start + (i - 2), sub, *args)
        kp_ref[i] = column_factor(packed + (i - 2), sub, *args)
    arrive(copies[:3])
    links = link[...].astype(F32)
    parts = [split3(forcing[f]) for f in range(FIELDS)]
    linked = mm(one_hot(links, rows), jnp.concatenate(sum(parts, ()), axis=1))
    chosen = mm(
        jnp.concatenate([jnp.concatenate(three, axis=1) for three in parts], axis=0), sel[...]
    )
    row = lax.broadcasted_iota(jnp.int32, (2 * SLOT, rows), 0)
    links = jnp.broadcast_to(links, row.shape)
    for f in range(FIELDS):
        three = [
            linked[:, (f * PARTS + i) * width : (f * PARTS + i + 1) * width] for i in range(PARTS)
        ]
        b0_ref[f] = (C0 + 1.0) * forcing[f] + CP * (three[0] + three[1] + three[2])
        turned = chosen[f * rows : (f + 1) * rows].T[: 2 * SLOT]
        if f == 0:
            turned = jnp.where(row % SLOT == LINK_ROW, links, turned)
        give(send_a, send_b, f, turned)
    arrive(copies[3:])


def one_hot(links, rows):
    row = lax.broadcasted_iota(jnp.int32, (rows, rows), 0).astype(F32)
    return jnp.where(links == row, 1.0, 0.0).astype(BF16)


def halo_selects(width):
    blocks = width // SEG
    forcing_sel = np.zeros((4 * SLOT, 5, SEG), np.float32)
    state_sel = np.zeros((4 * SLOT, 2, SEG), np.float32)
    edge = np.zeros((4 * SLOT, width), np.float32)

    def place(column, size):
        if column < 0:
            return 0, column + size
        if column < size:
            return 1, column
        if column < width:
            return 2, column - (width - size)
        return 3, column - width

    def forcing_rows(column):
        source, j = place(column, FW)
        return [source * SLOT + part * FW + j for part in range(PARTS)] if 0 <= j < FW else []

    for p in range(SEG):
        column = p - QW if p < HALF else width - QW + p - HALF
        for i in range(5):
            for row in forcing_rows(column + i - 2):
                forcing_sel[row, i, p] = 1.0
        source, j = place(column, QW)
        for i, n in ((0, STEPS - 1), (1, STEPS - 2)):
            state_sel[source * SLOT + n * QW + j, i, p] = 1.0
    for lane, column in ((width - 2, -2), (width - 1, -1), (0, width), (1, width + 1)):
        for row in forcing_rows(column):
            edge[row, lane] = 1.0

    def tiled(x):
        return np.repeat(x[:, :, None, :], blocks, axis=2).reshape(4 * SLOT, -1)

    return tuple(x.astype(jnp.bfloat16) for x in (tiled(forcing_sel), tiled(state_sel), edge))


def stencil_selects(width):
    blocks = width // SEG
    inner = np.zeros((2, width, 2 * width), np.float32)
    outer = np.zeros((blocks, 2, width, 2 * width), np.float32)

    def spread(column):
        out = []
        for c, w in ((column + 1, 1.0), (column - 1, -1.0)):
            if 0 <= c < width:
                out.append((c, w))
        for c, w in (
            (column, CENTRE),
            (column - 1, NEAR),
            (column + 1, NEAR),
            (column - 2, -1.0),
            (column + 2, -1.0),
        ):
            if 0 <= c < width:
                out.append((width + c, w))
        return out

    for column in range(width):
        for lane, w in spread(column):
            inner[:, column, lane] = w
    for j in range(blocks):
        for p, column in ((2, -2), (3, -1), (HALF + QW, width), (HALF + QW + 1, width + 1)):
            for lane, w in spread(column):
                outer[j, :, j * SEG + p, lane] = w
    return (
        inner.reshape(2 * width, 2 * width).astype(jnp.bfloat16),
        outer.reshape(blocks, 2 * width, 2 * width)
        .swapaxes(0, 1)
        .reshape(2 * width, blocks * 2 * width)
        .astype(jnp.bfloat16),
    )


def halves(x):
    hi = x.astype(BF16)
    return jnp.concatenate([hi, (x - hi.astype(F32)).astype(BF16)], axis=1)


def gather_sources(sa, sb, ra, rb):
    even = lax.axis_index("blk") % 2 == 0
    sa, sb, ra, rb = (x[...].astype(F32) for x in (sa, sb, ra, rb))
    own_left, own_right = jnp.where(even, sb, sa), jnp.where(even, sa, sb)
    left, right = jnp.where(even, rb, ra), jnp.where(even, ra, rb)
    turned = []
    for f in range(FIELDS):
        s = slice(f * SLOT, (f + 1) * SLOT)
        g = jnp.concatenate([left[s], own_left[s], own_right[s], right[s]], axis=0)
        turned.append(g.T.astype(BF16))
    return left, right, turned


def in_segments(sets, tiled, big, step):
    blocks = big.shape[0] // (4 * SLOT)
    width = blocks * SEG
    lane_block = lax.broadcasted_iota(jnp.int32, tiled.shape, 1) % width // SEG
    for j in range(blocks):
        big[j * 4 * SLOT : (j + 1) * 4 * SLOT, :] = jnp.where(
            lane_block == j, tiled[...].astype(F32), 0.0
        ).astype(BF16)
    pieces = []
    for x in sets:
        for f in range(FIELDS):
            mine = x[:, f * 4 * SLOT : (f + 1) * 4 * SLOT]
            pieces.append(
                jnp.concatenate([mine[j * step : (j + 1) * step] for j in range(blocks)], axis=1)
            )
    y = mm(jnp.concatenate(pieces, axis=0), big[...])

    def part(i, f, which):
        start = (i * FIELDS + f) * step
        return y[start : start + step, which * width : (which + 1) * width]

    return part


def left_lanes(step, width):
    return lax.broadcasted_iota(jnp.int32, (step, width), 1) & (SEG - 1) < HALF


def halo_forcing_kernel(fm, link, sa, sb, ra, rb, tiled, edge, y_ref, fe_ref, hot_ref, big):
    rows, width = link.shape[1], edge.shape[1]
    step = rows // (width // SEG)
    left, right, turned = gather_sources(sa, sb, ra, rb)
    hot = jnp.concatenate(
        [
            one_hot(left[LINK_ROW : LINK_ROW + 1], rows),
            one_hot(link[...].astype(F32), rows),
            one_hot(right[LINK_ROW : LINK_ROW + 1], rows),
        ],
        axis=0,
    )
    hot_ref[...] = hot
    k_wide = 4 * SLOT
    source = lax.broadcasted_iota(jnp.int32, (rows, FIELDS * k_wide), 1) % k_wide // SLOT

    def permuted(x):
        y = mm(hot, x)
        by_left, by_right = y[:rows], y[2 * rows :]
        outer = jnp.where(source == 0, by_left, by_right)
        by_tile = jnp.where((source == 1) | (source == 2), y[rows : 2 * rows], outer)
        return by_left.astype(BF16), by_right.astype(BF16), by_tile.astype(BF16)

    fe = mm(jnp.concatenate(turned, axis=0), edge[...])
    for f in range(FIELDS):
        fe_ref[f] = fe[f * rows : (f + 1) * rows]
    g = jnp.concatenate(turned, axis=1)
    by_left, by_right, by_tile = permuted(g)
    part = in_segments((g, by_tile, permuted(by_tile)[2], by_left, by_right), tiled, big, step)
    is_left = left_lanes(step, width)

    def at(linked, f, which):
        if linked:
            return jnp.where(is_left, part(3, f, which), part(4, f, which))
        return part(0, f, which)

    for i in range(2):
        shifted = [[at(i, f, d) for f in range(FIELDS)] for d in range(5)]
        for f in range(FIELDS):
            minus = sum(fm[e, f] * CM * shifted[1][e] for e in range(FIELDS))
            plus = sum(fm[e, f] * CM * shifted[3][e] for e in range(FIELDS))
            b = (
                C2 * shifted[0][f],
                C1 * shifted[1][f] - minus,
                (C0 + 1.0) * shifted[2][f] + CP * part(i + 1, f, 2),
                C1 * shifted[3][f] + plus,
                C2 * shifted[4][f],
                shifted[1][f],
                shifted[3][f],
                shifted[2][f],
            )
            for d, value in enumerate(b):
                y_ref[i * 8 + d, f] = value


def halo_kernel(fm, sa, sb, ra, rb, tiled, kp_ref, hot, y_in, e1_ref, e2_ref, y_ref, big, q_ref, fmc):
    for i in (1, 3, 9, 11):
        y_ref[i] = y_in[i]
    rows, width = hot.shape[1], kp_ref.shape[2]
    step = rows // (width // SEG)
    for f in range(FIELDS):
        for e in range(FIELDS):
            fmc[f, e] = fm[f, e] * CM
    _, _, turned = gather_sources(sa, sb, ra, rb)
    g = jnp.concatenate(turned, axis=1)
    y = mm(hot[...], g).astype(BF16)
    part = in_segments((g, y[:rows], y[2 * rows :]), tiled, big, step)
    is_left = left_lanes(step, width)
    for i in range(2):
        if i:
            q2 = [jnp.where(is_left, part(1, f, 0), part(2, f, 0)) for f in range(FIELDS)]
        else:
            q2 = [part(0, f, 0) for f in range(FIELDS)]
        u = CU * q2[1]
        for d, near, sign in ((1, 5, -1.0), (3, 6, 1.0)):
            inner = sum(q2[f] * y_in[i * 8 + near, f] for f in range(FIELDS))
            for f in range(FIELDS):
                value = u * y_in[i * 8 + near, f]
                if f == 1:
                    value = value + CU * inner
                y_ref[i * 8 + d, f] = y_ref[i * 8 + d, f] + sign * value
    for f in range(FIELDS):
        q_ref[f] = part(0, f, 1)
    kp = [kp_ref[i] for i in range(5)]

    def body(r, c):
        def row(ref, index):
            return jnp.broadcast_to(ref[(*index, pl.ds(r, 1), slice(None))], (8, width))

        mu, linked, d, base = [], [], [], []
        for f in range(FIELDS):
            for i, out in ((0, mu), (8, linked)):
                value = row(y_in, (i, f)) * kp[0]
                for n in range(1, 5):
                    value = value + row(y_ref if n % 2 else y_in, (i + n, f)) * kp[n]
                out.append(value)
            x = mu[f]
            m1, p1 = pltpu.roll(x, 1, 1), pltpu.roll(x, width - 1, 1)
            m2, p2 = pltpu.roll(x, 2, 1), pltpu.roll(x, width - 2, 1)
            d.append(m1 - p1)
            base.append(
                C0 * x + C1 * (m1 + p1) + C2 * (m2 + p2) + CP * linked[f]
                + row(y_in, (7, f)) * kp[2]
            )
        moved = flux(fmc, [row(q_ref, (f,)) for f in range(FIELDS)], d)
        at = pl.ds(pl.multiple_of(r * (FIELDS * 8), 8), FIELDS * 8)
        e1_ref[at, :] = halves(jnp.concatenate(mu, axis=0))
        e2_ref[at, :] = halves(
            jnp.concatenate([b - m for b, m in zip(base, moved)], axis=0)
        )
        return c

    lax.fori_loop(0, step, body, 0, unroll=8)


def main_kernel(
    cycle, fm, inv, forcing, fe, b0, k_ref, inner, outer, e1, e2, q0, q1, q2,
    out_hbm, sens_ref,
    bs, coef, mu1, mu2, dz, dze, stage, weighted, fmc, out_sems,
):
    rows, width = forcing.shape[1], forcing.shape[2]
    total = cycle * width

    for f in range(FIELDS):
        for e in range(FIELDS):
            fmc[f, e] = fm[f, e] * CM
    lane = lax.broadcasted_iota(jnp.int32, (8, width), 1)
    start = lax.axis_index("blk") * width
    weight = 1.0 + 2.0 * (lane + start).astype(F32) / total
    norm = 1.0 / math.sqrt(FIELDS * rows * total)

    def around(x, edge):
        return (
            pltpu.roll(jnp.where(lane == width - 1, edge, x), 1, 1),
            pltpu.roll(jnp.where(lane == 0, edge, x), width - 1, 1),
            pltpu.roll(jnp.where(lane >= width - 2, edge, x), 2, 1),
            pltpu.roll(jnp.where(lane < 2, edge, x), width - 2, 1),
        )

    def dense(i, z):
        rs = pl.ds(pl.multiple_of(i * 16, 16), 16)
        q = [q2[f, rs, :].astype(F32) for f in range(FIELDS)]
        for half in range(2):
            r8 = pl.ds(pl.multiple_of(i * 16 + half * 8, 8), 8)
            near = [around(forcing[f, r8, :], fe[f, r8, :]) for f in range(FIELDS)]
            mine = [x[half * 8 : half * 8 + 8] for x in q]
            minus = flux(fmc, mine, [a[0] for a in near])
            plus = flux(fmc, mine, [a[1] for a in near])
            for f in range(FIELDS):
                m1, p1, m2, p2 = near[f]
                bs[0, f, r8, :] = C2 * m2
                bs[1, f, r8, :] = C1 * m1 - minus[f]
                bs[2, f, r8, :] = C1 * p1 + plus[f]
                bs[3, f, r8, :] = C2 * p2
                w = forcing[f, r8, :] * weight
                weighted[f, r8, :] = w
                z = z + w * forcing[f, r8, :]
        return z

    def coefficients(i, c):
        rs = pl.ds(pl.multiple_of(i * 16, 16), 16)
        for n, q_ref in enumerate((q0, q1)):
            q = [q_ref[f, rs, :].astype(F32) for f in range(FIELDS)]
            u = CU * q[1]
            for e in range(FIELDS):
                coef[n, e, rs, :] = (u if e != 1 else u + u) + fmc[e, e]
            for j, f in enumerate((0, 2, 3, 4)):
                coef[n, FIELDS + j, rs, :] = CU * q[f] + fmc[f, 1]
        return c

    zero = jnp.zeros((8, width), F32)
    z = lax.fori_loop(0, rows // 16, dense, zero)
    lax.fori_loop(0, rows // 16, coefficients, 0)
    k = [k_ref[i] for i in range(5)]

    def spread(ref, index, r):
        return jnp.broadcast_to(ref[(*index, pl.ds(r, 1), slice(None))], (8, width))

    def place(r, f):
        return pl.ds(pl.multiple_of((r * FIELDS + f) * 8, 8), 8)

    def first(i, acc):
        acc = list(acc)
        for j in range(8):
            r = i * 8 + j
            for f in range(FIELDS):
                value = spread(bs, (0, f), r) * k[0] + spread(bs, (1, f), r) * k[1]
                value = value + spread(b0, (f,), r) * k[2] + spread(bs, (2, f), r) * k[3]
                value = value + spread(bs, (3, f), r) * k[4]
                mu1[place(r, f), :] = value
                acc[f] = acc[f] + value * spread(weighted, (f,), r)
        return tuple(acc)

    acc = lax.fori_loop(0, rows // 8, first, (zero,) * FIELDS)

    blocks = width // SEG
    size = rows // blocks
    fmv = [[jnp.full((8, width), fmc[f, e]) for e in range(FIELDS)] for f in range(FIELDS)]

    def products(source, edges):
        dz[...] = mm(halves(source[...]), inner[...])
        dze[...] = mm(edges[...], outer[...])

    def row(n, source, j, i, acc, keep):
        r = j * size + i
        linked = inv[r]
        chunk = i * FIELDS * 8

        def both(f, half):
            own = dz[place(r, f), half * width : (half + 1) * width]
            lanes = pl.ds(pl.multiple_of(j * (2 * width) + half * width, width), width)
            return own + dze[chunk + f * 8 : chunk + f * 8 + 8, lanes]

        d = [both(f, 0) for f in range(FIELDS)]
        for e in range(FIELDS):
            value = UNIT * both(e, 1) + CP * source[place(linked, e), :]
            for f in range(FIELDS):
                if f == e:
                    m = spread(coef, (n, e), r)
                elif e == 1:
                    m = spread(coef, (n, FIELDS + (0, 2, 3, 4).index(f)), r)
                else:
                    m = fmv[f][e]
                value = value - m * d[f]
            value = keep(r, e, value)
            acc[e] = acc[e] + value * spread(weighted, (e,), r)

    def second(j, acc):
        acc = list(acc)

        def keep(r, e, value):
            value = value + spread(forcing, (e,), r) * k[2]
            mu2[place(r, e), :] = value
            return value

        for i in range(size):
            row(1, mu1, j, i, acc, keep)
        return tuple(acc)

    products(mu1, e1)
    acc = lax.fori_loop(0, blocks, second, acc)

    def send(j):
        at = pl.ds(pl.multiple_of(j * size, size), size)
        return pltpu.make_async_copy(stage.at[:, at, :], out_hbm.at[:, at, :], out_sems.at[j])

    def third(j, acc):
        acc = list(acc)
        for part in range(size // 8):
            made = [[] for _ in range(FIELDS)]

            def keep(r, e, value):
                made[e].append(value)
                return value

            for i in range(8):
                row(0, mu2, j, part * 8 + i, acc, keep)
            at = pl.ds(pl.multiple_of(j * size + part * 8, 8), 8)
            for e in range(FIELDS):
                turned = jnp.swapaxes(jnp.stack(made[e]), 0, 1)
                for pair in range(PAIRS):
                    stage[pair * FIELDS + e, at, :] = turned[pair]
        send(j).start()
        return tuple(acc)

    products(mu2, e2)
    acc = lax.fori_loop(0, blocks, third, acc)
    source_part = jnp.sum(z, axis=0, keepdims=True) * k[2]
    acc = (sum(acc) - 2.0 * source_part) * norm
    acc = jnp.broadcast_to(jnp.sum(acc, axis=1, keepdims=True), (8, width))
    sub = lax.broadcasted_iota(jnp.int32, (8, width), 0)
    for group in range(GRP_DEV):
        mine = jnp.where(sub == group * AMP + lane, acc, 0.0)
        sens_ref[group : group + 1, :] = jnp.sum(mine, axis=0, keepdims=True)[:, :AMP]
    for j in range(blocks):
        send(j).wait()


def shift_pairs(devices, k):
    return [(i, (i + k) % devices) for i in range(devices)]


def total_over(x, axis):
    devices = lax.axis_size(axis)
    if devices & (devices - 1):
        return lax.psum(x, axis)
    bit = 1
    while bit < devices:
        x = x + lax.ppermute(x, axis, [(i, i ^ bit) for i in range(devices)])
        bit *= 2
    return x


def to_neighbours(send_a, send_b, cycle):
    return (
        lax.ppermute(send_a, "blk", [(i, i ^ 1) for i in range(cycle)]),
        lax.ppermute(
            send_b,
            "blk",
            [(i, (i + 1) % cycle if i % 2 else (i - 1) % cycle) for i in range(cycle)],
        ),
    )


def on_device(checkpoints, owner, flux_matrix, row_link, blade_group, forcing):
    n_out = lax.axis_size("out")
    cycle = lax.axis_size("blk")
    rows, width = forcing.shape[1], forcing.shape[2]
    blocks = width // SEG
    step_rows = rows // blocks
    slot = checkpoints[0]

    def struct(shape, kind=F32):
        return jax.ShapeDtypeStruct(shape, kind)

    sems = pltpu.SemaphoreType.DMA
    field = struct((FIELDS, rows, width))
    strip = struct((FIELDS * SLOT, rows), BF16)
    factors = struct((5, PAIRS, width))
    slots = [slot] + [lax.ppermute(slot, "out", shift_pairs(n_out, k)) for k in range(1, n_out)]

    def stay(x):
        return pltpu.with_memory_space_constraint(x, pltpu.HBM)

    def call(kernel, out_shape, smem, hbm, vmem, scratch, limit, flops, name, out_specs=None):
        return pl.pallas_call(
            kernel,
            out_shape=out_shape,
            in_specs=[SMEM] * len(smem) + [HBM] * len(hbm) + [VMEM] * len(vmem),
            out_specs=out_specs or (VMEM,) * len(out_shape),
            scratch_shapes=scratch,
            compiler_params=pltpu.CompilerParams(vmem_limit_bytes=limit),
            cost_estimate=cost(flops, 10**6),
            name=name,
        )(*map(stay, smem), *map(stay, hbm), *vmem)

    kept = (
        forcing, row_link, forcing_select(width), slot, state_select(width),
        *halo_selects(width), *stencil_selects(width),
    )
    made = (
        factors, factors, field, strip, strip,
        struct((rows,), jnp.int32), struct(owner.shape, jnp.int32), struct(flux_matrix.shape),
    )
    made += tuple(struct(x.shape, x.dtype) for x in kept)
    k, kp, b0, f_a, f_b, inv, owner_s, fm_s, *held = call(
        functools.partial(prepare_kernel, cycle),
        made,
        (blade_group, row_link[0], owner, flux_matrix),
        kept,
        (),
        [sems((len(kept),))],
        SMALL_LIMIT,
        10**8,
        "prepare",
        (VMEM,) * 5 + (SMEM,) * 3 + (VMEM,) * len(kept),
    )
    forcing_v, link, _, slot_v, state_sel, forcing_tiled, state_tiled, edge, inner, outer = held
    f_sent = (f_a, f_b, *to_neighbours(f_a, f_b, cycle))

    q_a, q_b, *chosen = call(
        functools.partial(strips_kernel, n_out),
        (strip, strip) + (struct(slot.shape, slot.dtype),) * STEPS,
        (owner_s,),
        (),
        (slot_v, *slots[1:], state_sel),
        [],
        SMALL_LIMIT,
        10**7,
        "strips",
    )
    q_sent = (q_a, q_b, *to_neighbours(q_a, q_b, cycle))

    y, fe, hot = call(
        halo_forcing_kernel,
        (struct((16, FIELDS, step_rows, width)), field, struct((3 * rows, rows), BF16)),
        (fm_s,),
        (),
        (link, *f_sent, forcing_tiled, edge),
        [pltpu.VMEM((blocks * 4 * SLOT, forcing_tiled.shape[1]), BF16)],
        SMALL_LIMIT,
        10**8,
        "halo_forcing",
    )
    edge_struct = struct((step_rows * FIELDS * 8, 2 * width), BF16)
    e1, e2 = call(
        halo_kernel,
        (edge_struct, edge_struct),
        (fm_s,),
        (),
        (*q_sent, state_tiled, kp, hot, y),
        [
            like(y),
            pltpu.VMEM((blocks * 4 * SLOT, state_tiled.shape[1]), BF16),
            pltpu.VMEM((FIELDS, step_rows, width), F32),
            pltpu.SMEM((FIELDS, FIELDS), F32),
        ],
        SMALL_LIMIT,
        10**8,
        "halo",
    )
    pairs_fields = PAIRS * FIELDS
    flat = rows * FIELDS * PAIRS
    adjoint, sens = call(
        functools.partial(main_kernel, cycle),
        (struct((pairs_fields, rows, width)), struct((GRP_DEV, AMP))),
        (fm_s, inv),
        (),
        (forcing_v, fe, b0, k, inner, outer, e1, e2, *chosen),
        [
            pltpu.VMEM((4, FIELDS, rows, width), F32),
            pltpu.VMEM((STEPS - 1, 2 * FIELDS - 1, rows, width), F32),
            pltpu.VMEM((flat, width), F32),
            pltpu.VMEM((flat, width), F32),
            pltpu.VMEM((flat, 2 * width), F32),
            pltpu.VMEM((flat // blocks, blocks * 2 * width), F32),
            pltpu.VMEM((pairs_fields, rows, width), F32),
            pltpu.VMEM((FIELDS, rows, width), F32),
            pltpu.SMEM((FIELDS, FIELDS), F32),
            sems((blocks,)),
        ],
        VMEM_LIMIT,
        10**9,
        "steps",
        (HBM, VMEM),
    )

    return adjoint.reshape(GRP_DEV, AMP, FIELDS, rows, width), total_over(sens, "blk")


def solution(mesh):
    return jax.shard_map(
        on_device,
        mesh=mesh,
        in_specs=(P("out", None, None, "blk"), P(), P(), P("blk", None), P(), P(None, None, "blk")),
        out_specs=(P("out", None, None, None, "blk"), P("out", None)),
        check_vma=False,
    )
```

```python
import functools
import math

import jax
import jax.numpy as jnp
import numpy as np
from jax import lax
from jax.experimental import pallas as pl
from jax.experimental.pallas import tpu as pltpu
from jax.sharding import PartitionSpec as P

FIELDS = 5
BLADES = 96
AMP = 4
GRP_DEV = 2
STEPS = 3
PAIRS = GRP_DEV * AMP

time_step = 0.25
second_diff = 0.1
fourth_diff = 0.02
link_weight = 0.5
two_pi = 2.0 * math.pi

C0 = 1.0 - time_step * (2.0 * second_diff + 6.0 * fourth_diff + link_weight)
C1 = time_step * (second_diff + 4.0 * fourth_diff)
C2 = -time_step * fourth_diff
CP = time_step * link_weight
CM = 0.5 * time_step
CU = 0.25 * time_step

FW = 6
QW = 4
PARTS = 3
SLOT = 32
LINK_ROW = PARTS * FW
SEG = 16
HALF = SEG // 2
VMEM_LIMIT = 40 * 2**20
SMALL_LIMIT = 16 * 2**20
PARTS_LAST = 1

VMEM = pl.BlockSpec(memory_space=pltpu.VMEM)
SMEM = pl.BlockSpec(memory_space=pltpu.SMEM)
HBM = pl.BlockSpec(memory_space=pltpu.HBM)
UNIT = time_step * fourth_diff
CENTRE = round(C0 / UNIT)
NEAR = round(C1 / UNIT)
F32 = jnp.float32
BF16 = jnp.bfloat16
NT = (((1,), (1,)), ((), ()))
TN = (((0,), (0,)), ((), ()))
NN = (((1,), (0,)), ((), ()))


def mm(a, b, dims=NN):
    return lax.dot_general(a, b, dims, preferred_element_type=F32)


def split3(x):
    hi = x.astype(BF16)
    rest = x - hi.astype(F32)
    mid = rest.astype(BF16)
    return hi, mid, (rest - mid.astype(F32)).astype(BF16)


def exact_mm(a, x):
    hi, mid, lo = split3(x)
    return mm(a, hi) + mm(a, mid) + mm(a, lo)


def fetch(moves, sems):
    copies = [pltpu.make_async_copy(src, dst, sems.at[i]) for i, (src, dst) in enumerate(moves)]
    for copy in copies:
        copy.start()
    return copies


def arrive(copies):
    for copy in copies:
        copy.wait()


def like(x):
    return pltpu.VMEM(x.shape, x.dtype)


def cost(flops, moved):
    return pl.CostEstimate(flops=flops, bytes_accessed=moved, transcendentals=0)


def forcing_select(width):
    out = np.zeros((PARTS, width, width), np.float32)
    for part in range(PARTS):
        for j in range(FW):
            out[part, j, part * FW + j] = 1.0
            out[part, width - FW + j, SLOT + part * FW + j] = 1.0
    return out.reshape(PARTS * width, width).astype(jnp.bfloat16)


def state_select(width):
    out = np.zeros((2 * SLOT, STEPS, width), np.float32)
    for n in range(STEPS):
        for j in range(QW):
            out[n * QW + j, n, j] = 1.0
            out[SLOT + n * QW + j, n, width - QW + j] = 1.0
    return out.reshape(2 * SLOT, STEPS * width).astype(jnp.bfloat16)


def give(send_a, send_b, f, both):
    even = lax.axis_index("blk") % 2 == 0
    left, right = both[:SLOT], both[SLOT:]
    send_a[f * SLOT : (f + 1) * SLOT] = jnp.where(even, right, left).astype(BF16)
    send_b[f * SLOT : (f + 1) * SLOT] = jnp.where(even, left, right).astype(BF16)


def strips_kernel(n_out, *refs):
    owner = refs[0]
    slots = refs[1 : 1 + n_out]
    sel, send_a, send_b, *chosen = refs[1 + n_out :]
    me = lax.axis_index("out")
    for n, target in enumerate(chosen):
        which = (me - owner[n] + n_out) % n_out
        for s, slot in enumerate(slots):

            @pl.when(which == s)
            def _():
                target[...] = slot[...]

    for f in range(FIELDS):
        give(send_a, send_b, f, mm(sel[...], jnp.concatenate([q[f] for q in chosen], axis=1), NT))


def column_factor(columns, pair, start, total, group_base, blade_group):
    scaled = columns * BLADES
    first = ((start + total - HALF) * BLADES) // total - BLADES
    group = jnp.full(columns.shape, -1, jnp.int32)
    numerator = jnp.zeros(columns.shape, jnp.int32)
    width = columns.shape[-1]
    for j in range((width + SEG) * BLADES // total + 2):
        blade = first + j
        inside = (scaled >= blade * total) & (scaled < (blade + 1) * total)
        group = jnp.where(inside, blade_group[(blade + BLADES) % BLADES], group)
        numerator = jnp.where(inside, scaled - blade * total, numerator)
    phase = numerator.astype(F32) / total
    amp = pair & (AMP - 1)
    order = ((amp >> 1) + 1).astype(F32)
    angle = two_pi * order * phase
    harmonic = jnp.where((amp & 1) == 0, jnp.cos(angle), jnp.sin(angle))
    return jnp.where(group == group_base + pair // AMP, harmonic, 0.0)


def column_weight(columns, total):
    columns = jnp.where(columns < 0, columns + total, columns)
    columns = jnp.where(columns >= total, columns - total, columns)
    return 1.0 + 2.0 * columns.astype(F32) / total


def flux(fm, q, d):
    inner = q[0] * d[0]
    for f in range(1, FIELDS):
        inner = inner + q[f] * d[f]
    u = q[1] * CU
    out = []
    for e in range(FIELDS):
        value = u * d[e]
        for f in range(FIELDS):
            value = value + fm[f, e] * d[f]
        if e == 1:
            value = value + CU * inner
        out.append(value)
    return out


def prepare_kernel(cycle, blade_group, link_s, *refs):
    owner, fm = refs[:2]
    kept = refs[2 : (len(refs) - 12) // 2 + 2]
    k_ref, kp_ref, b0_ref, v0_ref, send_a, send_b, inv_ref, owner_out, fm_out, *held, sems = refs[
        2 + len(kept) :
    ]
    copies = fetch(zip(kept, held), sems)
    for i in range(owner.shape[0]):
        owner_out[i] = owner[i]
    for f in range(FIELDS):
        for e in range(FIELDS):
            fm_out[f, e] = fm[f, e]
    forcing, link, sel = held[:3]
    rows, width = forcing.shape[1:]
    total = cycle * width
    start = lax.axis_index("blk") * width

    def invert(r, c):
        inv_ref[link_s[r]] = r
        return c

    lax.fori_loop(0, rows, invert, 0, unroll=8)
    lane = lax.broadcasted_iota(jnp.int32, (8, width), 1)
    sub = lax.broadcasted_iota(jnp.int32, (8, width), 0)
    p = lane & (SEG - 1)
    packed = jnp.where(p < HALF, p - QW, width - QW + p - HALF) + start
    args = (start, total, lax.axis_index("out") * GRP_DEV, blade_group)
    for i in range(5):
        k_ref[i] = column_factor(lane + start + (i - 2), sub, *args)
        kp_ref[i] = column_factor(packed + (i - 2), sub, *args)
    arrive(copies[:3])
    links = link[...].astype(F32)
    parts = [split3(forcing[f]) for f in range(FIELDS)]
    hot = one_hot(links, rows)
    flat = jnp.concatenate(sum(parts, ()), axis=1)
    linked = mm(hot, flat)
    linking = mm(hot, flat, TN)
    weight = column_weight(lax.broadcasted_iota(jnp.int32, (1, width), 1) + start, total)
    chosen = mm(
        jnp.concatenate([jnp.concatenate(three, axis=1) for three in parts], axis=0), sel[...]
    )
    row = lax.broadcasted_iota(jnp.int32, (2 * SLOT, rows), 0)
    links = jnp.broadcast_to(links, row.shape)
    for f in range(FIELDS):

        def moved(x):
            three = [x[:, (f * PARTS + i) * width : (f * PARTS + i + 1) * width] for i in range(PARTS)]
            return three[0] + three[1] + three[2]

        b0_ref[f] = (C0 + 1.0) * forcing[f] + CP * moved(linked)
        v0_ref[f] = (C0 * forcing[f] + CP * moved(linking)) * weight
        turned = chosen[f * rows : (f + 1) * rows].T[: 2 * SLOT]
        if f == 0:
            turned = jnp.where(row % SLOT == LINK_ROW, links, turned)
        give(send_a, send_b, f, turned)
    arrive(copies[3:])


def one_hot(links, rows):
    row = lax.broadcasted_iota(jnp.int32, (rows, rows), 0).astype(F32)
    return jnp.where(links == row, 1.0, 0.0).astype(BF16)


def halo_selects(width):
    blocks = width // SEG
    forcing_sel = np.zeros((4 * SLOT, 5, SEG), np.float32)
    state_sel = np.zeros((4 * SLOT, 2, SEG), np.float32)
    edge = np.zeros((4 * SLOT, width), np.float32)

    def place(column, size):
        if column < 0:
            return 0, column + size
        if column < size:
            return 1, column
        if column < width:
            return 2, column - (width - size)
        return 3, column - width

    def forcing_rows(column):
        source, j = place(column, FW)
        return [source * SLOT + part * FW + j for part in range(PARTS)] if 0 <= j < FW else []

    for p in range(SEG):
        column = p - QW if p < HALF else width - QW + p - HALF
        for i in range(5):
            for row in forcing_rows(column + i - 2):
                forcing_sel[row, i, p] = 1.0
        source, j = place(column, QW)
        for i, n in ((0, STEPS - 1), (1, STEPS - 2)):
            state_sel[source * SLOT + n * QW + j, i, p] = 1.0
    for lane, column in ((width - 2, -2), (width - 1, -1), (0, width), (1, width + 1)):
        for row in forcing_rows(column):
            edge[row, lane] = 1.0
    state_edge = np.zeros((4 * SLOT, width), np.float32)
    for lane, column in ((width - 1, -1), (0, width)):
        source, j = place(column, QW)
        state_edge[source * SLOT + j, lane] = 1.0

    def tiled(x):
        return np.repeat(x[:, :, None, :], blocks, axis=2).reshape(4 * SLOT, -1)

    return tuple(
        x.astype(jnp.bfloat16) for x in (tiled(forcing_sel), tiled(state_sel), edge, state_edge)
    )


def stencil_selects(width):
    blocks = width // SEG
    inner = np.zeros((2, width, 2 * width), np.float32)
    outer = np.zeros((blocks, 2, width, 2 * width), np.float32)

    def spread(column):
        out = []
        for c, w in ((column + 1, 1.0), (column - 1, -1.0)):
            if 0 <= c < width:
                out.append((c, w))
        for c, w in (
            (column, CENTRE),
            (column - 1, NEAR),
            (column + 1, NEAR),
            (column - 2, -1.0),
            (column + 2, -1.0),
        ):
            if 0 <= c < width:
                out.append((width + c, w))
        return out

    for column in range(width):
        for lane, w in spread(column):
            inner[:, column, lane] = w
    for j in range(blocks):
        for p, column in ((2, -2), (3, -1), (HALF + QW, width), (HALF + QW + 1, width + 1)):
            for lane, w in spread(column):
                outer[j, :, j * SEG + p, lane] = w
    return (
        inner.reshape(2 * width, 2 * width).astype(jnp.bfloat16),
        outer.reshape(blocks, 2 * width, 2 * width)
        .swapaxes(0, 1)
        .reshape(2 * width, blocks * 2 * width)
        .astype(jnp.bfloat16),
    )


def halves(x):
    hi = x.astype(BF16)
    return jnp.concatenate([hi, (x - hi.astype(F32)).astype(BF16)], axis=1)


def gather_sources(sa, sb, ra, rb):
    even = lax.axis_index("blk") % 2 == 0
    sa, sb, ra, rb = (x[...].astype(F32) for x in (sa, sb, ra, rb))
    own_left, own_right = jnp.where(even, sb, sa), jnp.where(even, sa, sb)
    left, right = jnp.where(even, rb, ra), jnp.where(even, ra, rb)
    turned = []
    for f in range(FIELDS):
        s = slice(f * SLOT, (f + 1) * SLOT)
        g = jnp.concatenate([left[s], own_left[s], own_right[s], right[s]], axis=0)
        turned.append(g.T.astype(BF16))
    return left, right, turned


def in_segments(sets, tiled, big, step):
    blocks = big.shape[0] // (4 * SLOT)
    width = blocks * SEG
    lane_block = lax.broadcasted_iota(jnp.int32, tiled.shape, 1) % width // SEG
    for j in range(blocks):
        big[j * 4 * SLOT : (j + 1) * 4 * SLOT, :] = jnp.where(
            lane_block == j, tiled[...].astype(F32), 0.0
        ).astype(BF16)
    pieces = []
    for x in sets:
        for f in range(FIELDS):
            mine = x[:, f * 4 * SLOT : (f + 1) * 4 * SLOT]
            pieces.append(
                jnp.concatenate([mine[j * step : (j + 1) * step] for j in range(blocks)], axis=1)
            )
    y = mm(jnp.concatenate(pieces, axis=0), big[...])

    def part(i, f, which):
        start = (i * FIELDS + f) * step
        return y[start : start + step, which * width : (which + 1) * width]

    return part


def left_lanes(step, width):
    return lax.broadcasted_iota(jnp.int32, (step, width), 1) & (SEG - 1) < HALF


def halo_forcing_kernel(fm, link, sa, sb, ra, rb, tiled, edge, y_ref, fe_ref, hot_ref, big):
    rows, width = link.shape[1], edge.shape[1]
    step = rows // (width // SEG)
    left, right, turned = gather_sources(sa, sb, ra, rb)
    hot = jnp.concatenate(
        [
            one_hot(left[LINK_ROW : LINK_ROW + 1], rows),
            one_hot(link[...].astype(F32), rows),
            one_hot(right[LINK_ROW : LINK_ROW + 1], rows),
        ],
        axis=0,
    )
    hot_ref[...] = hot
    k_wide = 4 * SLOT
    source = lax.broadcasted_iota(jnp.int32, (rows, FIELDS * k_wide), 1) % k_wide // SLOT

    def permuted(x):
        y = mm(hot, x)
        by_left, by_right = y[:rows], y[2 * rows :]
        outer = jnp.where(source == 0, by_left, by_right)
        by_tile = jnp.where((source == 1) | (source == 2), y[rows : 2 * rows], outer)
        return by_left.astype(BF16), by_right.astype(BF16), by_tile.astype(BF16)

    fe = mm(jnp.concatenate(turned, axis=0), edge[...])
    for f in range(FIELDS):
        fe_ref[f] = fe[f * rows : (f + 1) * rows]
    g = jnp.concatenate(turned, axis=1)
    by_left, by_right, by_tile = permuted(g)
    part = in_segments((g, by_tile, permuted(by_tile)[2], by_left, by_right), tiled, big, step)
    is_left = left_lanes(step, width)

    def at(linked, f, which):
        if linked:
            return jnp.where(is_left, part(3, f, which), part(4, f, which))
        return part(0, f, which)

    for i in range(2):
        shifted = [[at(i, f, d) for f in range(FIELDS)] for d in range(5)]
        for f in range(FIELDS):
            minus = sum(fm[e, f] * CM * shifted[1][e] for e in range(FIELDS))
            plus = sum(fm[e, f] * CM * shifted[3][e] for e in range(FIELDS))
            b = (
                C2 * shifted[0][f],
                C1 * shifted[1][f] - minus,
                (C0 + 1.0) * shifted[2][f] + CP * part(i + 1, f, 2),
                C1 * shifted[3][f] + plus,
                C2 * shifted[4][f],
                shifted[1][f],
                shifted[3][f],
                shifted[2][f],
            )
            for d, value in enumerate(b):
                y_ref[i * 8 + d, f] = value


def halo_kernel(
    fm, sa, sb, ra, rb, tiled, edge, kp_ref, hot, y_in,
    e1_ref, e2_ref, qe_ref, y_ref, big, q_ref, fmc,
):
    for i in (1, 3, 9, 11):
        y_ref[i] = y_in[i]
    rows, width = hot.shape[1], kp_ref.shape[2]
    step = rows // (width // SEG)
    for f in range(FIELDS):
        for e in range(FIELDS):
            fmc[f, e] = fm[f, e] * CM
    _, _, turned = gather_sources(sa, sb, ra, rb)
    g = jnp.concatenate(turned, axis=1)
    qe = mm(jnp.concatenate(turned, axis=0), edge[...])
    for f in range(FIELDS):
        qe_ref[f] = qe[f * rows : (f + 1) * rows]
    y = mm(hot[...], g).astype(BF16)
    part = in_segments((g, y[:rows], y[2 * rows :]), tiled, big, step)
    is_left = left_lanes(step, width)
    for i in range(2):
        if i:
            q2 = [jnp.where(is_left, part(1, f, 0), part(2, f, 0)) for f in range(FIELDS)]
        else:
            q2 = [part(0, f, 0) for f in range(FIELDS)]
        u = CU * q2[1]
        for d, near, sign in ((1, 5, -1.0), (3, 6, 1.0)):
            inner = sum(q2[f] * y_in[i * 8 + near, f] for f in range(FIELDS))
            for f in range(FIELDS):
                value = u * y_in[i * 8 + near, f]
                if f == 1:
                    value = value + CU * inner
                y_ref[i * 8 + d, f] = y_ref[i * 8 + d, f] + sign * value
    for f in range(FIELDS):
        q_ref[f] = part(0, f, 1)
    kp = [kp_ref[i] for i in range(5)]

    def body(r, c):
        def row(ref, index):
            return jnp.broadcast_to(ref[(*index, pl.ds(r, 1), slice(None))], (8, width))

        mu, linked, d, base = [], [], [], []
        for f in range(FIELDS):
            for i, out in ((0, mu), (8, linked)):
                value = row(y_in, (i, f)) * kp[0]
                for n in range(1, 5):
                    value = value + row(y_ref if n % 2 else y_in, (i + n, f)) * kp[n]
                out.append(value)
            x = mu[f]
            m1, p1 = pltpu.roll(x, 1, 1), pltpu.roll(x, width - 1, 1)
            m2, p2 = pltpu.roll(x, 2, 1), pltpu.roll(x, width - 2, 1)
            d.append(m1 - p1)
            base.append(
                C0 * x + C1 * (m1 + p1) + C2 * (m2 + p2) + CP * linked[f]
                + row(y_in, (7, f)) * kp[2]
            )
        moved = flux(fmc, [row(q_ref, (f,)) for f in range(FIELDS)], d)
        at = pl.ds(pl.multiple_of(r * (FIELDS * 8), 8), FIELDS * 8)
        e1_ref[at, :] = halves(jnp.concatenate(mu, axis=0))
        e2_ref[at, :] = halves(
            jnp.concatenate([b - m for b, m in zip(base, moved)], axis=0)
        )
        return c

    lax.fori_loop(0, step, body, 0, unroll=8)


def shift_edges(x, edge, lane, width):
    return (
        pltpu.roll(jnp.where(lane == width - 1, edge, x), 1, 1),
        pltpu.roll(jnp.where(lane == 0, edge, x), width - 1, 1),
    )


def spread(ref, index, r):
    return jnp.broadcast_to(ref[(*index, pl.ds(r, 1), slice(None))], (8, ref.shape[-1]))


def place(r, f):
    return pl.ds(pl.multiple_of((r * FIELDS + f) * 8, 8), 8)


def scaled_matrix(fm, fmc):
    for f in range(FIELDS):
        for e in range(FIELDS):
            fmc[f, e] = fm[f, e] * CM


def matrix_rows(fmc, width):
    return [[jnp.full((8, width), fmc[f, e]) for e in range(FIELDS)] for f in range(FIELDS)]


def stencil_products(dz, dze, source, first, count, edges, inner, outer, lanes):
    dz[...] = mm(halves(source[first : first + count, :]), inner[...])
    dze[...] = mm(edges[...], outer[:, lanes])


def step_row(source, dz, dze, coef, fmv, linked, r, local, j, chunk):
    width = source.shape[1]

    def both(f, half):
        own = dz[place(local, f), half * width : (half + 1) * width]
        lanes = pl.ds(pl.multiple_of(j * (2 * width) + half * width, width), width)
        return own + dze[chunk + f * 8 : chunk + f * 8 + 8, lanes]

    d = [both(f, 0) for f in range(FIELDS)]
    out = []
    for e in range(FIELDS):
        value = UNIT * both(e, 1) + CP * source[place(linked, e), :]
        for f in range(FIELDS):
            if f == e:
                m = spread(coef, (e,), r)
            elif e == 1:
                m = spread(coef, (FIELDS + (0, 2, 3, 4).index(f),), r)
            else:
                m = fmv[f][e]
            value = value - m * d[f]
        out.append(value)
    return out


def first_steps_kernel(
    cycle, fm, inv, forcing, fe, b0, v0, qe, k_ref, inner, outer, e1, q0, q1, q2,
    mu2, coef0, sens_ref,
    bs, coef1, mu1, dz, dze, weighted, heavy, fmc,
):
    rows, width = forcing.shape[1], forcing.shape[2]
    total = cycle * width
    blocks = width // SEG
    size = rows // blocks
    scaled_matrix(fm, fmc)
    lane = lax.broadcasted_iota(jnp.int32, (8, width), 1)
    start = lax.axis_index("blk") * width
    norm = 1.0 / math.sqrt(FIELDS * rows * total)
    weight = {d: column_weight(lane + (start + d), total) for d in range(-2, 3)}
    beside = column_weight(jnp.where(lane < width // 2, lane + width, lane - width) + start, total)

    def dense(i, z):
        rs = pl.ds(pl.multiple_of(i * 16, 16), 16)
        for n, (q_ref, coef) in enumerate(((q0, coef0), (q1, coef1))):
            q = [q_ref[f, rs, :].astype(F32) for f in range(FIELDS)]
            u = CU * q[1]
            for e in range(FIELDS):
                coef[e, rs, :] = (u if e != 1 else u + u) + fmc[e, e]
            for j, f in enumerate((0, 2, 3, 4)):
                coef[FIELDS + j, rs, :] = CU * q[f] + fmc[f, 1]
        both_q = [[q[f, rs, :].astype(F32) for f in range(FIELDS)] for q in (q0, q2)]
        for half in range(2):
            r8 = pl.ds(pl.multiple_of(i * 16 + half * 8, 8), 8)
            mine, last = [[x[half * 8 : half * 8 + 8] for x in q] for q in both_q]
            near, w, we = [], [], []
            for f in range(FIELDS):
                x, edge = forcing[f, r8, :], fe[f, r8, :]
                near.append(
                    (
                        *shift_edges(x, edge, lane, width),
                        pltpu.roll(jnp.where(lane >= width - 2, edge, x), 2, 1),
                        pltpu.roll(jnp.where(lane < 2, edge, x), width - 2, 1),
                    )
                )
                w.append(x * weight[0])
                we.append(edge * beside)
            minus = flux(fmc, last, [a[0] for a in near])
            plus = flux(fmc, last, [a[1] for a in near])
            q_edge = [qe[f, r8, :] for f in range(FIELDS)]
            for f in range(FIELDS):
                m1, p1, m2, p2 = near[f]
                bs[0, f, r8, :] = C2 * m2
                bs[1, f, r8, :] = C1 * m1 - minus[f]
                bs[2, f, r8, :] = C1 * p1 + plus[f]
                bs[3, f, r8, :] = C2 * p2
                weighted[f, r8, :] = w[f]
                z = z + w[f] * forcing[f, r8, :]
                x = CU * (mine[1] * w[f] + mine[f] * w[1])
                xe = CU * (q_edge[1] * we[f] + q_edge[f] * we[1])
                for e in range(FIELDS):
                    x = x + fmc[f, e] * w[e]
                    xe = xe + fmc[f, e] * we[e]
                before, after = shift_edges(x, xe, lane, width)
                turned = v0[f, r8, :] + C1 * (m1 * weight[-1] + p1 * weight[1])
                turned = turned + C2 * (m2 * weight[-2] + p2 * weight[2])
                heavy[f, r8, :] = w[f] + turned + (before - after)
        return z

    zero = jnp.zeros((8, width), F32)
    z = lax.fori_loop(0, rows // 16, dense, zero)
    k = [k_ref[i] for i in range(5)]

    def first(j, acc):
        acc = list(acc)
        for i in range(size):
            r = j * size + i
            for f in range(FIELDS):
                value = spread(bs, (0, f), r) * k[0] + spread(bs, (1, f), r) * k[1]
                value = value + spread(b0, (f,), r) * k[2] + spread(bs, (2, f), r) * k[3]
                value = value + spread(bs, (3, f), r) * k[4]
                mu1[place(r, f), :] = value
                acc[f] = acc[f] + value * spread(weighted, (f,), r)
        return tuple(acc)

    acc = lax.fori_loop(0, blocks, first, (zero,) * FIELDS)
    fmv = matrix_rows(fmc, width)
    stencil_products(dz, dze, mu1, 0, rows * FIELDS * 8, e1, inner, outer, slice(None))

    def second(j, acc):
        acc = list(acc)
        for i in range(size):
            r = j * size + i
            made = step_row(mu1, dz, dze, coef1, fmv, inv[r], r, r, j, i * FIELDS * 8)
            for f, value in enumerate(made):
                value = value + spread(forcing, (f,), r) * k[2]
                mu2[place(r, f), :] = value
                acc[f] = acc[f] + value * spread(heavy, (f,), r)
        return tuple(acc)

    acc = lax.fori_loop(0, blocks, second, acc)
    source_part = jnp.sum(z, axis=0, keepdims=True) * k[2]
    acc = (sum(acc) - 2.0 * source_part) * norm
    acc = jnp.broadcast_to(jnp.sum(acc, axis=1, keepdims=True), (8, width))
    sub = lax.broadcasted_iota(jnp.int32, (8, width), 0)
    for group in range(GRP_DEV):
        mine = jnp.where(sub == group * AMP + lane, acc, 0.0)
        sens_ref[group : group + 1, :] = jnp.sum(mine, axis=0, keepdims=True)[:, :AMP]


def last_step_kernel(part, parts, fm, inv, *refs):
    mu2, coef0, e2, inner, outer = refs[-11:-6]
    out_hbm, dz, dze, stage, fmc, out_sems = refs[-6:]
    rows, width = coef0.shape[1:]
    blocks = width // SEG
    size = rows // blocks
    here = blocks // parts
    begin = part * here
    scaled_matrix(fm, fmc)
    fmv = matrix_rows(fmc, width)
    chunk = size * FIELDS * 8
    lanes = slice(begin * 2 * width, (begin + here) * 2 * width)
    stencil_products(dz, dze, mu2, begin * chunk, here * chunk, e2, inner, outer, lanes)

    def send(j):
        at = pl.ds(pl.multiple_of(j * 8, 8), 8)
        to = pl.ds(pl.multiple_of(begin * size + j * 8, 8), 8)
        return pltpu.make_async_copy(stage.at[:, at, :], out_hbm.at[:, to, :], out_sems.at[j])

    def third(j, c):
        for half in range(size // 8):
            made = []
            for i in range(half * 8, half * 8 + 8):
                local = j * size + i
                r = begin * size + local
                made.append(
                    step_row(mu2, dz, dze, coef0, fmv, inv[r], r, local, j, i * FIELDS * 8)
                )
            at = pl.ds(pl.multiple_of(j * size + half * 8, 8), 8)
            for e in range(FIELDS):
                turned = jnp.swapaxes(jnp.stack([x[e] for x in made]), 0, 1)
                for pair in range(PAIRS):
                    stage[pair * FIELDS + e, at, :] = turned[pair]
            send(j * (size // 8) + half).start()
        return c

    lax.fori_loop(0, here, third, 0)
    for j in range(here * size // 8):
        send(j).wait()


def shift_pairs(devices, k):
    return [(i, (i + k) % devices) for i in range(devices)]


def round_over(x, axis, bit):
    return x + lax.ppermute(x, axis, [(i, i ^ bit) for i in range(lax.axis_size(axis))])


def to_neighbours(send_a, send_b, cycle):
    return (
        lax.ppermute(send_a, "blk", [(i, i ^ 1) for i in range(cycle)]),
        lax.ppermute(
            send_b,
            "blk",
            [(i, (i + 1) % cycle if i % 2 else (i - 1) % cycle) for i in range(cycle)],
        ),
    )


def on_device(checkpoints, owner, flux_matrix, row_link, blade_group, forcing):
    n_out = lax.axis_size("out")
    cycle = lax.axis_size("blk")
    rows, width = forcing.shape[1], forcing.shape[2]
    blocks = width // SEG
    step_rows = rows // blocks
    slot = checkpoints[0]

    def struct(shape, kind=F32):
        return jax.ShapeDtypeStruct(shape, kind)

    sems = pltpu.SemaphoreType.DMA
    field = struct((FIELDS, rows, width))
    strip = struct((FIELDS * SLOT, rows), BF16)
    factors = struct((5, PAIRS, width))
    slots = [slot] + [lax.ppermute(slot, "out", shift_pairs(n_out, k)) for k in range(1, n_out)]

    def stay(x):
        return pltpu.with_memory_space_constraint(x, pltpu.HBM)

    def call(kernel, out_shape, smem, hbm, vmem, scratch, limit, flops, name, out_specs=None):
        return pl.pallas_call(
            kernel,
            out_shape=out_shape,
            in_specs=[SMEM] * len(smem) + [HBM] * len(hbm) + [VMEM] * len(vmem),
            out_specs=out_specs or (VMEM,) * len(out_shape),
            scratch_shapes=scratch,
            compiler_params=pltpu.CompilerParams(vmem_limit_bytes=limit),
            cost_estimate=cost(flops, 10**6),
            name=name,
        )(*map(stay, smem), *map(stay, hbm), *vmem)

    kept = (
        forcing, row_link, forcing_select(width), slot, state_select(width),
        *halo_selects(width), *stencil_selects(width),
    )
    made = (
        factors, factors, field, field, strip, strip,
        struct((rows,), jnp.int32), struct(owner.shape, jnp.int32), struct(flux_matrix.shape),
    )
    made += tuple(struct(x.shape, x.dtype) for x in kept)
    k, kp, b0, v0, f_a, f_b, inv, owner_s, fm_s, *held = call(
        functools.partial(prepare_kernel, cycle),
        made,
        (blade_group, row_link[0], owner, flux_matrix),
        kept,
        (),
        [sems((len(kept),))],
        SMALL_LIMIT,
        10**8,
        "prepare",
        (VMEM,) * 6 + (SMEM,) * 3 + (VMEM,) * len(kept),
    )
    forcing_v, link, _, slot_v, state_sel, *held = held
    forcing_tiled, state_tiled, edge, state_edge, inner, outer = held
    f_sent = (f_a, f_b, *to_neighbours(f_a, f_b, cycle))

    q_a, q_b, *chosen = call(
        functools.partial(strips_kernel, n_out),
        (strip, strip) + (struct(slot.shape, slot.dtype),) * STEPS,
        (owner_s,),
        (),
        (slot_v, *slots[1:], state_sel),
        [],
        SMALL_LIMIT,
        10**7,
        "strips",
    )
    q_sent = (q_a, q_b, *to_neighbours(q_a, q_b, cycle))

    y, fe, hot = call(
        halo_forcing_kernel,
        (struct((16, FIELDS, step_rows, width)), field, struct((3 * rows, rows), BF16)),
        (fm_s,),
        (),
        (link, *f_sent, forcing_tiled, edge),
        [pltpu.VMEM((blocks * 4 * SLOT, forcing_tiled.shape[1]), BF16)],
        SMALL_LIMIT,
        10**8,
        "halo_forcing",
    )
    edge_struct = struct((step_rows * FIELDS * 8, 2 * width), BF16)
    e1, e2, qe = call(
        halo_kernel,
        (edge_struct, edge_struct, field),
        (fm_s,),
        (),
        (*q_sent, state_tiled, state_edge, kp, hot, y),
        [
            like(y),
            pltpu.VMEM((blocks * 4 * SLOT, state_tiled.shape[1]), BF16),
            pltpu.VMEM((FIELDS, step_rows, width), F32),
            pltpu.SMEM((FIELDS, FIELDS), F32),
        ],
        SMALL_LIMIT,
        10**8,
        "halo",
    )
    flat = rows * FIELDS * PAIRS
    coefficients = (2 * FIELDS - 1, rows, width)
    outside = (flat // blocks, blocks * 2 * width)
    mu2, coef0, sens = call(
        functools.partial(first_steps_kernel, cycle),
        (struct((flat, width)), struct(coefficients), struct((GRP_DEV, AMP))),
        (fm_s, inv),
        (),
        (forcing_v, fe, b0, v0, qe, k, inner, outer, e1, *chosen),
        [
            pltpu.VMEM((4, FIELDS, rows, width), F32),
            pltpu.VMEM(coefficients, F32),
            pltpu.VMEM((flat, width), F32),
            pltpu.VMEM((flat, 2 * width), F32),
            pltpu.VMEM(outside, F32),
            pltpu.VMEM((FIELDS, rows, width), F32),
            pltpu.VMEM((FIELDS, rows, width), F32),
            pltpu.SMEM((FIELDS, FIELDS), F32),
        ],
        VMEM_LIMIT,
        10**9,
        "first_steps",
    )

    pairs_fields = PAIRS * FIELDS
    bits = [1 << i for i in reversed(range(cycle.bit_length() - 1))]
    exact = 1 << len(bits) == cycle
    if not exact:
        sens = lax.psum(sens, "blk")
    adjoint = None
    for part in range(PARTS_LAST):
        if part:
            adjoint, sens = lax.optimization_barrier((adjoint, sens))
        if exact and bits:
            sens = round_over(sens, "blk", bits.pop(0))
        before = () if adjoint is None else (adjoint,)
        adjoint = pl.pallas_call(
            functools.partial(last_step_kernel, part, PARTS_LAST),
            out_shape=struct((pairs_fields, rows, width)),
            in_specs=[SMEM] * 2 + [HBM] * len(before) + [VMEM] * 5,
            out_specs=HBM,
            scratch_shapes=[
                pltpu.VMEM((flat // PARTS_LAST, 2 * width), F32),
                pltpu.VMEM((flat // blocks, blocks // PARTS_LAST * 2 * width), F32),
                pltpu.VMEM((pairs_fields, rows // PARTS_LAST, width), F32),
                pltpu.SMEM((FIELDS, FIELDS), F32),
                sems((rows // 8 // PARTS_LAST,)),
            ],
            input_output_aliases={2: 0} if before else {},
            compiler_params=pltpu.CompilerParams(vmem_limit_bytes=SMALL_LIMIT),
            cost_estimate=cost(10**9, 10**6),
            name="last_step",
        )(fm_s, inv, *before, mu2, coef0, e2, inner, outer)
    for bit in bits if exact else ():
        sens = round_over(sens, "blk", bit)
    return adjoint.reshape(GRP_DEV, AMP, FIELDS, rows, width), sens


def solution(mesh):
    return jax.shard_map(
        on_device,
        mesh=mesh,
        in_specs=(P("out", None, None, "blk"), P(), P(), P("blk", None), P(), P(None, None, "blk")),
        out_specs=(P("out", None, None, None, "blk"), P("out", None)),
        check_vma=False,
    )
```

```python
import functools
import math

import jax
import jax.numpy as jnp
import numpy as np
from jax import lax
from jax.experimental import pallas as pl
from jax.experimental.pallas import tpu as pltpu
from jax.sharding import PartitionSpec as P

FIELDS = 5
BLADES = 96
AMP = 4
GRP_DEV = 2
STEPS = 3
PAIRS = GRP_DEV * AMP

time_step = 0.25
second_diff = 0.1
fourth_diff = 0.02
link_weight = 0.5
two_pi = 2.0 * math.pi

C0 = 1.0 - time_step * (2.0 * second_diff + 6.0 * fourth_diff + link_weight)
C1 = time_step * (second_diff + 4.0 * fourth_diff)
C2 = -time_step * fourth_diff
CP = time_step * link_weight
CM = 0.5 * time_step
CU = 0.25 * time_step

FW = 6
QW = 4
PARTS = 3
SLOT = 32
LINK_ROW = PARTS * FW
SEG = 16
HALF = SEG // 2
HALO_LANES = (2, 3, 5, 12, 13, 14)
VMEM_LIMIT = 40 * 2**20
SMALL_LIMIT = 16 * 2**20

VMEM = pl.BlockSpec(memory_space=pltpu.VMEM)
SMEM = pl.BlockSpec(memory_space=pltpu.SMEM)
HBM = pl.BlockSpec(memory_space=pltpu.HBM)
UNIT = time_step * fourth_diff
NEAR = round(C1 / UNIT)
F32 = jnp.float32
BF16 = jnp.bfloat16
NT = (((1,), (1,)), ((), ()))
TN = (((0,), (0,)), ((), ()))
NN = (((1,), (0,)), ((), ()))


def mm(a, b, dims=NN):
    return lax.dot_general(a, b, dims, preferred_element_type=F32)


def split3(x):
    hi = x.astype(BF16)
    rest = x - hi.astype(F32)
    mid = rest.astype(BF16)
    return hi, mid, (rest - mid.astype(F32)).astype(BF16)


def exact_mm(a, x):
    hi, mid, lo = split3(x)
    return mm(a, hi) + mm(a, mid) + mm(a, lo)


def fetch(moves, sems):
    copies = [pltpu.make_async_copy(src, dst, sems.at[i]) for i, (src, dst) in enumerate(moves)]
    for copy in copies:
        copy.start()
    return copies


def arrive(copies):
    for copy in copies:
        copy.wait()


def like(x):
    return pltpu.VMEM(x.shape, x.dtype)


def cost(flops, moved):
    return pl.CostEstimate(flops=flops, bytes_accessed=moved, transcendentals=0)


def forcing_select(width):
    out = np.zeros((PARTS, width, width), np.float32)
    for part in range(PARTS):
        for j in range(FW):
            out[part, j, part * FW + j] = 1.0
            out[part, width - FW + j, SLOT + part * FW + j] = 1.0
    return out.reshape(PARTS * width, width).astype(jnp.bfloat16)


def state_select(width):
    out = np.zeros((2 * SLOT, STEPS, width), np.float32)
    for n in range(STEPS):
        for j in range(QW):
            out[n * QW + j, n, j] = 1.0
            out[SLOT + n * QW + j, n, width - QW + j] = 1.0
    return out.reshape(2 * SLOT, STEPS * width).astype(jnp.bfloat16)


def give(send_a, send_b, f, both):
    even = lax.axis_index("blk") % 2 == 0
    left, right = both[:SLOT], both[SLOT:]
    send_a[f * SLOT : (f + 1) * SLOT] = jnp.where(even, right, left).astype(BF16)
    send_b[f * SLOT : (f + 1) * SLOT] = jnp.where(even, left, right).astype(BF16)


def strips_kernel(n_out, *refs):
    owner = refs[0]
    slots = refs[1 : 1 + n_out]
    sel, send_a, send_b, *chosen = refs[1 + n_out :]
    me = lax.axis_index("out")
    for n, target in enumerate(chosen):
        which = (me - owner[n] + n_out) % n_out
        for s, slot in enumerate(slots):

            @pl.when(which == s)
            def _():
                target[...] = slot[...]

    for f in range(FIELDS):
        give(send_a, send_b, f, mm(sel[...], jnp.concatenate([q[f] for q in chosen], axis=1), NT))


def column_factor(columns, pair, start, total, group_base, blade_group):
    scaled = columns * BLADES
    first = ((start + total - HALF) * BLADES) // total - BLADES
    group = jnp.full(columns.shape, -1, jnp.int32)
    numerator = jnp.zeros(columns.shape, jnp.int32)
    width = columns.shape[-1]
    for j in range((width + SEG) * BLADES // total + 2):
        blade = first + j
        inside = (scaled >= blade * total) & (scaled < (blade + 1) * total)
        group = jnp.where(inside, blade_group[(blade + BLADES) % BLADES], group)
        numerator = jnp.where(inside, scaled - blade * total, numerator)
    phase = numerator.astype(F32) / total
    amp = pair & (AMP - 1)
    order = ((amp >> 1) + 1).astype(F32)
    angle = two_pi * order * phase
    harmonic = jnp.where((amp & 1) == 0, jnp.cos(angle), jnp.sin(angle))
    return jnp.where(group == group_base + pair // AMP, harmonic, 0.0)


def column_weight(columns, total):
    columns = jnp.where(columns < 0, columns + total, columns)
    columns = jnp.where(columns >= total, columns - total, columns)
    return 1.0 + 2.0 * columns.astype(F32) / total


def flux(fm, q, d):
    inner = q[0] * d[0]
    for f in range(1, FIELDS):
        inner = inner + q[f] * d[f]
    u = q[1] * CU
    out = []
    for e in range(FIELDS):
        value = u * d[e]
        for f in range(FIELDS):
            value = value + fm[f, e] * d[f]
        if e == 1:
            value = value + CU * inner
        out.append(value)
    return out


def prepare_kernel(cycle, blade_group, link_s, *refs):
    owner, fm = refs[:2]
    kept = refs[2 : (len(refs) - 12) // 2 + 2]
    k_ref, kp_ref, b0_ref, v0_ref, send_a, send_b, inv_ref, owner_out, fm_out, *held, sems = refs[
        2 + len(kept) :
    ]
    copies = fetch(zip(kept, held), sems)
    for i in range(owner.shape[0]):
        owner_out[i] = owner[i]
    for f in range(FIELDS):
        for e in range(FIELDS):
            fm_out[f, e] = fm[f, e]
    forcing, link, sel = held[:3]
    rows, width = forcing.shape[1:]
    total = cycle * width
    start = lax.axis_index("blk") * width

    def invert(r, c):
        inv_ref[link_s[r]] = r
        return c

    lax.fori_loop(0, rows, invert, 0, unroll=8)
    lane = lax.broadcasted_iota(jnp.int32, (8, width), 1)
    sub = lax.broadcasted_iota(jnp.int32, (8, width), 0)
    p = lane & (SEG - 1)
    packed = jnp.where(p < HALF, p - QW, width - QW + p - HALF) + start
    args = (start, total, lax.axis_index("out") * GRP_DEV, blade_group)
    for i in range(5):
        k_ref[i] = column_factor(lane + start + (i - 2), sub, *args)
        kp_ref[i] = column_factor(packed + (i - 2), sub, *args)
    arrive(copies[:3])
    links = link[...].astype(F32)
    parts = [split3(forcing[f]) for f in range(FIELDS)]
    hot = one_hot(links, rows)
    flat = jnp.concatenate(sum(parts, ()), axis=1)
    linked = mm(hot, flat)
    linking = mm(hot, flat, TN)
    weight = column_weight(lax.broadcasted_iota(jnp.int32, (1, width), 1) + start, total)
    chosen = mm(
        jnp.concatenate([jnp.concatenate(three, axis=1) for three in parts], axis=0), sel[...]
    )
    row = lax.broadcasted_iota(jnp.int32, (2 * SLOT, rows), 0)
    links = jnp.broadcast_to(links, row.shape)
    for f in range(FIELDS):

        def moved(x):
            three = [x[:, (f * PARTS + i) * width : (f * PARTS + i + 1) * width] for i in range(PARTS)]
            return three[0] + three[1] + three[2]

        b0_ref[f] = (C0 + 1.0) * forcing[f] + CP * moved(linked)
        v0_ref[f] = (C0 * forcing[f] + CP * moved(linking)) * weight
        turned = chosen[f * rows : (f + 1) * rows].T[: 2 * SLOT]
        if f == 0:
            turned = jnp.where(row % SLOT == LINK_ROW, links, turned)
        give(send_a, send_b, f, turned)
    arrive(copies[3:])


def one_hot(links, rows):
    row = lax.broadcasted_iota(jnp.int32, (rows, rows), 0).astype(F32)
    return jnp.where(links == row, 1.0, 0.0).astype(BF16)


def halo_selects(width):
    blocks = width // SEG
    forcing_sel = np.zeros((4 * SLOT, 5, SEG), np.float32)
    state_sel = np.zeros((4 * SLOT, 2, SEG), np.float32)
    edge = np.zeros((4 * SLOT, width), np.float32)

    def place(column, size):
        if column < 0:
            return 0, column + size
        if column < size:
            return 1, column
        if column < width:
            return 2, column - (width - size)
        return 3, column - width

    def forcing_rows(column):
        source, j = place(column, FW)
        return [source * SLOT + part * FW + j for part in range(PARTS)] if 0 <= j < FW else []

    for p in range(SEG):
        column = p - QW if p < HALF else width - QW + p - HALF
        for i in range(5):
            for row in forcing_rows(column + i - 2):
                forcing_sel[row, i, p] = 1.0
        source, j = place(column, QW)
        for i, n in ((0, STEPS - 1), (1, STEPS - 2)):
            state_sel[source * SLOT + n * QW + j, i, p] = 1.0
    for lane, column in ((width - 2, -2), (width - 1, -1), (0, width), (1, width + 1)):
        for row in forcing_rows(column):
            edge[row, lane] = 1.0
    state_edge = np.zeros((4 * SLOT, width), np.float32)
    for lane, column in ((width - 1, -1), (0, width)):
        source, j = place(column, QW)
        state_edge[source * SLOT + j, lane] = 1.0

    def tiled(x):
        return np.repeat(x[:, :, None, :], blocks, axis=2).reshape(4 * SLOT, -1)

    return tuple(
        x.astype(jnp.bfloat16) for x in (tiled(forcing_sel), tiled(state_sel), edge, state_edge)
    )


def stencil_selects(width):
    blocks = width // SEG
    out = np.zeros((blocks, 2, width, 2 * width), np.float32)

    def spread(column):
        near = ((1, 1.0), (-1, -1.0))
        far = ((-1, NEAR), (1, NEAR), (-2, -1.0), (2, -1.0))
        pairs = [(column + d, w) for d, w in near if 0 <= column + d < width]
        return pairs + [(width + column + d, w) for d, w in far if 0 <= column + d < width]

    for column in range(width):
        for lane, w in spread(column):
            out[:, :, column, lane] = w
    for j in range(blocks):
        for p, column in ((2, -2), (3, -1), (HALF + QW, width), (HALF + QW + 1, width + 1)):
            for held in (p, p + 2) if column in (-1, width) else (p,):
                out[j, 1, j * SEG + held] = 0.0
                for to, w in spread(column):
                    out[j, 1, j * SEG + held, to] = w
    return out.reshape(blocks, 2 * width, 2 * width).astype(jnp.bfloat16)


def high(x):
    return x.astype(BF16).astype(F32)


def gather_sources(sa, sb, ra, rb):
    even = lax.axis_index("blk") % 2 == 0
    sa, sb, ra, rb = (x[...].astype(F32) for x in (sa, sb, ra, rb))
    own_left, own_right = jnp.where(even, sb, sa), jnp.where(even, sa, sb)
    left, right = jnp.where(even, rb, ra), jnp.where(even, ra, rb)
    turned = []
    for f in range(FIELDS):
        s = slice(f * SLOT, (f + 1) * SLOT)
        g = jnp.concatenate([left[s], own_left[s], own_right[s], right[s]], axis=0)
        turned.append(g.T.astype(BF16))
    return left, right, turned


def in_segments(sets, tiled, big, step):
    blocks = big.shape[0] // (4 * SLOT)
    width = blocks * SEG
    lane_block = lax.broadcasted_iota(jnp.int32, tiled.shape, 1) % width // SEG
    for j in range(blocks):
        big[j * 4 * SLOT : (j + 1) * 4 * SLOT, :] = jnp.where(
            lane_block == j, tiled[...].astype(F32), 0.0
        ).astype(BF16)
    pieces = []
    for x in sets:
        for f in range(FIELDS):
            mine = x[:, f * 4 * SLOT : (f + 1) * 4 * SLOT]
            pieces.append(
                jnp.concatenate([mine[j * step : (j + 1) * step] for j in range(blocks)], axis=1)
            )
    y = mm(jnp.concatenate(pieces, axis=0), big[...])

    def part(i, f, which):
        start = (i * FIELDS + f) * step
        return y[start : start + step, which * width : (which + 1) * width]

    return part


def left_lanes(step, width):
    return lax.broadcasted_iota(jnp.int32, (step, width), 1) & (SEG - 1) < HALF


def halo_forcing_kernel(fm, link, sa, sb, ra, rb, tiled, edge, y_ref, fe_ref, hot_ref, big):
    rows, width = link.shape[1], edge.shape[1]
    step = rows // (width // SEG)
    left, right, turned = gather_sources(sa, sb, ra, rb)
    hot = jnp.concatenate(
        [
            one_hot(left[LINK_ROW : LINK_ROW + 1], rows),
            one_hot(link[...].astype(F32), rows),
            one_hot(right[LINK_ROW : LINK_ROW + 1], rows),
        ],
        axis=0,
    )
    hot_ref[...] = hot
    k_wide = 4 * SLOT
    source = lax.broadcasted_iota(jnp.int32, (rows, FIELDS * k_wide), 1) % k_wide // SLOT

    def permuted(x):
        y = mm(hot, x)
        by_left, by_right = y[:rows], y[2 * rows :]
        outer = jnp.where(source == 0, by_left, by_right)
        by_tile = jnp.where((source == 1) | (source == 2), y[rows : 2 * rows], outer)
        return by_left.astype(BF16), by_right.astype(BF16), by_tile.astype(BF16)

    fe = mm(jnp.concatenate(turned, axis=0), edge[...])
    for f in range(FIELDS):
        fe_ref[f] = fe[f * rows : (f + 1) * rows]
    g = jnp.concatenate(turned, axis=1)
    by_left, by_right, by_tile = permuted(g)
    part = in_segments((g, by_tile, permuted(by_tile)[2], by_left, by_right), tiled, big, step)
    is_left = left_lanes(step, width)

    def at(linked, f, which):
        if linked:
            return jnp.where(is_left, part(3, f, which), part(4, f, which))
        return part(0, f, which)

    for i in range(2):
        shifted = [[at(i, f, d) for f in range(FIELDS)] for d in range(5)]
        for f in range(FIELDS):
            minus = sum(fm[e, f] * CM * shifted[1][e] for e in range(FIELDS))
            plus = sum(fm[e, f] * CM * shifted[3][e] for e in range(FIELDS))
            b = (
                C2 * shifted[0][f],
                C1 * shifted[1][f] - minus,
                (C0 + 1.0) * shifted[2][f] + CP * part(i + 1, f, 2),
                C1 * shifted[3][f] + plus,
                C2 * shifted[4][f],
                shifted[1][f],
                shifted[3][f],
                shifted[2][f],
            )
            for d, value in enumerate(b):
                y_ref[i * 8 + d, f] = value


def halo_kernel(
    fm, sa, sb, ra, rb, tiled, edge, kp_ref, hot, y_in,
    e1_ref, e2_ref, qe_ref, y_ref, big, q_ref, fmc,
):
    for i in (1, 3, 9, 11):
        y_ref[i] = y_in[i]
    rows, width = hot.shape[1], kp_ref.shape[2]
    step = rows // (width // SEG)
    for f in range(FIELDS):
        for e in range(FIELDS):
            fmc[f, e] = fm[f, e] * CM
    _, _, turned = gather_sources(sa, sb, ra, rb)
    g = jnp.concatenate(turned, axis=1)
    qe = mm(jnp.concatenate(turned, axis=0), edge[...])
    for f in range(FIELDS):
        qe_ref[f] = qe[f * rows : (f + 1) * rows]
    y = mm(hot[...], g).astype(BF16)
    part = in_segments((g, y[:rows], y[2 * rows :]), tiled, big, step)
    is_left = left_lanes(step, width)
    for i in range(2):
        if i:
            q2 = [jnp.where(is_left, part(1, f, 0), part(2, f, 0)) for f in range(FIELDS)]
        else:
            q2 = [part(0, f, 0) for f in range(FIELDS)]
        u = CU * q2[1]
        for d, near, sign in ((1, 5, -1.0), (3, 6, 1.0)):
            inner = sum(q2[f] * y_in[i * 8 + near, f] for f in range(FIELDS))
            for f in range(FIELDS):
                value = u * y_in[i * 8 + near, f]
                if f == 1:
                    value = value + CU * inner
                y_ref[i * 8 + d, f] = y_ref[i * 8 + d, f] + sign * value
    for f in range(FIELDS):
        q_ref[f] = part(0, f, 1)
    kp = [kp_ref[i] for i in range(5)]
    p = lax.broadcasted_iota(jnp.int32, (8, width), 1) & (SEG - 1)
    holds_high = (p != 5) & (p != 14)

    def both_halves(x):
        top = high(x)
        return jnp.where(holds_high, top, pltpu.roll(x - top, 2, 1))


    def body(r, c):
        def row(ref, index):
            return jnp.broadcast_to(ref[(*index, pl.ds(r, 1), slice(None))], (8, width))

        mu, linked, d, base = [], [], [], []
        for f in range(FIELDS):
            for i, out in ((0, mu), (8, linked)):
                value = row(y_in, (i, f)) * kp[0]
                for n in range(1, 5):
                    value = value + row(y_ref if n % 2 else y_in, (i + n, f)) * kp[n]
                out.append(value)
            x = mu[f]
            m1, p1 = pltpu.roll(x, 1, 1), pltpu.roll(x, width - 1, 1)
            m2, p2 = pltpu.roll(x, 2, 1), pltpu.roll(x, width - 2, 1)
            d.append(m1 - p1)
            base.append(
                C0 * x + C1 * (m1 + p1) + C2 * (m2 + p2) + CP * linked[f]
                + row(y_in, (7, f)) * kp[2]
            )
        moved = flux(fmc, [row(q_ref, (f,)) for f in range(FIELDS)], d)
        at = pl.ds(pl.multiple_of(r * (FIELDS * 8), 8), FIELDS * 8)
        e1_ref[at, :] = jnp.concatenate([both_halves(x) for x in mu], axis=0)
        e2_ref[at, :] = jnp.concatenate(
            [both_halves(b - m) for b, m in zip(base, moved)], axis=0
        )
        return c

    lax.fori_loop(0, step, body, 0, unroll=16)


def shift_edges(x, edge, lane, width):
    return (
        pltpu.roll(jnp.where(lane == width - 1, edge, x), 1, 1),
        pltpu.roll(jnp.where(lane == 0, edge, x), width - 1, 1),
    )


def spread(ref, index, r):
    return jnp.broadcast_to(ref[(*index, pl.ds(r, 1), slice(None))], (8, ref.shape[-1]))


def place(r, f):
    return pl.ds(pl.multiple_of((r * FIELDS + f) * 8, 8), 8)


def scaled_matrix(fm, fmc):
    for f in range(FIELDS):
        for e in range(FIELDS):
            fmc[f, e] = fm[f, e] * CM


def matrix_rows(fmc, width):
    return [[jnp.full((8, width), fmc[f, e]) for e in range(FIELDS)] for f in range(FIELDS)]


def stencil_products(dz, source, edges, products):
    width = source.shape[1]
    count = edges.shape[0]
    lane = lax.broadcasted_iota(jnp.int32, (count, width), 1)
    p = lane & (SEG - 1)
    halo = functools.reduce(jnp.logical_or, [p == held for held in HALO_LANES])
    for j in range(products.shape[0]):
        x = source[j * count : (j + 1) * count, :]
        top = x.astype(BF16)
        rest = jnp.where(halo & (lane // SEG == j), edges[...], x - top.astype(F32))
        dz[j * count : (j + 1) * count, :] = mm(
            jnp.concatenate([top, rest.astype(BF16)], axis=1), products[j]
        )


def step_row(source, dz, coef, fmv, linked, r):
    width = source.shape[1]

    d = [dz[place(r, f), :width] for f in range(FIELDS)]
    out = []
    for e in range(FIELDS):
        value = C0 * source[place(r, e), :] + UNIT * dz[place(r, e), width:]
        value = value + CP * source[place(linked, e), :]
        for f in range(FIELDS):
            if f == e:
                m = spread(coef, (e,), r)
            elif e == 1:
                m = spread(coef, (FIELDS + (0, 2, 3, 4).index(f),), r)
            else:
                m = fmv[f][e]
            value = value - m * d[f]
        out.append(value)
    return out


def first_steps_kernel(
    cycle, fm, inv, forcing, fe, b0, v0, qe, k_ref, products, e1, q0, q1, q2,
    mu2, coef0, sens_ref,
    bs, coef1, mu1, dz, weighted, heavy, fmc,
):
    rows, width = forcing.shape[1], forcing.shape[2]
    total = cycle * width
    blocks = width // SEG
    size = rows // blocks
    scaled_matrix(fm, fmc)
    lane = lax.broadcasted_iota(jnp.int32, (8, width), 1)
    start = lax.axis_index("blk") * width
    norm = 1.0 / math.sqrt(FIELDS * rows * total)
    weight = {d: column_weight(lane + (start + d), total) for d in range(-2, 3)}
    beside = column_weight(jnp.where(lane < width // 2, lane + width, lane - width) + start, total)

    def dense(i, z):
        rs = pl.ds(pl.multiple_of(i * 16, 16), 16)
        for n, (q_ref, coef) in enumerate(((q0, coef0), (q1, coef1))):
            q = [q_ref[f, rs, :].astype(F32) for f in range(FIELDS)]
            u = CU * q[1]
            for e in range(FIELDS):
                coef[e, rs, :] = (u if e != 1 else u + u) + fmc[e, e]
            for j, f in enumerate((0, 2, 3, 4)):
                coef[FIELDS + j, rs, :] = CU * q[f] + fmc[f, 1]
        both_q = [[q[f, rs, :].astype(F32) for f in range(FIELDS)] for q in (q0, q2)]
        for half in range(2):
            r8 = pl.ds(pl.multiple_of(i * 16 + half * 8, 8), 8)
            mine, last = [[x[half * 8 : half * 8 + 8] for x in q] for q in both_q]
            near, w, we = [], [], []
            for f in range(FIELDS):
                x, edge = forcing[f, r8, :], fe[f, r8, :]
                near.append(
                    (
                        *shift_edges(x, edge, lane, width),
                        pltpu.roll(jnp.where(lane >= width - 2, edge, x), 2, 1),
                        pltpu.roll(jnp.where(lane < 2, edge, x), width - 2, 1),
                    )
                )
                w.append(x * weight[0])
                we.append(edge * beside)
            minus = flux(fmc, last, [a[0] for a in near])
            plus = flux(fmc, last, [a[1] for a in near])
            q_edge = [qe[f, r8, :] for f in range(FIELDS)]
            for f in range(FIELDS):
                m1, p1, m2, p2 = near[f]
                bs[0, f, r8, :] = C2 * m2
                bs[1, f, r8, :] = C1 * m1 - minus[f]
                bs[2, f, r8, :] = C1 * p1 + plus[f]
                bs[3, f, r8, :] = C2 * p2
                weighted[f, r8, :] = w[f]
                z = z + w[f] * forcing[f, r8, :]
                x = CU * (mine[1] * w[f] + mine[f] * w[1])
                xe = CU * (q_edge[1] * we[f] + q_edge[f] * we[1])
                for e in range(FIELDS):
                    x = x + fmc[f, e] * w[e]
                    xe = xe + fmc[f, e] * we[e]
                before, after = shift_edges(x, xe, lane, width)
                turned = v0[f, r8, :] + C1 * (m1 * weight[-1] + p1 * weight[1])
                turned = turned + C2 * (m2 * weight[-2] + p2 * weight[2])
                heavy[f, r8, :] = w[f] + turned + (before - after)
        return z

    zero = jnp.zeros((8, width), F32)
    z = lax.fori_loop(0, rows // 16, dense, zero)
    k = [k_ref[i] for i in range(5)]

    def first(j, acc):
        acc = list(acc)
        for i in range(size):
            r = j * size + i
            for f in range(FIELDS):
                value = spread(bs, (0, f), r) * k[0] + spread(bs, (1, f), r) * k[1]
                value = value + spread(b0, (f,), r) * k[2] + spread(bs, (2, f), r) * k[3]
                value = value + spread(bs, (3, f), r) * k[4]
                mu1[place(r, f), :] = value
                acc[f] = acc[f] + value * spread(weighted, (f,), r)
        return tuple(acc)

    acc = lax.fori_loop(0, blocks, first, (zero,) * FIELDS)
    fmv = matrix_rows(fmc, width)
    stencil_products(dz, mu1, e1, products)

    def second(j, acc):
        acc = list(acc)
        for i in range(size):
            r = j * size + i
            made = step_row(mu1, dz, coef1, fmv, inv[r], r)
            for f, value in enumerate(made):
                value = value + spread(forcing, (f,), r) * k[2]
                mu2[place(r, f), :] = value
                acc[f] = acc[f] + value * spread(heavy, (f,), r)
        return tuple(acc)

    acc = lax.fori_loop(0, blocks, second, acc)
    source_part = jnp.sum(z, axis=0, keepdims=True) * k[2]
    acc = (sum(acc) - 2.0 * source_part) * norm
    acc = jnp.broadcast_to(jnp.sum(acc, axis=1, keepdims=True), (8, width))
    sub = lax.broadcasted_iota(jnp.int32, (8, width), 0)
    for group in range(GRP_DEV):
        mine = jnp.where(sub == group * AMP + lane, acc, 0.0)
        sens_ref[group : group + 1, :] = jnp.sum(mine, axis=0, keepdims=True)[:, :AMP]


def last_step_kernel(fm, inv, mu2, coef0, e2, products, out_hbm, dz, stage, fmc, out_sems):
    rows, width = coef0.shape[1:]
    blocks = width // SEG
    size = rows // blocks
    scaled_matrix(fm, fmc)
    fmv = matrix_rows(fmc, width)
    stencil_products(dz, mu2, e2, products)

    def send(j):
        at = pl.ds(pl.multiple_of(j * 8, 8), 8)
        return pltpu.make_async_copy(stage.at[:, at, :], out_hbm.at[:, at, :], out_sems.at[j])

    def third(j, c):
        for half in range(size // 8):
            r0 = j * size + half * 8
            made = [step_row(mu2, dz, coef0, fmv, inv[r0 + i], r0 + i) for i in range(8)]
            at = pl.ds(pl.multiple_of(r0, 8), 8)
            for e in range(FIELDS):
                turned = jnp.swapaxes(jnp.stack([x[e] for x in made]), 0, 1)
                for pair in range(PAIRS):
                    stage[pair * FIELDS + e, at, :] = turned[pair]
            send(j * (size // 8) + half).start()
        return c

    lax.fori_loop(0, blocks, third, 0)
    for j in range(rows // 8):
        send(j).wait()


def shift_pairs(devices, k):
    return [(i, (i + k) % devices) for i in range(devices)]


def round_over(x, axis, bit):
    return x + lax.ppermute(x, axis, [(i, i ^ bit) for i in range(lax.axis_size(axis))])


def to_neighbours(send_a, send_b, cycle):
    return (
        lax.ppermute(send_a, "blk", [(i, i ^ 1) for i in range(cycle)]),
        lax.ppermute(
            send_b,
            "blk",
            [(i, (i + 1) % cycle if i % 2 else (i - 1) % cycle) for i in range(cycle)],
        ),
    )


def on_device(checkpoints, owner, flux_matrix, row_link, blade_group, forcing):
    n_out = lax.axis_size("out")
    cycle = lax.axis_size("blk")
    rows, width = forcing.shape[1], forcing.shape[2]
    blocks = width // SEG
    step_rows = rows // blocks
    slot = checkpoints[0]

    def struct(shape, kind=F32):
        return jax.ShapeDtypeStruct(shape, kind)

    sems = pltpu.SemaphoreType.DMA
    field = struct((FIELDS, rows, width))
    strip = struct((FIELDS * SLOT, rows), BF16)
    factors = struct((5, PAIRS, width))
    slots = [slot] + [lax.ppermute(slot, "out", shift_pairs(n_out, k)) for k in range(1, n_out)]

    def stay(x):
        return pltpu.with_memory_space_constraint(x, pltpu.HBM)

    def call(kernel, out_shape, smem, hbm, vmem, scratch, limit, flops, name, out_specs=None):
        return pl.pallas_call(
            kernel,
            out_shape=out_shape,
            in_specs=[SMEM] * len(smem) + [HBM] * len(hbm) + [VMEM] * len(vmem),
            out_specs=out_specs or (VMEM,) * len(out_shape),
            scratch_shapes=scratch,
            compiler_params=pltpu.CompilerParams(vmem_limit_bytes=limit),
            cost_estimate=cost(flops, 10**6),
            name=name,
        )(*map(stay, smem), *map(stay, hbm), *vmem)

    kept = (
        forcing, row_link, forcing_select(width), slot, state_select(width),
        *halo_selects(width), stencil_selects(width),
    )
    made = (
        factors, factors, field, field, strip, strip,
        struct((rows,), jnp.int32), struct(owner.shape, jnp.int32), struct(flux_matrix.shape),
    )
    made += tuple(struct(x.shape, x.dtype) for x in kept)
    k, kp, b0, v0, f_a, f_b, inv, owner_s, fm_s, *held = call(
        functools.partial(prepare_kernel, cycle),
        made,
        (blade_group, row_link[0], owner, flux_matrix),
        kept,
        (),
        [sems((len(kept),))],
        SMALL_LIMIT,
        10**8,
        "prepare",
        (VMEM,) * 6 + (SMEM,) * 3 + (VMEM,) * len(kept),
    )
    forcing_v, link, _, slot_v, state_sel, *held = held
    forcing_tiled, state_tiled, edge, state_edge, products = held
    f_sent = (f_a, f_b, *to_neighbours(f_a, f_b, cycle))

    q_a, q_b, *chosen = call(
        functools.partial(strips_kernel, n_out),
        (strip, strip) + (struct(slot.shape, slot.dtype),) * STEPS,
        (owner_s,),
        (),
        (slot_v, *slots[1:], state_sel),
        [],
        SMALL_LIMIT,
        10**7,
        "strips",
    )
    q_sent = (q_a, q_b, *to_neighbours(q_a, q_b, cycle))

    y, fe, hot = call(
        halo_forcing_kernel,
        (struct((16, FIELDS, step_rows, width)), field, struct((3 * rows, rows), BF16)),
        (fm_s,),
        (),
        (link, *f_sent, forcing_tiled, edge),
        [pltpu.VMEM((blocks * 4 * SLOT, forcing_tiled.shape[1]), BF16)],
        SMALL_LIMIT,
        10**8,
        "halo_forcing",
    )
    flat = rows * FIELDS * PAIRS
    coefficients = (2 * FIELDS - 1, rows, width)
    edges = (step_rows * FIELDS * 8, width)
    halo_operands = (*q_sent, state_tiled, state_edge, kp, hot, y)
    halo_scratch = [
        pltpu.VMEM(edges, F32),
        pltpu.VMEM((FIELDS, rows, width), F32),
        like(y),
        pltpu.VMEM((blocks * 4 * SLOT, state_tiled.shape[1]), BF16),
        pltpu.VMEM((FIELDS, step_rows, width), F32),
        pltpu.SMEM((FIELDS, FIELDS), F32),
    ]

    def halo_and_first_steps(fm, inv, *refs):
        halo_in, refs = refs[: len(halo_operands)], refs[len(halo_operands) :]
        forcing, fe, b0, v0, k_ref, products, q0, q1, q2 = refs[:9]
        mu2, coef0, sens, e2, e1, qe, *work = refs[9 : 13 + len(halo_scratch)]
        halo_kernel(fm, *halo_in, e1, e2, qe, *work)
        first_steps_kernel(
            cycle, fm, inv, forcing, fe, b0, v0, qe, k_ref, products, e1, q0, q1, q2,
            mu2, coef0, sens, *refs[13 + len(halo_scratch) :],
        )

    mu2, coef0, sens, e2 = call(
        halo_and_first_steps,
        (
            struct((flat, width)), struct(coefficients), struct((GRP_DEV, AMP)), struct(edges),
        ),
        (fm_s, inv),
        (),
        (*halo_operands, forcing_v, fe, b0, v0, k, products, *chosen),
        halo_scratch
        + [
            pltpu.VMEM((4, FIELDS, rows, width), F32),
            pltpu.VMEM(coefficients, F32),
            pltpu.VMEM((flat, width), F32),
            pltpu.VMEM((flat, 2 * width), F32),
            pltpu.VMEM((FIELDS, rows, width), F32),
            pltpu.VMEM((FIELDS, rows, width), F32),
            pltpu.SMEM((FIELDS, FIELDS), F32),
        ],
        VMEM_LIMIT,
        10**9,
        "first_steps",
    )

    pairs_fields = PAIRS * FIELDS
    bits = [1 << i for i in reversed(range(cycle.bit_length() - 1))]
    exact = 1 << len(bits) == cycle
    if not exact:
        sens = lax.psum(sens, "blk")
    if exact and bits:
        sens = round_over(sens, "blk", bits.pop(0))
    (adjoint,) = call(
        last_step_kernel,
        (struct((pairs_fields, rows, width)),),
        (fm_s, inv),
        (),
        (mu2, coef0, e2, products),
        [
            pltpu.VMEM((flat, 2 * width), F32),
            pltpu.VMEM((pairs_fields, rows, width), F32),
            pltpu.SMEM((FIELDS, FIELDS), F32),
            sems((rows // 8,)),
        ],
        VMEM_LIMIT,
        10**9,
        "last_step",
        (HBM,),
    )
    for bit in bits if exact else ():
        sens = round_over(sens, "blk", bit)
    return adjoint.reshape(GRP_DEV, AMP, FIELDS, rows, width), sens


def solution(mesh):
    return jax.shard_map(
        on_device,
        mesh=mesh,
        in_specs=(P("out", None, None, "blk"), P(), P(), P("blk", None), P(), P(None, None, "blk")),
        out_specs=(P("out", None, None, None, "blk"), P("out", None)),
        check_vma=False,
    )
```

```python
import functools
import math

import jax
import jax.numpy as jnp
import numpy as np
from jax import lax
from jax.experimental import pallas as pl
from jax.experimental.pallas import tpu as pltpu
from jax.sharding import PartitionSpec as P

FIELDS = 5
BLADES = 96
AMP = 4
GRP_DEV = 2
STEPS = 3
PAIRS = GRP_DEV * AMP

time_step = 0.25
second_diff = 0.1
fourth_diff = 0.02
link_weight = 0.5
two_pi = 2.0 * math.pi

C0 = 1.0 - time_step * (2.0 * second_diff + 6.0 * fourth_diff + link_weight)
C1 = time_step * (second_diff + 4.0 * fourth_diff)
C2 = -time_step * fourth_diff
CP = time_step * link_weight
CM = 0.5 * time_step
CU = 0.25 * time_step

FW = 6
QW = 4
PARTS = 3
SLOT = 32
LINK_ROW = PARTS * FW
SEG = 16
HALF = SEG // 2
HALO_LANES = (2, 3, 5, 12, 13, 14)
VMEM_LIMIT = 40 * 2**20
SMALL_LIMIT = 16 * 2**20

VMEM = pl.BlockSpec(memory_space=pltpu.VMEM)
SMEM = pl.BlockSpec(memory_space=pltpu.SMEM)
HBM = pl.BlockSpec(memory_space=pltpu.HBM)
UNIT = time_step * fourth_diff
NEAR = round(C1 / UNIT)
F32 = jnp.float32
BF16 = jnp.bfloat16
NT = (((1,), (1,)), ((), ()))
TN = (((0,), (0,)), ((), ()))
NN = (((1,), (0,)), ((), ()))


def mm(a, b, dims=NN):
    return lax.dot_general(a, b, dims, preferred_element_type=F32)


def split3(x):
    hi = x.astype(BF16)
    rest = x - hi.astype(F32)
    mid = rest.astype(BF16)
    return hi, mid, (rest - mid.astype(F32)).astype(BF16)


def exact_mm(a, x):
    hi, mid, lo = split3(x)
    return mm(a, hi) + mm(a, mid) + mm(a, lo)


def fetch(moves, sems):
    copies = [pltpu.make_async_copy(src, dst, sems.at[i]) for i, (src, dst) in enumerate(moves)]
    for copy in copies:
        copy.start()
    return copies


def arrive(copies):
    for copy in copies:
        copy.wait()


def like(x):
    return pltpu.VMEM(x.shape, x.dtype)


def cost(flops, moved):
    return pl.CostEstimate(flops=flops, bytes_accessed=moved, transcendentals=0)


def forcing_select(width):
    out = np.zeros((PARTS, width, width), np.float32)
    for part in range(PARTS):
        for j in range(FW):
            out[part, j, part * FW + j] = 1.0
            out[part, width - FW + j, SLOT + part * FW + j] = 1.0
    return out.reshape(PARTS * width, width).astype(jnp.bfloat16)


def state_select(width):
    out = np.zeros((2 * SLOT, STEPS, width), np.float32)
    for n in range(STEPS):
        for j in range(QW):
            out[n * QW + j, n, j] = 1.0
            out[SLOT + n * QW + j, n, width - QW + j] = 1.0
    return out.reshape(2 * SLOT, STEPS * width).astype(jnp.bfloat16)


def give(send_a, send_b, f, both):
    even = lax.axis_index("blk") % 2 == 0
    left, right = both[:SLOT], both[SLOT:]
    send_a[f * SLOT : (f + 1) * SLOT] = jnp.where(even, right, left).astype(BF16)
    send_b[f * SLOT : (f + 1) * SLOT] = jnp.where(even, left, right).astype(BF16)


def strips_kernel(n_out, *refs):
    owner = refs[0]
    slots = refs[1 : 1 + n_out]
    sel, send_a, send_b, *chosen = refs[1 + n_out :]
    me = lax.axis_index("out")
    for n, target in enumerate(chosen):
        which = (me - owner[n] + n_out) % n_out
        for s, slot in enumerate(slots):

            @pl.when(which == s)
            def _():
                target[...] = slot[...]

    for f in range(FIELDS):
        give(send_a, send_b, f, mm(sel[...], jnp.concatenate([q[f] for q in chosen], axis=1), NT))


def column_factor(columns, pair, start, total, group_base, blade_group):
    scaled = columns * BLADES
    first = ((start + total - HALF) * BLADES) // total - BLADES
    group = jnp.full(columns.shape, -1, jnp.int32)
    numerator = jnp.zeros(columns.shape, jnp.int32)
    width = columns.shape[-1]
    for j in range((width + SEG) * BLADES // total + 2):
        blade = first + j
        inside = (scaled >= blade * total) & (scaled < (blade + 1) * total)
        group = jnp.where(inside, blade_group[(blade + BLADES) % BLADES], group)
        numerator = jnp.where(inside, scaled - blade * total, numerator)
    phase = numerator.astype(F32) / total
    amp = pair & (AMP - 1)
    order = ((amp >> 1) + 1).astype(F32)
    angle = two_pi * order * phase
    harmonic = jnp.where((amp & 1) == 0, jnp.cos(angle), jnp.sin(angle))
    return jnp.where(group == group_base + pair // AMP, harmonic, 0.0)


def column_weight(columns, total):
    columns = jnp.where(columns < 0, columns + total, columns)
    columns = jnp.where(columns >= total, columns - total, columns)
    return 1.0 + 2.0 * columns.astype(F32) / total


def flux(fm, q, d):
    inner = q[0] * d[0]
    for f in range(1, FIELDS):
        inner = inner + q[f] * d[f]
    u = q[1] * CU
    out = []
    for e in range(FIELDS):
        value = u * d[e]
        for f in range(FIELDS):
            value = value + fm[f, e] * d[f]
        if e == 1:
            value = value + CU * inner
        out.append(value)
    return out


def prepare_kernel(cycle, blade_group, link_s, *refs):
    owner, fm = refs[:2]
    kept = refs[2 : (len(refs) - 12) // 2 + 2]
    k_ref, kp_ref, b0_ref, v0_ref, send_a, send_b, inv_ref, owner_out, fm_out, *held, sems = refs[
        2 + len(kept) :
    ]
    copies = fetch(zip(kept, held), sems)
    for i in range(owner.shape[0]):
        owner_out[i] = owner[i]
    for f in range(FIELDS):
        for e in range(FIELDS):
            fm_out[f, e] = fm[f, e]
    forcing, link, sel = held[:3]
    rows, width = forcing.shape[1:]
    total = cycle * width
    start = lax.axis_index("blk") * width

    def invert(r, c):
        inv_ref[link_s[r]] = r
        return c

    lax.fori_loop(0, rows, invert, 0, unroll=8)
    lane = lax.broadcasted_iota(jnp.int32, (8, width), 1)
    sub = lax.broadcasted_iota(jnp.int32, (8, width), 0)
    p = lane & (SEG - 1)
    packed = jnp.where(p < HALF, p - QW, width - QW + p - HALF) + start
    args = (start, total, lax.axis_index("out") * GRP_DEV, blade_group)
    for i in range(5):
        k_ref[i] = column_factor(lane + start + (i - 2), sub, *args)
        kp_ref[i] = column_factor(packed + (i - 2), sub, *args)
    arrive(copies[:3])
    links = link[...].astype(F32)
    parts = [split3(forcing[f]) for f in range(FIELDS)]
    hot = one_hot(links, rows)
    flat = jnp.concatenate(sum(parts, ()), axis=1)
    linked = mm(hot, flat)
    linking = mm(hot, flat, TN)
    weight = column_weight(lax.broadcasted_iota(jnp.int32, (1, width), 1) + start, total)
    chosen = mm(
        jnp.concatenate([jnp.concatenate(three, axis=1) for three in parts], axis=0), sel[...]
    )
    row = lax.broadcasted_iota(jnp.int32, (2 * SLOT, rows), 0)
    links = jnp.broadcast_to(links, row.shape)
    for f in range(FIELDS):

        def moved(x):
            three = [x[:, (f * PARTS + i) * width : (f * PARTS + i + 1) * width] for i in range(PARTS)]
            return three[0] + three[1] + three[2]

        b0_ref[f] = (C0 + 1.0) * forcing[f] + CP * moved(linked)
        v0_ref[f] = (C0 * forcing[f] + CP * moved(linking)) * weight
        turned = chosen[f * rows : (f + 1) * rows].T[: 2 * SLOT]
        if f == 0:
            turned = jnp.where(row % SLOT == LINK_ROW, links, turned)
        give(send_a, send_b, f, turned)
    arrive(copies[3:])


def one_hot(links, rows):
    row = lax.broadcasted_iota(jnp.int32, (rows, rows), 0).astype(F32)
    return jnp.where(links == row, 1.0, 0.0).astype(BF16)


def halo_selects(width):
    blocks = width // SEG
    forcing_sel = np.zeros((4 * SLOT, 5, SEG), np.float32)
    state_sel = np.zeros((4 * SLOT, 2, SEG), np.float32)
    edge = np.zeros((4 * SLOT, width), np.float32)

    def place(column, size):
        if column < 0:
            return 0, column + size
        if column < size:
            return 1, column
        if column < width:
            return 2, column - (width - size)
        return 3, column - width

    def forcing_rows(column):
        source, j = place(column, FW)
        return [source * SLOT + part * FW + j for part in range(PARTS)] if 0 <= j < FW else []

    for p in range(SEG):
        column = p - QW if p < HALF else width - QW + p - HALF
        for i in range(5):
            for row in forcing_rows(column + i - 2):
                forcing_sel[row, i, p] = 1.0
        source, j = place(column, QW)
        for i, n in ((0, STEPS - 1), (1, STEPS - 2)):
            state_sel[source * SLOT + n * QW + j, i, p] = 1.0
    for lane, column in ((width - 2, -2), (width - 1, -1), (0, width), (1, width + 1)):
        for row in forcing_rows(column):
            edge[row, lane] = 1.0
    state_edge = np.zeros((4 * SLOT, width), np.float32)
    for lane, column in ((width - 1, -1), (0, width)):
        source, j = place(column, QW)
        state_edge[source * SLOT + j, lane] = 1.0

    def tiled(x):
        return np.repeat(x[:, :, None, :], blocks, axis=2).reshape(4 * SLOT, -1)

    return tuple(
        x.astype(jnp.bfloat16) for x in (tiled(forcing_sel), tiled(state_sel), edge, state_edge)
    )


def stencil_selects(width):
    blocks = width // SEG
    out = np.zeros((blocks, 2, width, 2 * width), np.float32)

    def spread(column):
        near = ((1, 1.0), (-1, -1.0))
        far = ((-1, NEAR), (1, NEAR), (-2, -1.0), (2, -1.0))
        pairs = [(column + d, w) for d, w in near if 0 <= column + d < width]
        return pairs + [(width + column + d, w) for d, w in far if 0 <= column + d < width]

    for column in range(width):
        for lane, w in spread(column):
            out[:, :, column, lane] = w
    for j in range(blocks):
        for p, column in ((2, -2), (3, -1), (HALF + QW, width), (HALF + QW + 1, width + 1)):
            for held in (p, p + 2) if column in (-1, width) else (p,):
                out[j, 1, j * SEG + held] = 0.0
                for to, w in spread(column):
                    out[j, 1, j * SEG + held, to] = w
    return out.reshape(blocks, 2 * width, 2 * width).astype(jnp.bfloat16)


def high(x):
    return x.astype(BF16).astype(F32)


def gather_sources(sa, sb, ra, rb):
    even = lax.axis_index("blk") % 2 == 0
    sa, sb, ra, rb = (x[...].astype(F32) for x in (sa, sb, ra, rb))
    own_left, own_right = jnp.where(even, sb, sa), jnp.where(even, sa, sb)
    left, right = jnp.where(even, rb, ra), jnp.where(even, ra, rb)
    turned = []
    for f in range(FIELDS):
        s = slice(f * SLOT, (f + 1) * SLOT)
        g = jnp.concatenate([left[s], own_left[s], own_right[s], right[s]], axis=0)
        turned.append(g.T.astype(BF16))
    return left, right, turned


def spread_selection(tiled, big):
    blocks = big.shape[0] // (4 * SLOT)
    lane_block = lax.broadcasted_iota(jnp.int32, tiled.shape, 1) % (blocks * SEG) // SEG
    for j in range(blocks):
        big[j * 4 * SLOT : (j + 1) * 4 * SLOT, :] = jnp.where(
            lane_block == j, tiled[...].astype(F32), 0.0
        ).astype(BF16)


def in_segments(sets, big, step):
    blocks = big.shape[0] // (4 * SLOT)
    width = blocks * SEG
    pieces = []
    for x in sets:
        for f in range(FIELDS):
            mine = x[:, f * 4 * SLOT : (f + 1) * 4 * SLOT]
            pieces.append(
                jnp.concatenate([mine[j * step : (j + 1) * step] for j in range(blocks)], axis=1)
            )
    y = mm(jnp.concatenate(pieces, axis=0), big)

    def part(i, f, which):
        start = (i * FIELDS + f) * step
        return y[start : start + step, which * width : (which + 1) * width]

    return part


def left_lanes(step, width):
    return lax.broadcasted_iota(jnp.int32, (step, width), 1) & (SEG - 1) < HALF


def halo_forcing_kernel(
    cycle, fm, link, sa, sb, ra, rb, tiled, edge, forcing, v0, q0, q1, q2,
    y_ref, fe_ref, hot_ref, bs, coef0, coef1, weighted, heavy, z_ref, big, fmc,
):
    rows, width = link.shape[1], edge.shape[1]
    step = rows // (width // SEG)
    left, right, turned = gather_sources(sa, sb, ra, rb)
    hot = jnp.concatenate(
        [
            one_hot(left[LINK_ROW : LINK_ROW + 1], rows),
            one_hot(link[...].astype(F32), rows),
            one_hot(right[LINK_ROW : LINK_ROW + 1], rows),
        ],
        axis=0,
    )
    hot_ref[...] = hot
    k_wide = 4 * SLOT
    source = lax.broadcasted_iota(jnp.int32, (rows, FIELDS * k_wide), 1) % k_wide // SLOT

    def permuted(x):
        y = mm(hot, x)
        by_left, by_right = y[:rows], y[2 * rows :]
        outer = jnp.where(source == 0, by_left, by_right)
        by_tile = jnp.where((source == 1) | (source == 2), y[rows : 2 * rows], outer)
        return by_left.astype(BF16), by_right.astype(BF16), by_tile.astype(BF16)

    fe = mm(jnp.concatenate(turned, axis=0), edge[...])
    for f in range(FIELDS):
        fe_ref[f] = fe[f * rows : (f + 1) * rows]
    g = jnp.concatenate(turned, axis=1)
    by_left, by_right, by_tile = permuted(g)
    spread_selection(tiled, big)
    part = in_segments((g, by_left, by_right), big[...], step)
    linked = in_segments((by_tile, permuted(by_tile)[2]), big[:, 2 * width : 3 * width], step)
    is_left = left_lanes(step, width)

    def at(linked, f, which):
        if linked:
            return jnp.where(is_left, part(1, f, which), part(2, f, which))
        return part(0, f, which)

    for i in range(2):
        shifted = [[at(i, f, d) for f in range(FIELDS)] for d in range(5)]
        for f in range(FIELDS):
            minus = sum(fm[e, f] * CM * shifted[1][e] for e in range(FIELDS))
            plus = sum(fm[e, f] * CM * shifted[3][e] for e in range(FIELDS))
            b = (
                C2 * shifted[0][f],
                C1 * shifted[1][f] - minus,
                (C0 + 1.0) * shifted[2][f] + CP * linked(i, f, 0),
                C1 * shifted[3][f] + plus,
                C2 * shifted[4][f],
                shifted[1][f],
                shifted[3][f],
                shifted[2][f],
            )
            for d, value in enumerate(b):
                y_ref[i * 8 + d, f] = value

    scaled_matrix(fm, fmc)
    total = cycle * width
    start = lax.axis_index("blk") * width
    lane = lax.broadcasted_iota(jnp.int32, (8, width), 1)
    weight = {d: column_weight(lane + (start + d), total) for d in range(-2, 3)}

    def dense(i, z):
        rs = pl.ds(pl.multiple_of(i * 16, 16), 16)
        for q_ref, coef in ((q0, coef0), (q1, coef1)):
            q = [q_ref[f, rs, :].astype(F32) for f in range(FIELDS)]
            u = CU * q[1]
            for e in range(FIELDS):
                coef[e, rs, :] = (u if e != 1 else u + u) + fmc[e, e]
            for j, f in enumerate((0, 2, 3, 4)):
                coef[FIELDS + j, rs, :] = CU * q[f] + fmc[f, 1]
        both_q = [[q[f, rs, :].astype(F32) for f in range(FIELDS)] for q in (q0, q2)]
        for half in range(2):
            r8 = pl.ds(pl.multiple_of(i * 16 + half * 8, 8), 8)
            mine, last = [[x[half * 8 : half * 8 + 8] for x in q] for q in both_q]
            near, w = [], []
            for f in range(FIELDS):
                x, beside = forcing[f, r8, :], fe_ref[f, r8, :]
                near.append(
                    (
                        *shift_edges(x, beside, lane, width),
                        pltpu.roll(jnp.where(lane >= width - 2, beside, x), 2, 1),
                        pltpu.roll(jnp.where(lane < 2, beside, x), width - 2, 1),
                    )
                )
                w.append(x * weight[0])
            minus = flux(fmc, last, [a[0] for a in near])
            plus = flux(fmc, last, [a[1] for a in near])
            for f in range(FIELDS):
                m1, p1, m2, p2 = near[f]
                bs[0, f, r8, :] = C2 * m2
                bs[1, f, r8, :] = C1 * m1 - minus[f]
                bs[2, f, r8, :] = C1 * p1 + plus[f]
                bs[3, f, r8, :] = C2 * p2
                weighted[f, r8, :] = w[f]
                z = z + w[f] * forcing[f, r8, :]
                x = CU * (mine[1] * w[f] + mine[f] * w[1])
                for e in range(FIELDS):
                    x = x + fmc[f, e] * w[e]
                before = jnp.where(lane == 0, 0.0, pltpu.roll(x, 1, 1))
                after = jnp.where(lane == width - 1, 0.0, pltpu.roll(x, width - 1, 1))
                turned = v0[f, r8, :] + C1 * (m1 * weight[-1] + p1 * weight[1])
                turned = turned + C2 * (m2 * weight[-2] + p2 * weight[2])
                heavy[f, r8, :] = w[f] + turned + (before - after)
        return z

    z_ref[...] = lax.fori_loop(0, rows // 16, dense, jnp.zeros((8, width), F32), unroll=2)


def halo_kernel(
    fm, sa, sb, ra, rb, tiled, edge, kp_ref, hot, y_in,
    e1_ref, e2_ref, qe_ref, y_ref, big, q_ref, fmc,
):
    for i in (1, 3, 9, 11):
        y_ref[i] = y_in[i]
    rows, width = hot.shape[1], kp_ref.shape[2]
    step = rows // (width // SEG)
    for f in range(FIELDS):
        for e in range(FIELDS):
            fmc[f, e] = fm[f, e] * CM
    _, _, turned = gather_sources(sa, sb, ra, rb)
    g = jnp.concatenate(turned, axis=1)
    qe = mm(jnp.concatenate(turned, axis=0), edge[...])
    for f in range(FIELDS):
        qe_ref[f] = qe[f * rows : (f + 1) * rows]
    y = mm(hot[...], g).astype(BF16)
    spread_selection(tiled, big)
    part = in_segments((g, y[:rows], y[2 * rows :]), big[...], step)
    is_left = left_lanes(step, width)
    for i in range(2):
        if i:
            q2 = [jnp.where(is_left, part(1, f, 0), part(2, f, 0)) for f in range(FIELDS)]
        else:
            q2 = [part(0, f, 0) for f in range(FIELDS)]
        u = CU * q2[1]
        for d, near, sign in ((1, 5, -1.0), (3, 6, 1.0)):
            inner = sum(q2[f] * y_in[i * 8 + near, f] for f in range(FIELDS))
            for f in range(FIELDS):
                value = u * y_in[i * 8 + near, f]
                if f == 1:
                    value = value + CU * inner
                y_ref[i * 8 + d, f] = y_ref[i * 8 + d, f] + sign * value
    for f in range(FIELDS):
        q_ref[f] = part(0, f, 1)
    kp = [kp_ref[i] for i in range(5)]
    p = lax.broadcasted_iota(jnp.int32, (8, width), 1) & (SEG - 1)
    holds_high = (p != 5) & (p != 14)

    def both_halves(x):
        top = high(x)
        return jnp.where(holds_high, top, pltpu.roll(x - top, 2, 1))


    def body(r, c):
        def row(ref, index):
            return jnp.broadcast_to(ref[(*index, pl.ds(r, 1), slice(None))], (8, width))

        mu, linked, d, base = [], [], [], []
        for f in range(FIELDS):
            for i, out in ((0, mu), (8, linked)):
                value = row(y_in, (i, f)) * kp[0]
                for n in range(1, 5):
                    value = value + row(y_ref if n % 2 else y_in, (i + n, f)) * kp[n]
                out.append(value)
            x = mu[f]
            m1, p1 = pltpu.roll(x, 1, 1), pltpu.roll(x, width - 1, 1)
            m2, p2 = pltpu.roll(x, 2, 1), pltpu.roll(x, width - 2, 1)
            d.append(m1 - p1)
            base.append(
                C0 * x + C1 * (m1 + p1) + C2 * (m2 + p2) + CP * linked[f]
                + row(y_in, (7, f)) * kp[2]
            )
        moved = flux(fmc, [row(q_ref, (f,)) for f in range(FIELDS)], d)
        at = pl.ds(pl.multiple_of(r * (FIELDS * 8), 8), FIELDS * 8)
        e1_ref[at, :] = jnp.concatenate([both_halves(x) for x in mu], axis=0)
        e2_ref[at, :] = jnp.concatenate(
            [both_halves(b - m) for b, m in zip(base, moved)], axis=0
        )
        return c

    lax.fori_loop(0, step, body, 0, unroll=16)


def shift_edges(x, edge, lane, width):
    return (
        pltpu.roll(jnp.where(lane == width - 1, edge, x), 1, 1),
        pltpu.roll(jnp.where(lane == 0, edge, x), width - 1, 1),
    )


def spread(ref, index, r):
    return jnp.broadcast_to(ref[(*index, pl.ds(r, 1), slice(None))], (8, ref.shape[-1]))


def place(r, f):
    return pl.ds(pl.multiple_of((r * FIELDS + f) * 8, 8), 8)


def scaled_matrix(fm, fmc):
    for f in range(FIELDS):
        for e in range(FIELDS):
            fmc[f, e] = fm[f, e] * CM


def matrix_rows(fmc, width):
    return [[jnp.full((8, width), fmc[f, e]) for e in range(FIELDS)] for f in range(FIELDS)]


def stencil_products(dz, source, edges, products):
    width = source.shape[1]
    count = edges.shape[0]
    lane = lax.broadcasted_iota(jnp.int32, (count, width), 1)
    p = lane & (SEG - 1)
    halo = functools.reduce(jnp.logical_or, [p == held for held in HALO_LANES])
    for j in range(products.shape[0]):
        x = source[j * count : (j + 1) * count, :]
        top = x.astype(BF16)
        rest = jnp.where(halo & (lane // SEG == j), edges[...], x - top.astype(F32))
        dz[j * count : (j + 1) * count, :] = mm(
            jnp.concatenate([top, rest.astype(BF16)], axis=1), products[j]
        )


def step_row(source, dz, coef, fmv, linked, r):
    width = source.shape[1]

    d = [dz[place(r, f), :width] for f in range(FIELDS)]
    out = []
    for e in range(FIELDS):
        value = C0 * source[place(r, e), :] + UNIT * dz[place(r, e), width:]
        value = value + CP * source[place(linked, e), :]
        for f in range(FIELDS):
            if f == e:
                m = spread(coef, (e,), r)
            elif e == 1:
                m = spread(coef, (FIELDS + (0, 2, 3, 4).index(f),), r)
            else:
                m = fmv[f][e]
            value = value - m * d[f]
        out.append(value)
    return out


def first_steps_kernel(
    cycle, fm, inv, forcing, fe, b0, qe, k_ref, products, e1, bs, coef1, weighted, heavy_in, z_ref,
    mu2, sens_ref,
    mu1, dz, heavy, fmc,
):
    rows, width = forcing.shape[1], forcing.shape[2]
    total = cycle * width
    blocks = width // SEG
    size = rows // blocks
    scaled_matrix(fm, fmc)
    lane = lax.broadcasted_iota(jnp.int32, (8, width), 1)
    start = lax.axis_index("blk") * width
    norm = 1.0 / math.sqrt(FIELDS * rows * total)
    beside = column_weight(jnp.where(lane < width // 2, lane + width, lane - width) + start, total)

    def finish(i, c):
        r8 = pl.ds(pl.multiple_of(i * 8, 8), 8)
        w = [fe[f, r8, :] * beside for f in range(FIELDS)]
        q = [qe[f, r8, :] for f in range(FIELDS)]
        for f in range(FIELDS):
            x = CU * (q[1] * w[f] + q[f] * w[1])
            for e in range(FIELDS):
                x = x + fmc[f, e] * w[e]
            before = jnp.where(lane == 0, pltpu.roll(x, 1, 1), 0.0)
            after = jnp.where(lane == width - 1, pltpu.roll(x, width - 1, 1), 0.0)
            heavy[f, r8, :] = heavy_in[f, r8, :] + (before - after)
        return c

    zero = jnp.zeros((8, width), F32)
    lax.fori_loop(0, rows // 8, finish, 0, unroll=8)
    z = z_ref[...]
    k = [k_ref[i] for i in range(5)]

    def first(j, acc):
        acc = list(acc)
        for i in range(size):
            r = j * size + i
            for f in range(FIELDS):
                value = spread(bs, (0, f), r) * k[0] + spread(bs, (1, f), r) * k[1]
                value = value + spread(b0, (f,), r) * k[2] + spread(bs, (2, f), r) * k[3]
                value = value + spread(bs, (3, f), r) * k[4]
                mu1[place(r, f), :] = value
                acc[f] = acc[f] + value * spread(weighted, (f,), r)
        return tuple(acc)

    acc = lax.fori_loop(0, blocks, first, (zero,) * FIELDS)
    fmv = matrix_rows(fmc, width)
    stencil_products(dz, mu1, e1, products)

    def second(j, acc):
        acc = list(acc)
        for i in range(size):
            r = j * size + i
            made = step_row(mu1, dz, coef1, fmv, inv[r], r)
            for f, value in enumerate(made):
                value = value + spread(forcing, (f,), r) * k[2]
                mu2[place(r, f), :] = value
                acc[f] = acc[f] + value * spread(heavy, (f,), r)
        return tuple(acc)

    acc = lax.fori_loop(0, blocks, second, acc)
    source_part = jnp.sum(z, axis=0, keepdims=True) * k[2]
    acc = (sum(acc) - 2.0 * source_part) * norm
    acc = jnp.broadcast_to(jnp.sum(acc, axis=1, keepdims=True), (8, width))
    sub = lax.broadcasted_iota(jnp.int32, (8, width), 0)
    for group in range(GRP_DEV):
        mine = jnp.where(sub == group * AMP + lane, acc, 0.0)
        sens_ref[group : group + 1, :] = jnp.sum(mine, axis=0, keepdims=True)[:, :AMP]


def last_step_kernel(fm, inv, mu2, coef0, e2, products, out_hbm, dz, stage, fmc, out_sems):
    rows, width = coef0.shape[1:]
    blocks = width // SEG
    size = rows // blocks
    scaled_matrix(fm, fmc)
    fmv = matrix_rows(fmc, width)
    stencil_products(dz, mu2, e2, products)

    def send(j):
        at = pl.ds(pl.multiple_of(j * 8, 8), 8)
        return pltpu.make_async_copy(stage.at[:, at, :], out_hbm.at[:, at, :], out_sems.at[j])

    def third(j, c):
        for half in range(size // 8):
            r0 = j * size + half * 8
            made = [step_row(mu2, dz, coef0, fmv, inv[r0 + i], r0 + i) for i in range(8)]
            at = pl.ds(pl.multiple_of(r0, 8), 8)
            for e in range(FIELDS):
                turned = jnp.swapaxes(jnp.stack([x[e] for x in made]), 0, 1)
                for pair in range(PAIRS):
                    stage[pair * FIELDS + e, at, :] = turned[pair]
            send(j * (size // 8) + half).start()
        return c

    lax.fori_loop(0, blocks, third, 0)
    for j in range(rows // 8):
        send(j).wait()


def shift_pairs(devices, k):
    return [(i, (i + k) % devices) for i in range(devices)]


def round_over(x, axis, bit):
    return x + lax.ppermute(x, axis, [(i, i ^ bit) for i in range(lax.axis_size(axis))])


def to_neighbours(send_a, send_b, cycle):
    return (
        lax.ppermute(send_a, "blk", [(i, i ^ 1) for i in range(cycle)]),
        lax.ppermute(
            send_b,
            "blk",
            [(i, (i + 1) % cycle if i % 2 else (i - 1) % cycle) for i in range(cycle)],
        ),
    )


def on_device(checkpoints, owner, flux_matrix, row_link, blade_group, forcing):
    n_out = lax.axis_size("out")
    cycle = lax.axis_size("blk")
    rows, width = forcing.shape[1], forcing.shape[2]
    blocks = width // SEG
    step_rows = rows // blocks
    slot = checkpoints[0]

    def struct(shape, kind=F32):
        return jax.ShapeDtypeStruct(shape, kind)

    sems = pltpu.SemaphoreType.DMA
    field = struct((FIELDS, rows, width))
    strip = struct((FIELDS * SLOT, rows), BF16)
    factors = struct((5, PAIRS, width))
    slots = [slot] + [lax.ppermute(slot, "out", shift_pairs(n_out, k)) for k in range(1, n_out)]

    def stay(x):
        return pltpu.with_memory_space_constraint(x, pltpu.HBM)

    def call(kernel, out_shape, smem, hbm, vmem, scratch, limit, flops, name, out_specs=None):
        return pl.pallas_call(
            kernel,
            out_shape=out_shape,
            in_specs=[SMEM] * len(smem) + [HBM] * len(hbm) + [VMEM] * len(vmem),
            out_specs=out_specs or (VMEM,) * len(out_shape),
            scratch_shapes=scratch,
            compiler_params=pltpu.CompilerParams(vmem_limit_bytes=limit),
            cost_estimate=cost(flops, 10**6),
            name=name,
        )(*map(stay, smem), *map(stay, hbm), *vmem)

    kept = (
        forcing, row_link, forcing_select(width), slot, state_select(width),
        *halo_selects(width), stencil_selects(width),
    )
    made = (
        factors, factors, field, field, strip, strip,
        struct((rows,), jnp.int32), struct(owner.shape, jnp.int32), struct(flux_matrix.shape),
    )
    made += tuple(struct(x.shape, x.dtype) for x in kept)
    k, kp, b0, v0, f_a, f_b, inv, owner_s, fm_s, *held = call(
        functools.partial(prepare_kernel, cycle),
        made,
        (blade_group, row_link[0], owner, flux_matrix),
        kept,
        (),
        [sems((len(kept),))],
        SMALL_LIMIT,
        10**8,
        "prepare",
        (VMEM,) * 6 + (SMEM,) * 3 + (VMEM,) * len(kept),
    )
    forcing_v, link, _, slot_v, state_sel, *held = held
    forcing_tiled, state_tiled, edge, state_edge, products = held
    f_sent = (f_a, f_b, *to_neighbours(f_a, f_b, cycle))

    q_a, q_b, *chosen = call(
        functools.partial(strips_kernel, n_out),
        (strip, strip) + (struct(slot.shape, slot.dtype),) * STEPS,
        (owner_s,),
        (),
        (slot_v, *slots[1:], state_sel),
        [],
        SMALL_LIMIT,
        10**7,
        "strips",
    )
    q_sent = (q_a, q_b, *to_neighbours(q_a, q_b, cycle))

    coefficients = struct((2 * FIELDS - 1, rows, width))
    y, fe, hot, bs, coef0, coef1, weighted, heavy, z = call(
        functools.partial(halo_forcing_kernel, cycle),
        (
            struct((16, FIELDS, step_rows, width)), field, struct((3 * rows, rows), BF16),
            struct((4, FIELDS, rows, width)), coefficients, coefficients, field, field,
            struct((PAIRS, width)),
        ),
        (fm_s,),
        (),
        (link, *f_sent, forcing_tiled, edge, forcing_v, v0, *chosen),
        [
            pltpu.VMEM((blocks * 4 * SLOT, forcing_tiled.shape[1]), BF16),
            pltpu.SMEM((FIELDS, FIELDS), F32),
        ],
        SMALL_LIMIT,
        10**8,
        "halo_forcing",
    )
    flat = rows * FIELDS * PAIRS
    edges = (step_rows * FIELDS * 8, width)
    halo_operands = (*q_sent, state_tiled, state_edge, kp, hot, y)
    halo_scratch = [
        pltpu.VMEM(edges, F32),
        pltpu.VMEM((FIELDS, rows, width), F32),
        like(y),
        pltpu.VMEM((blocks * 4 * SLOT, state_tiled.shape[1]), BF16),
        pltpu.VMEM((FIELDS, step_rows, width), F32),
        pltpu.SMEM((FIELDS, FIELDS), F32),
    ]

    def halo_and_first_steps(fm, inv, *refs):
        halo_in, refs = refs[: len(halo_operands)], refs[len(halo_operands) :]
        forcing, fe, b0, k_ref, products, *ready = refs[:10]
        mu2, sens, e2, e1, qe, *work = refs[10 : 13 + len(halo_scratch)]
        halo_kernel(fm, *halo_in, e1, e2, qe, *work)
        first_steps_kernel(
            cycle, fm, inv, forcing, fe, b0, qe, k_ref, products, e1, *ready,
            mu2, sens, *refs[13 + len(halo_scratch) :],
        )

    mu2, sens, e2 = call(
        halo_and_first_steps,
        (struct((flat, width)), struct((GRP_DEV, AMP)), struct(edges)),
        (fm_s, inv),
        (),
        (*halo_operands, forcing_v, fe, b0, k, products, bs, coef1, weighted, heavy, z),
        halo_scratch
        + [
            pltpu.VMEM((flat, width), F32),
            pltpu.VMEM((flat, 2 * width), F32),
            pltpu.VMEM((FIELDS, rows, width), F32),
            pltpu.SMEM((FIELDS, FIELDS), F32),
        ],
        VMEM_LIMIT,
        10**9,
        "first_steps",
    )

    pairs_fields = PAIRS * FIELDS
    bits = [1 << i for i in reversed(range(cycle.bit_length() - 1))]
    exact = 1 << len(bits) == cycle
    if not exact:
        sens = lax.psum(sens, "blk")
    if exact and bits:
        sens = round_over(sens, "blk", bits.pop(0))
    (adjoint,) = call(
        last_step_kernel,
        (struct((pairs_fields, rows, width)),),
        (fm_s, inv),
        (),
        (mu2, coef0, e2, products),
        [
            pltpu.VMEM((flat, 2 * width), F32),
            pltpu.VMEM((pairs_fields, rows, width), F32),
            pltpu.SMEM((FIELDS, FIELDS), F32),
            sems((rows // 8,)),
        ],
        VMEM_LIMIT,
        10**9,
        "last_step",
        (HBM,),
    )
    for bit in bits if exact else ():
        sens = round_over(sens, "blk", bit)
    return adjoint.reshape(GRP_DEV, AMP, FIELDS, rows, width), sens


def solution(mesh):
    return jax.shard_map(
        on_device,
        mesh=mesh,
        in_specs=(P("out", None, None, "blk"), P(), P(), P("blk", None), P(), P(None, None, "blk")),
        out_specs=(P("out", None, None, None, "blk"), P("out", None)),
        check_vma=False,
    )
```

```python
import functools
import math

import jax
import jax.numpy as jnp
import numpy as np
from jax import lax
from jax.experimental import pallas as pl
from jax.experimental.pallas import tpu as pltpu
from jax.sharding import PartitionSpec as P

FIELDS = 5
BLADES = 96
AMP = 4
GRP_DEV = 2
STEPS = 3
PAIRS = GRP_DEV * AMP

time_step = 0.25
second_diff = 0.1
fourth_diff = 0.02
link_weight = 0.5
two_pi = 2.0 * math.pi

C0 = 1.0 - time_step * (2.0 * second_diff + 6.0 * fourth_diff + link_weight)
C1 = time_step * (second_diff + 4.0 * fourth_diff)
C2 = -time_step * fourth_diff
CP = time_step * link_weight
CM = 0.5 * time_step
CU = 0.25 * time_step

FW = 6
QW = 4
PARTS = 3
SLOT = 32
LINK_ROW = PARTS * FW
SEG = 16
HALF = SEG // 2
VMEM_LIMIT = 40 * 2**20
SMALL_LIMIT = 16 * 2**20

VMEM = pl.BlockSpec(memory_space=pltpu.VMEM)
SMEM = pl.BlockSpec(memory_space=pltpu.SMEM)
HBM = pl.BlockSpec(memory_space=pltpu.HBM)
UNIT = time_step * fourth_diff
NEAR = round(C1 / UNIT)
F32 = jnp.float32
BF16 = jnp.bfloat16
NT = (((1,), (1,)), ((), ()))
TN = (((0,), (0,)), ((), ()))
NN = (((1,), (0,)), ((), ()))


def mm(a, b, dims=NN):
    return lax.dot_general(a, b, dims, preferred_element_type=F32)


def split3(x):
    hi = x.astype(BF16)
    rest = x - hi.astype(F32)
    mid = rest.astype(BF16)
    return hi, mid, (rest - mid.astype(F32)).astype(BF16)


def exact_mm(a, x):
    hi, mid, lo = split3(x)
    return mm(a, hi) + mm(a, mid) + mm(a, lo)


def fetch(moves, sems):
    copies = [pltpu.make_async_copy(src, dst, sems.at[i]) for i, (src, dst) in enumerate(moves)]
    for copy in copies:
        copy.start()
    return copies


def arrive(copies):
    for copy in copies:
        copy.wait()


def like(x):
    return pltpu.VMEM(x.shape, x.dtype)


def cost(flops, moved):
    return pl.CostEstimate(flops=flops, bytes_accessed=moved, transcendentals=0)


def forcing_select(width):
    out = np.zeros((PARTS, width, width), np.float32)
    for part in range(PARTS):
        for j in range(FW):
            out[part, j, part * FW + j] = 1.0
            out[part, width - FW + j, SLOT + part * FW + j] = 1.0
    return out.reshape(PARTS * width, width).astype(jnp.bfloat16)


def state_select(width):
    out = np.zeros((2 * SLOT, STEPS, width), np.float32)
    for n in range(STEPS):
        for j in range(QW):
            out[n * QW + j, n, j] = 1.0
            out[SLOT + n * QW + j, n, width - QW + j] = 1.0
    return out.reshape(2 * SLOT, STEPS * width).astype(jnp.bfloat16)


def give(send_a, send_b, f, both):
    even = lax.axis_index("blk") % 2 == 0
    left, right = both[:SLOT], both[SLOT:]
    send_a[f * SLOT : (f + 1) * SLOT] = jnp.where(even, right, left).astype(BF16)
    send_b[f * SLOT : (f + 1) * SLOT] = jnp.where(even, left, right).astype(BF16)


def strips_kernel(n_out, *refs):
    owner = refs[0]
    slots = refs[1 : 1 + n_out]
    sel, send_a, send_b, *chosen = refs[1 + n_out :]
    me = lax.axis_index("out")
    for n, target in enumerate(chosen):
        which = (me - owner[n] + n_out) % n_out
        for s, slot in enumerate(slots):

            @pl.when(which == s)
            def _():
                target[...] = slot[...]

    for f in range(FIELDS):
        give(send_a, send_b, f, mm(sel[...], jnp.concatenate([q[f] for q in chosen], axis=1), NT))


def column_factor(columns, pair, start, total, group_base, blade_group):
    scaled = columns * BLADES
    first = ((start + total - HALF) * BLADES) // total - BLADES
    group = jnp.full(columns.shape, -1, jnp.int32)
    numerator = jnp.zeros(columns.shape, jnp.int32)
    width = columns.shape[-1]
    for j in range((width + SEG) * BLADES // total + 2):
        blade = first + j
        inside = (scaled >= blade * total) & (scaled < (blade + 1) * total)
        group = jnp.where(inside, blade_group[(blade + BLADES) % BLADES], group)
        numerator = jnp.where(inside, scaled - blade * total, numerator)
    phase = numerator.astype(F32) / total
    amp = pair & (AMP - 1)
    order = ((amp >> 1) + 1).astype(F32)
    angle = two_pi * order * phase
    harmonic = jnp.where((amp & 1) == 0, jnp.cos(angle), jnp.sin(angle))
    return jnp.where(group == group_base + pair // AMP, harmonic, 0.0)


def column_weight(columns, total):
    columns = jnp.where(columns < 0, columns + total, columns)
    columns = jnp.where(columns >= total, columns - total, columns)
    return 1.0 + 2.0 * columns.astype(F32) / total


def flux(fm, q, d):
    inner = q[0] * d[0]
    for f in range(1, FIELDS):
        inner = inner + q[f] * d[f]
    u = q[1] * CU
    out = []
    for e in range(FIELDS):
        value = u * d[e]
        for f in range(FIELDS):
            value = value + fm[f, e] * d[f]
        if e == 1:
            value = value + CU * inner
        out.append(value)
    return out


def prepare_kernel(cycle, blade_group, link_s, *refs):
    owner, fm = refs[:2]
    kept = refs[2 : (len(refs) - 12) // 2 + 2]
    k_ref, kp_ref, b0_ref, v0_ref, send_a, send_b, inv_ref, owner_out, fm_out, *held, sems = refs[
        2 + len(kept) :
    ]
    copies = fetch(zip(kept, held), sems)
    for i in range(owner.shape[0]):
        owner_out[i] = owner[i]
    for f in range(FIELDS):
        for e in range(FIELDS):
            fm_out[f, e] = fm[f, e]
    forcing, link, sel = held[:3]
    rows, width = forcing.shape[1:]
    total = cycle * width
    start = lax.axis_index("blk") * width

    def invert(r, c):
        inv_ref[link_s[r]] = r
        return c

    lax.fori_loop(0, rows, invert, 0, unroll=8)
    lane = lax.broadcasted_iota(jnp.int32, (8, width), 1)
    sub = lax.broadcasted_iota(jnp.int32, (8, width), 0)
    p = lane & (SEG - 1)
    packed = jnp.where(p < HALF, p - QW, width - QW + p - HALF) + start
    args = (start, total, lax.axis_index("out") * GRP_DEV, blade_group)
    for i in range(5):
        k_ref[i] = column_factor(lane + start + (i - 2), sub, *args)
        kp_ref[i] = column_factor(packed + (i - 2), sub, *args)
    arrive(copies[:3])
    links = link[...].astype(F32)
    parts = [split3(forcing[f]) for f in range(FIELDS)]
    hot = one_hot(links, rows)
    flat = jnp.concatenate(sum(parts, ()), axis=1)
    linked = mm(hot, flat)
    linking = mm(hot, flat, TN)
    weight = column_weight(lax.broadcasted_iota(jnp.int32, (1, width), 1) + start, total)
    chosen = mm(
        jnp.concatenate([jnp.concatenate(three, axis=1) for three in parts], axis=0), sel[...]
    )
    row = lax.broadcasted_iota(jnp.int32, (2 * SLOT, rows), 0)
    links = jnp.broadcast_to(links, row.shape)
    for f in range(FIELDS):

        def moved(x):
            three = [x[:, (f * PARTS + i) * width : (f * PARTS + i + 1) * width] for i in range(PARTS)]
            return three[0] + three[1] + three[2]

        b0_ref[f] = (C0 + 1.0) * forcing[f] + CP * moved(linked)
        v0_ref[f] = (C0 * forcing[f] + CP * moved(linking)) * weight
        turned = chosen[f * rows : (f + 1) * rows].T[: 2 * SLOT]
        if f == 0:
            turned = jnp.where(row % SLOT == LINK_ROW, links, turned)
        give(send_a, send_b, f, turned)
    arrive(copies[3:])


def one_hot(links, rows):
    row = lax.broadcasted_iota(jnp.int32, (rows, rows), 0).astype(F32)
    return jnp.where(links == row, 1.0, 0.0).astype(BF16)


def halo_selects(width):
    blocks = width // SEG
    forcing_sel = np.zeros((4 * SLOT, 5, SEG), np.float32)
    state_sel = np.zeros((4 * SLOT, 2, SEG), np.float32)
    edge = np.zeros((4 * SLOT, width), np.float32)

    def place(column, size):
        if column < 0:
            return 0, column + size
        if column < size:
            return 1, column
        if column < width:
            return 2, column - (width - size)
        return 3, column - width

    def forcing_rows(column):
        source, j = place(column, FW)
        return [source * SLOT + part * FW + j for part in range(PARTS)] if 0 <= j < FW else []

    for p in range(SEG):
        column = p - QW if p < HALF else width - QW + p - HALF
        for i in range(5):
            for row in forcing_rows(column + i - 2):
                forcing_sel[row, i, p] = 1.0
        source, j = place(column, QW)
        for i, n in ((0, STEPS - 1), (1, STEPS - 2)):
            state_sel[source * SLOT + n * QW + j, i, p] = 1.0
    for lane, column in ((width - 2, -2), (width - 1, -1), (0, width), (1, width + 1)):
        for row in forcing_rows(column):
            edge[row, lane] = 1.0
    state_edge = np.zeros((4 * SLOT, width), np.float32)
    for lane, column in ((width - 1, -1), (0, width)):
        source, j = place(column, QW)
        state_edge[source * SLOT + j, lane] = 1.0

    def tiled(x):
        return np.repeat(x[:, :, None, :], blocks, axis=2).reshape(4 * SLOT, -1)

    return tuple(
        x.astype(jnp.bfloat16) for x in (tiled(forcing_sel), tiled(state_sel), edge, state_edge)
    )


def stencil_selects(width):
    blocks = width // SEG
    out = np.zeros((blocks, 3, width, 2 * width), np.float32)

    def spread(column):
        near = ((1, 1.0), (-1, -1.0))
        far = ((-1, NEAR), (1, NEAR), (-2, -1.0), (2, -1.0))
        pairs = [(column + d, w) for d, w in near if 0 <= column + d < width]
        return pairs + [(width + column + d, w) for d, w in far if 0 <= column + d < width]

    for column in range(width):
        for lane, w in spread(column):
            out[:, :2, column, lane] = w
    for j in range(blocks):
        for p, column in ((2, -2), (3, -1), (HALF + QW, width), (HALF + QW + 1, width + 1)):
            for held in (p, p + 2) if column in (-1, width) else (p,):
                for to, w in spread(column):
                    out[j, 2, j * SEG + held, to] = w
    return out.reshape(blocks, 3 * width, 2 * width).astype(jnp.bfloat16)


def high(x):
    return x.astype(BF16).astype(F32)


def gather_sources(sa, sb, ra, rb):
    even = lax.axis_index("blk") % 2 == 0
    sa, sb, ra, rb = (x[...].astype(F32) for x in (sa, sb, ra, rb))
    own_left, own_right = jnp.where(even, sb, sa), jnp.where(even, sa, sb)
    left, right = jnp.where(even, rb, ra), jnp.where(even, ra, rb)
    turned = []
    for f in range(FIELDS):
        s = slice(f * SLOT, (f + 1) * SLOT)
        g = jnp.concatenate([left[s], own_left[s], own_right[s], right[s]], axis=0)
        turned.append(g.T.astype(BF16))
    return left, right, turned


def spread_selection(tiled, big):
    blocks = big.shape[0] // (4 * SLOT)
    lane_block = lax.broadcasted_iota(jnp.int32, tiled.shape, 1) % (blocks * SEG) // SEG
    for j in range(blocks):
        big[j * 4 * SLOT : (j + 1) * 4 * SLOT, :] = jnp.where(
            lane_block == j, tiled[...].astype(F32), 0.0
        ).astype(BF16)


def in_segments(sets, big, step):
    blocks = big.shape[0] // (4 * SLOT)
    width = blocks * SEG
    pieces = []
    for x in sets:
        for f in range(FIELDS):
            mine = x[:, f * 4 * SLOT : (f + 1) * 4 * SLOT]
            pieces.append(
                jnp.concatenate([mine[j * step : (j + 1) * step] for j in range(blocks)], axis=1)
            )
    y = mm(jnp.concatenate(pieces, axis=0), big)

    def part(i, f, which):
        start = (i * FIELDS + f) * step
        return y[start : start + step, which * width : (which + 1) * width]

    return part


def left_lanes(step, width):
    return lax.broadcasted_iota(jnp.int32, (step, width), 1) & (SEG - 1) < HALF


def halo_forcing_kernel(
    cycle, fm, link, sa, sb, ra, rb, tiled, edge, forcing, v0, q0, q1, q2,
    y_ref, fe_ref, hot_ref, bs, coef0, coef1, weighted, heavy, z_ref, big, fmc,
):
    rows, width = link.shape[1], edge.shape[1]
    step = rows // (width // SEG)
    left, right, turned = gather_sources(sa, sb, ra, rb)
    hot = jnp.concatenate(
        [
            one_hot(left[LINK_ROW : LINK_ROW + 1], rows),
            one_hot(link[...].astype(F32), rows),
            one_hot(right[LINK_ROW : LINK_ROW + 1], rows),
        ],
        axis=0,
    )
    hot_ref[...] = hot
    k_wide = 4 * SLOT
    source = lax.broadcasted_iota(jnp.int32, (rows, FIELDS * k_wide), 1) % k_wide // SLOT

    def permuted(x):
        y = mm(hot, x)
        by_left, by_right = y[:rows], y[2 * rows :]
        outer = jnp.where(source == 0, by_left, by_right)
        by_tile = jnp.where((source == 1) | (source == 2), y[rows : 2 * rows], outer)
        return by_left.astype(BF16), by_right.astype(BF16), by_tile.astype(BF16)

    fe = mm(jnp.concatenate(turned, axis=0), edge[...])
    for f in range(FIELDS):
        fe_ref[f] = fe[f * rows : (f + 1) * rows]
    g = jnp.concatenate(turned, axis=1)
    by_left, by_right, by_tile = permuted(g)
    spread_selection(tiled, big)
    part = in_segments((g, by_left, by_right), big[...], step)
    linked = in_segments((by_tile, permuted(by_tile)[2]), big[:, 2 * width : 3 * width], step)
    is_left = left_lanes(step, width)

    def at(linked, f, which):
        if linked:
            return jnp.where(is_left, part(1, f, which), part(2, f, which))
        return part(0, f, which)

    for i in range(2):
        shifted = [[at(i, f, d) for f in range(FIELDS)] for d in range(5)]
        for f in range(FIELDS):
            minus = sum(fm[e, f] * CM * shifted[1][e] for e in range(FIELDS))
            plus = sum(fm[e, f] * CM * shifted[3][e] for e in range(FIELDS))
            b = (
                C2 * shifted[0][f],
                C1 * shifted[1][f] - minus,
                (C0 + 1.0) * shifted[2][f] + CP * linked(i, f, 0),
                C1 * shifted[3][f] + plus,
                C2 * shifted[4][f],
                shifted[1][f],
                shifted[3][f],
                shifted[2][f],
            )
            for d, value in enumerate(b):
                y_ref[i * 8 + d, f] = value

    scaled_matrix(fm, fmc)
    total = cycle * width
    start = lax.axis_index("blk") * width
    lane = lax.broadcasted_iota(jnp.int32, (8, width), 1)
    weight = {d: column_weight(lane + (start + d), total) for d in range(-2, 3)}

    def dense(i, z):
        rs = pl.ds(pl.multiple_of(i * 16, 16), 16)
        for q_ref, coef in ((q0, coef0), (q1, coef1)):
            q = [q_ref[f, rs, :].astype(F32) for f in range(FIELDS)]
            u = CU * q[1]
            for e in range(FIELDS):
                coef[e, rs, :] = (u if e != 1 else u + u) + fmc[e, e]
            for j, f in enumerate((0, 2, 3, 4)):
                coef[FIELDS + j, rs, :] = CU * q[f] + fmc[f, 1]
        both_q = [[q[f, rs, :].astype(F32) for f in range(FIELDS)] for q in (q0, q2)]
        for half in range(2):
            r8 = pl.ds(pl.multiple_of(i * 16 + half * 8, 8), 8)
            mine, last = [[x[half * 8 : half * 8 + 8] for x in q] for q in both_q]
            near, w = [], []
            for f in range(FIELDS):
                x, beside = forcing[f, r8, :], fe_ref[f, r8, :]
                near.append(
                    (
                        *shift_edges(x, beside, lane, width),
                        pltpu.roll(jnp.where(lane >= width - 2, beside, x), 2, 1),
                        pltpu.roll(jnp.where(lane < 2, beside, x), width - 2, 1),
                    )
                )
                w.append(x * weight[0])
            minus = flux(fmc, last, [a[0] for a in near])
            plus = flux(fmc, last, [a[1] for a in near])
            for f in range(FIELDS):
                m1, p1, m2, p2 = near[f]
                bs[0, f, r8, :] = C2 * m2
                bs[1, f, r8, :] = C1 * m1 - minus[f]
                bs[2, f, r8, :] = C1 * p1 + plus[f]
                bs[3, f, r8, :] = C2 * p2
                weighted[f, r8, :] = w[f]
                z = z + w[f] * forcing[f, r8, :]
                x = CU * (mine[1] * w[f] + mine[f] * w[1])
                for e in range(FIELDS):
                    x = x + fmc[f, e] * w[e]
                before = jnp.where(lane == 0, 0.0, pltpu.roll(x, 1, 1))
                after = jnp.where(lane == width - 1, 0.0, pltpu.roll(x, width - 1, 1))
                turned = v0[f, r8, :] + C1 * (m1 * weight[-1] + p1 * weight[1])
                turned = turned + C2 * (m2 * weight[-2] + p2 * weight[2])
                heavy[f, r8, :] = w[f] + turned + (before - after)
        return z

    z_ref[...] = lax.fori_loop(0, rows // 16, dense, jnp.zeros((8, width), F32), unroll=2)


def halo_kernel(
    fm, sa, sb, ra, rb, tiled, edge, kp_ref, hot, y_in,
    e1_ref, e2_ref, qe_ref, y_ref, big, q_ref, fmc,
):
    for i in (1, 3, 9, 11):
        y_ref[i] = y_in[i]
    rows, width = hot.shape[1], kp_ref.shape[2]
    step = rows // (width // SEG)
    for f in range(FIELDS):
        for e in range(FIELDS):
            fmc[f, e] = fm[f, e] * CM
    _, _, turned = gather_sources(sa, sb, ra, rb)
    g = jnp.concatenate(turned, axis=1)
    qe = mm(jnp.concatenate(turned, axis=0), edge[...])
    for f in range(FIELDS):
        qe_ref[f] = qe[f * rows : (f + 1) * rows]
    y = mm(hot[...], g).astype(BF16)
    spread_selection(tiled, big)
    part = in_segments((g, y[:rows], y[2 * rows :]), big[...], step)
    is_left = left_lanes(step, width)
    for i in range(2):
        if i:
            q2 = [jnp.where(is_left, part(1, f, 0), part(2, f, 0)) for f in range(FIELDS)]
        else:
            q2 = [part(0, f, 0) for f in range(FIELDS)]
        u = CU * q2[1]
        for d, near, sign in ((1, 5, -1.0), (3, 6, 1.0)):
            inner = sum(q2[f] * y_in[i * 8 + near, f] for f in range(FIELDS))
            for f in range(FIELDS):
                value = u * y_in[i * 8 + near, f]
                if f == 1:
                    value = value + CU * inner
                y_ref[i * 8 + d, f] = y_ref[i * 8 + d, f] + sign * value
    for f in range(FIELDS):
        q_ref[f] = part(0, f, 1)
    kp = [kp_ref[i] for i in range(5)]
    p = lax.broadcasted_iota(jnp.int32, (8, width), 1) & (SEG - 1)
    holds_high = (p != 5) & (p != 14)

    def both_halves(x):
        top = high(x)
        return jnp.where(holds_high, top, pltpu.roll(x - top, 2, 1))


    def body(r, c):
        def row(ref, index):
            return jnp.broadcast_to(ref[(*index, pl.ds(r, 1), slice(None))], (8, width))

        mu, linked, d, base = [], [], [], []
        for f in range(FIELDS):
            for i, out in ((0, mu), (8, linked)):
                value = row(y_in, (i, f)) * kp[0]
                for n in range(1, 5):
                    value = value + row(y_ref if n % 2 else y_in, (i + n, f)) * kp[n]
                out.append(value)
            x = mu[f]
            m1, p1 = pltpu.roll(x, 1, 1), pltpu.roll(x, width - 1, 1)
            m2, p2 = pltpu.roll(x, 2, 1), pltpu.roll(x, width - 2, 1)
            d.append(m1 - p1)
            base.append(
                C0 * x + C1 * (m1 + p1) + C2 * (m2 + p2) + CP * linked[f]
                + row(y_in, (7, f)) * kp[2]
            )
        moved = flux(fmc, [row(q_ref, (f,)) for f in range(FIELDS)], d)
        at = pl.ds(pl.multiple_of(r * (FIELDS * 8), 8), FIELDS * 8)
        e1_ref[at, :] = jnp.concatenate([both_halves(x) for x in mu], axis=0)
        e2_ref[at, :] = jnp.concatenate(
            [both_halves(b - m) for b, m in zip(base, moved)], axis=0
        )
        return c

    lax.fori_loop(0, step, body, 0, unroll=16)


def shift_edges(x, edge, lane, width):
    return (
        pltpu.roll(jnp.where(lane == width - 1, edge, x), 1, 1),
        pltpu.roll(jnp.where(lane == 0, edge, x), width - 1, 1),
    )


def spread(ref, index, r):
    return jnp.broadcast_to(ref[(*index, pl.ds(r, 1), slice(None))], (8, ref.shape[-1]))


def place(r, f):
    return pl.ds(pl.multiple_of((r * FIELDS + f) * 8, 8), 8)


def scaled_matrix(fm, fmc):
    for f in range(FIELDS):
        for e in range(FIELDS):
            fmc[f, e] = fm[f, e] * CM


def matrix_rows(fmc, width):
    return [[jnp.full((8, width), fmc[f, e]) for e in range(FIELDS)] for f in range(FIELDS)]


def stencil_products(dz, source, edges, products):
    count = edges.shape[0]
    outside = edges[...].astype(BF16)
    for j in range(products.shape[0]):
        x = source[j * count : (j + 1) * count, :]
        top = x.astype(BF16)
        rest = (x - top.astype(F32)).astype(BF16)
        dz[j * count : (j + 1) * count, :] = mm(
            jnp.concatenate([top, rest, outside], axis=1), products[j]
        )


def step_row(source, dz, coef, fmv, linked, r):
    width = source.shape[1]

    d = [dz[place(r, f), :width] for f in range(FIELDS)]
    out = []
    for e in range(FIELDS):
        value = C0 * source[place(r, e), :] + UNIT * dz[place(r, e), width:]
        value = value + CP * source[place(linked, e), :]
        for f in range(FIELDS):
            if f == e:
                m = spread(coef, (e,), r)
            elif e == 1:
                m = spread(coef, (FIELDS + (0, 2, 3, 4).index(f),), r)
            else:
                m = fmv[f][e]
            value = value - m * d[f]
        out.append(value)
    return out


def first_steps_kernel(
    cycle, fm, inv, forcing, fe, b0, qe, k_ref, products, e1, bs, coef1, weighted, heavy_in, z_ref,
    mu2, sens_ref,
    mu1, dz, heavy, fmc,
):
    rows, width = forcing.shape[1], forcing.shape[2]
    total = cycle * width
    blocks = width // SEG
    size = rows // blocks
    scaled_matrix(fm, fmc)
    lane = lax.broadcasted_iota(jnp.int32, (8, width), 1)
    start = lax.axis_index("blk") * width
    norm = 1.0 / math.sqrt(FIELDS * rows * total)
    beside = column_weight(jnp.where(lane < width // 2, lane + width, lane - width) + start, total)

    def finish(i, c):
        r8 = pl.ds(pl.multiple_of(i * 8, 8), 8)
        w = [fe[f, r8, :] * beside for f in range(FIELDS)]
        q = [qe[f, r8, :] for f in range(FIELDS)]
        for f in range(FIELDS):
            x = CU * (q[1] * w[f] + q[f] * w[1])
            for e in range(FIELDS):
                x = x + fmc[f, e] * w[e]
            before = jnp.where(lane == 0, pltpu.roll(x, 1, 1), 0.0)
            after = jnp.where(lane == width - 1, pltpu.roll(x, width - 1, 1), 0.0)
            heavy[f, r8, :] = heavy_in[f, r8, :] + (before - after)
        return c

    zero = jnp.zeros((8, width), F32)
    lax.fori_loop(0, rows // 8, finish, 0, unroll=8)
    z = z_ref[...]
    k = [k_ref[i] for i in range(5)]

    def first(j, acc):
        acc = list(acc)
        for i in range(size):
            r = j * size + i
            for f in range(FIELDS):
                value = spread(bs, (0, f), r) * k[0] + spread(bs, (1, f), r) * k[1]
                value = value + spread(b0, (f,), r) * k[2] + spread(bs, (2, f), r) * k[3]
                value = value + spread(bs, (3, f), r) * k[4]
                mu1[place(r, f), :] = value
                acc[f] = acc[f] + value * spread(weighted, (f,), r)
        return tuple(acc)

    acc = lax.fori_loop(0, blocks, first, (zero,) * FIELDS)
    fmv = matrix_rows(fmc, width)
    stencil_products(dz, mu1, e1, products)

    def second(j, acc):
        acc = list(acc)
        for i in range(size):
            r = j * size + i
            made = step_row(mu1, dz, coef1, fmv, inv[r], r)
            for f, value in enumerate(made):
                value = value + spread(forcing, (f,), r) * k[2]
                mu2[place(r, f), :] = value
                acc[f] = acc[f] + value * spread(heavy, (f,), r)
        return tuple(acc)

    acc = lax.fori_loop(0, blocks, second, acc)
    source_part = jnp.sum(z, axis=0, keepdims=True) * k[2]
    acc = (sum(acc) - 2.0 * source_part) * norm
    acc = jnp.broadcast_to(jnp.sum(acc, axis=1, keepdims=True), (8, width))
    sub = lax.broadcasted_iota(jnp.int32, (8, width), 0)
    for group in range(GRP_DEV):
        mine = jnp.where(sub == group * AMP + lane, acc, 0.0)
        sens_ref[group : group + 1, :] = jnp.sum(mine, axis=0, keepdims=True)[:, :AMP]


def last_step_kernel(fm, inv, mu2, coef0, e2, products, out_hbm, dz, stage, fmc, out_sems):
    rows, width = coef0.shape[1:]
    blocks = width // SEG
    size = rows // blocks
    scaled_matrix(fm, fmc)
    fmv = matrix_rows(fmc, width)
    stencil_products(dz, mu2, e2, products)

    def send(j):
        at = pl.ds(pl.multiple_of(j * 8, 8), 8)
        return pltpu.make_async_copy(stage.at[:, at, :], out_hbm.at[:, at, :], out_sems.at[j])

    def third(j, c):
        for half in range(size // 8):
            r0 = j * size + half * 8
            made = [step_row(mu2, dz, coef0, fmv, inv[r0 + i], r0 + i) for i in range(8)]
            at = pl.ds(pl.multiple_of(r0, 8), 8)
            for e in range(FIELDS):
                turned = jnp.swapaxes(jnp.stack([x[e] for x in made]), 0, 1)
                for pair in range(PAIRS):
                    stage[pair * FIELDS + e, at, :] = turned[pair]
            send(j * (size // 8) + half).start()
        return c

    lax.fori_loop(0, blocks, third, 0)
    for j in range(rows // 8):
        send(j).wait()


def shift_pairs(devices, k):
    return [(i, (i + k) % devices) for i in range(devices)]


def round_over(x, axis, bit):
    return x + lax.ppermute(x, axis, [(i, i ^ bit) for i in range(lax.axis_size(axis))])


def to_neighbours(send_a, send_b, cycle):
    return (
        lax.ppermute(send_a, "blk", [(i, i ^ 1) for i in range(cycle)]),
        lax.ppermute(
            send_b,
            "blk",
            [(i, (i + 1) % cycle if i % 2 else (i - 1) % cycle) for i in range(cycle)],
        ),
    )


def on_device(checkpoints, owner, flux_matrix, row_link, blade_group, forcing):
    n_out = lax.axis_size("out")
    cycle = lax.axis_size("blk")
    rows, width = forcing.shape[1], forcing.shape[2]
    blocks = width // SEG
    step_rows = rows // blocks
    slot = checkpoints[0]

    def struct(shape, kind=F32):
        return jax.ShapeDtypeStruct(shape, kind)

    sems = pltpu.SemaphoreType.DMA
    field = struct((FIELDS, rows, width))
    strip = struct((FIELDS * SLOT, rows), BF16)
    factors = struct((5, PAIRS, width))
    slots = [slot] + [lax.ppermute(slot, "out", shift_pairs(n_out, k)) for k in range(1, n_out)]

    def stay(x):
        return pltpu.with_memory_space_constraint(x, pltpu.HBM)

    def call(kernel, out_shape, smem, hbm, vmem, scratch, limit, flops, name, out_specs=None):
        return pl.pallas_call(
            kernel,
            out_shape=out_shape,
            in_specs=[SMEM] * len(smem) + [HBM] * len(hbm) + [VMEM] * len(vmem),
            out_specs=out_specs or (VMEM,) * len(out_shape),
            scratch_shapes=scratch,
            compiler_params=pltpu.CompilerParams(vmem_limit_bytes=limit),
            cost_estimate=cost(flops, 10**6),
            name=name,
        )(*map(stay, smem), *map(stay, hbm), *vmem)

    kept = (
        forcing, row_link, forcing_select(width), slot, state_select(width),
        *halo_selects(width), stencil_selects(width),
    )
    made = (
        factors, factors, field, field, strip, strip,
        struct((rows,), jnp.int32), struct(owner.shape, jnp.int32), struct(flux_matrix.shape),
    )
    made += tuple(struct(x.shape, x.dtype) for x in kept)
    k, kp, b0, v0, f_a, f_b, inv, owner_s, fm_s, *held = call(
        functools.partial(prepare_kernel, cycle),
        made,
        (blade_group, row_link[0], owner, flux_matrix),
        kept,
        (),
        [sems((len(kept),))],
        SMALL_LIMIT,
        10**8,
        "prepare",
        (VMEM,) * 6 + (SMEM,) * 3 + (VMEM,) * len(kept),
    )
    forcing_v, link, _, slot_v, state_sel, *held = held
    forcing_tiled, state_tiled, edge, state_edge, products = held
    f_sent = (f_a, f_b, *to_neighbours(f_a, f_b, cycle))

    q_a, q_b, *chosen = call(
        functools.partial(strips_kernel, n_out),
        (strip, strip) + (struct(slot.shape, slot.dtype),) * STEPS,
        (owner_s,),
        (),
        (slot_v, *slots[1:], state_sel),
        [],
        SMALL_LIMIT,
        10**7,
        "strips",
    )
    q_sent = (q_a, q_b, *to_neighbours(q_a, q_b, cycle))

    coefficients = struct((2 * FIELDS - 1, rows, width))
    y, fe, hot, bs, coef0, coef1, weighted, heavy, z = call(
        functools.partial(halo_forcing_kernel, cycle),
        (
            struct((16, FIELDS, step_rows, width)), field, struct((3 * rows, rows), BF16),
            struct((4, FIELDS, rows, width)), coefficients, coefficients, field, field,
            struct((PAIRS, width)),
        ),
        (fm_s,),
        (),
        (link, *f_sent, forcing_tiled, edge, forcing_v, v0, *chosen),
        [
            pltpu.VMEM((blocks * 4 * SLOT, forcing_tiled.shape[1]), BF16),
            pltpu.SMEM((FIELDS, FIELDS), F32),
        ],
        SMALL_LIMIT,
        10**8,
        "halo_forcing",
    )
    flat = rows * FIELDS * PAIRS
    edges = (step_rows * FIELDS * 8, width)
    halo_operands = (*q_sent, state_tiled, state_edge, kp, hot, y)
    halo_scratch = [
        pltpu.VMEM(edges, F32),
        pltpu.VMEM((FIELDS, rows, width), F32),
        like(y),
        pltpu.VMEM((blocks * 4 * SLOT, state_tiled.shape[1]), BF16),
        pltpu.VMEM((FIELDS, step_rows, width), F32),
        pltpu.SMEM((FIELDS, FIELDS), F32),
    ]

    def halo_and_first_steps(fm, inv, *refs):
        halo_in, refs = refs[: len(halo_operands)], refs[len(halo_operands) :]
        forcing, fe, b0, k_ref, products, *ready = refs[:10]
        mu2, sens, e2, e1, qe, *work = refs[10 : 13 + len(halo_scratch)]
        halo_kernel(fm, *halo_in, e1, e2, qe, *work)
        first_steps_kernel(
            cycle, fm, inv, forcing, fe, b0, qe, k_ref, products, e1, *ready,
            mu2, sens, *refs[13 + len(halo_scratch) :],
        )

    mu2, sens, e2 = call(
        halo_and_first_steps,
        (struct((flat, width)), struct((GRP_DEV, AMP)), struct(edges)),
        (fm_s, inv),
        (),
        (*halo_operands, forcing_v, fe, b0, k, products, bs, coef1, weighted, heavy, z),
        halo_scratch
        + [
            pltpu.VMEM((flat, width), F32),
            pltpu.VMEM((flat, 2 * width), F32),
            pltpu.VMEM((FIELDS, rows, width), F32),
            pltpu.SMEM((FIELDS, FIELDS), F32),
        ],
        VMEM_LIMIT,
        10**9,
        "first_steps",
    )

    pairs_fields = PAIRS * FIELDS
    bits = [1 << i for i in reversed(range(cycle.bit_length() - 1))]
    exact = 1 << len(bits) == cycle
    if not exact:
        sens = lax.psum(sens, "blk")
    if exact and bits:
        sens = round_over(sens, "blk", bits.pop(0))
    (adjoint,) = call(
        last_step_kernel,
        (struct((pairs_fields, rows, width)),),
        (fm_s, inv),
        (),
        (mu2, coef0, e2, products),
        [
            pltpu.VMEM((flat, 2 * width), F32),
            pltpu.VMEM((pairs_fields, rows, width), F32),
            pltpu.SMEM((FIELDS, FIELDS), F32),
            sems((rows // 8,)),
        ],
        VMEM_LIMIT,
        10**9,
        "last_step",
        (HBM,),
    )
    for bit in bits if exact else ():
        sens = round_over(sens, "blk", bit)
    return adjoint.reshape(GRP_DEV, AMP, FIELDS, rows, width), sens


def solution(mesh):
    return jax.shard_map(
        on_device,
        mesh=mesh,
        in_specs=(P("out", None, None, "blk"), P(), P(), P("blk", None), P(), P(None, None, "blk")),
        out_specs=(P("out", None, None, None, "blk"), P("out", None)),
        check_vma=False,
    )
```

```python
import functools
import math

import jax
import jax.numpy as jnp
import numpy as np
from jax import lax
from jax.experimental import pallas as pl
from jax.experimental.pallas import tpu as pltpu
from jax.sharding import PartitionSpec as P

FIELDS = 5
BLADES = 96
AMP = 4
GRP_DEV = 2
STEPS = 3
PAIRS = GRP_DEV * AMP

time_step = 0.25
second_diff = 0.1
fourth_diff = 0.02
link_weight = 0.5
two_pi = 2.0 * math.pi

C0 = 1.0 - time_step * (2.0 * second_diff + 6.0 * fourth_diff + link_weight)
C1 = time_step * (second_diff + 4.0 * fourth_diff)
C2 = -time_step * fourth_diff
CP = time_step * link_weight
CM = 0.5 * time_step
CU = 0.25 * time_step

FW = 6
QW = 4
PARTS = 3
SLOT = 32
LINK_ROW = PARTS * FW
SEG = 16
HALF = SEG // 2
VMEM_LIMIT = 40 * 2**20
SMALL_LIMIT = 16 * 2**20

VMEM = pl.BlockSpec(memory_space=pltpu.VMEM)
SMEM = pl.BlockSpec(memory_space=pltpu.SMEM)
HBM = pl.BlockSpec(memory_space=pltpu.HBM)
UNIT = time_step * fourth_diff
NEAR = round(C1 / UNIT)
F32 = jnp.float32
BF16 = jnp.bfloat16
NT = (((1,), (1,)), ((), ()))
TN = (((0,), (0,)), ((), ()))
NN = (((1,), (0,)), ((), ()))


def mm(a, b, dims=NN):
    return lax.dot_general(a, b, dims, preferred_element_type=F32)


def split3(x):
    hi = x.astype(BF16)
    rest = x - hi.astype(F32)
    mid = rest.astype(BF16)
    return hi, mid, (rest - mid.astype(F32)).astype(BF16)


def exact_mm(a, x):
    hi, mid, lo = split3(x)
    return mm(a, hi) + mm(a, mid) + mm(a, lo)


def fetch(moves, sems):
    copies = [pltpu.make_async_copy(src, dst, sems.at[i]) for i, (src, dst) in enumerate(moves)]
    for copy in copies:
        copy.start()
    return copies


def arrive(copies):
    for copy in copies:
        copy.wait()


def like(x):
    return pltpu.VMEM(x.shape, x.dtype)


def cost(flops, moved):
    return pl.CostEstimate(flops=flops, bytes_accessed=moved, transcendentals=0)


def forcing_select(width):
    out = np.zeros((PARTS, width, width), np.float32)
    for part in range(PARTS):
        for j in range(FW):
            out[part, j, part * FW + j] = 1.0
            out[part, width - FW + j, SLOT + part * FW + j] = 1.0
    return out.reshape(PARTS * width, width).astype(jnp.bfloat16)


def state_select(width):
    out = np.zeros((2 * SLOT, STEPS, width), np.float32)
    for n in range(STEPS):
        for j in range(QW):
            out[n * QW + j, n, j] = 1.0
            out[SLOT + n * QW + j, n, width - QW + j] = 1.0
    return out.reshape(2 * SLOT, STEPS * width).astype(jnp.bfloat16)


def give(send_a, send_b, f, both):
    even = lax.axis_index("blk") % 2 == 0
    left, right = both[:SLOT], both[SLOT:]
    send_a[f * SLOT : (f + 1) * SLOT] = jnp.where(even, right, left).astype(BF16)
    send_b[f * SLOT : (f + 1) * SLOT] = jnp.where(even, left, right).astype(BF16)


def strips_kernel(n_out, *refs):
    owner = refs[0]
    slots = refs[1 : 1 + n_out]
    sel, send_a, send_b, *chosen = refs[1 + n_out :]
    me = lax.axis_index("out")
    for n, target in enumerate(chosen):
        which = (me - owner[n] + n_out) % n_out
        for s, slot in enumerate(slots):

            @pl.when(which == s)
            def _():
                target[...] = slot[...]

    beside = [jnp.concatenate([q[f] for q in chosen], axis=1) for f in range(FIELDS)]
    rows = beside[0].shape[0]
    both = mm(sel[...], jnp.concatenate(beside, axis=0), NT)
    for f in range(FIELDS):
        give(send_a, send_b, f, both[:, f * rows : (f + 1) * rows])


def column_factor(columns, pair, start, total, group_base, blade_group):
    scaled = columns * BLADES
    first = ((start + total - HALF) * BLADES) // total - BLADES
    group = jnp.full(columns.shape, -1, jnp.int32)
    numerator = jnp.zeros(columns.shape, jnp.int32)
    width = columns.shape[-1]
    for j in range((width + SEG) * BLADES // total + 2):
        blade = first + j
        inside = (scaled >= blade * total) & (scaled < (blade + 1) * total)
        group = jnp.where(inside, blade_group[(blade + BLADES) % BLADES], group)
        numerator = jnp.where(inside, scaled - blade * total, numerator)
    phase = numerator.astype(F32) / total
    amp = pair & (AMP - 1)
    order = ((amp >> 1) + 1).astype(F32)
    angle = two_pi * order * phase
    harmonic = jnp.where((amp & 1) == 0, jnp.cos(angle), jnp.sin(angle))
    return jnp.where(group == group_base + pair // AMP, harmonic, 0.0)


def column_weight(columns, total):
    columns = jnp.where(columns < 0, columns + total, columns)
    columns = jnp.where(columns >= total, columns - total, columns)
    return 1.0 + 2.0 * columns.astype(F32) / total


def flux(fm, q, d):
    inner = q[0] * d[0]
    for f in range(1, FIELDS):
        inner = inner + q[f] * d[f]
    u = q[1] * CU
    out = []
    for e in range(FIELDS):
        value = u * d[e]
        for f in range(FIELDS):
            value = value + fm[f, e] * d[f]
        if e == 1:
            value = value + CU * inner
        out.append(value)
    return out


def prepare_kernel(cycle, blade_group, link_s, *refs):
    owner, fm = refs[:2]
    kept = refs[2 : (len(refs) - 12) // 2 + 2]
    k_ref, kp_ref, b0_ref, v0_ref, send_a, send_b, inv_ref, owner_out, fm_out, *held, sems = refs[
        2 + len(kept) :
    ]
    copies = fetch(zip(kept, held), sems)
    for i in range(owner.shape[0]):
        owner_out[i] = owner[i]
    for f in range(FIELDS):
        for e in range(FIELDS):
            fm_out[f, e] = fm[f, e]
    forcing, link, sel = held[:3]
    rows, width = forcing.shape[1:]
    total = cycle * width
    start = lax.axis_index("blk") * width

    def invert(r, c):
        inv_ref[link_s[r]] = r
        return c

    lax.fori_loop(0, rows, invert, 0, unroll=8)
    lane = lax.broadcasted_iota(jnp.int32, (8, width), 1)
    sub = lax.broadcasted_iota(jnp.int32, (8, width), 0)
    p = lane & (SEG - 1)
    packed = jnp.where(p < HALF, p - QW, width - QW + p - HALF) + start
    args = (start, total, lax.axis_index("out") * GRP_DEV, blade_group)
    for i in range(5):
        k_ref[i] = column_factor(lane + start + (i - 2), sub, *args)
        kp_ref[i] = column_factor(packed + (i - 2), sub, *args)
    arrive(copies[:3])
    links = link[...].astype(F32)
    parts = [split3(forcing[f]) for f in range(FIELDS)]
    hot = one_hot(links, rows)
    flat = jnp.concatenate(sum(parts, ()), axis=1)
    linked = mm(hot, flat)
    linking = mm(hot, flat, TN)
    weight = column_weight(lax.broadcasted_iota(jnp.int32, (1, width), 1) + start, total)
    chosen = mm(
        jnp.concatenate([jnp.concatenate(three, axis=1) for three in parts], axis=0), sel[...]
    )
    row = lax.broadcasted_iota(jnp.int32, (2 * SLOT, rows), 0)
    links = jnp.broadcast_to(links, row.shape)
    for f in range(FIELDS):

        def moved(x):
            three = [x[:, (f * PARTS + i) * width : (f * PARTS + i + 1) * width] for i in range(PARTS)]
            return three[0] + three[1] + three[2]

        b0_ref[f] = (C0 + 1.0) * forcing[f] + CP * moved(linked)
        v0_ref[f] = (C0 * forcing[f] + CP * moved(linking)) * weight
        turned = chosen[f * rows : (f + 1) * rows].T[: 2 * SLOT]
        if f == 0:
            turned = jnp.where(row % SLOT == LINK_ROW, links, turned)
        give(send_a, send_b, f, turned)
    arrive(copies[3:])


def one_hot(links, rows):
    row = lax.broadcasted_iota(jnp.int32, (rows, rows), 0).astype(F32)
    return jnp.where(links == row, 1.0, 0.0).astype(BF16)


def halo_selects(width):
    blocks = width // SEG
    forcing_sel = np.zeros((4 * SLOT, 5, SEG), np.float32)
    state_sel = np.zeros((4 * SLOT, 2, SEG), np.float32)
    edge = np.zeros((4 * SLOT, width), np.float32)

    def place(column, size):
        if column < 0:
            return 0, column + size
        if column < size:
            return 1, column
        if column < width:
            return 2, column - (width - size)
        return 3, column - width

    def forcing_rows(column):
        source, j = place(column, FW)
        return [source * SLOT + part * FW + j for part in range(PARTS)] if 0 <= j < FW else []

    for p in range(SEG):
        column = p - QW if p < HALF else width - QW + p - HALF
        for i in range(5):
            for row in forcing_rows(column + i - 2):
                forcing_sel[row, i, p] = 1.0
        source, j = place(column, QW)
        for i, n in ((0, STEPS - 1), (1, STEPS - 2)):
            state_sel[source * SLOT + n * QW + j, i, p] = 1.0
    for lane, column in ((width - 2, -2), (width - 1, -1), (0, width), (1, width + 1)):
        for row in forcing_rows(column):
            edge[row, lane] = 1.0
    state_edge = np.zeros((4 * SLOT, width), np.float32)
    for lane, column in ((width - 1, -1), (0, width)):
        source, j = place(column, QW)
        state_edge[source * SLOT + j, lane] = 1.0

    def tiled(x):
        return np.repeat(x[:, :, None, :], blocks, axis=2).reshape(4 * SLOT, -1)

    return tuple(
        x.astype(jnp.bfloat16) for x in (tiled(forcing_sel), tiled(state_sel), edge, state_edge)
    )


def stencil_selects(width):
    blocks = width // SEG
    out = np.zeros((blocks, 3, width, 2 * width), np.float32)

    def spread(column):
        near = ((1, 1.0), (-1, -1.0))
        far = ((-1, NEAR), (1, NEAR), (-2, -1.0), (2, -1.0))
        pairs = [(column + d, w) for d, w in near if 0 <= column + d < width]
        return pairs + [(width + column + d, w) for d, w in far if 0 <= column + d < width]

    for column in range(width):
        for lane, w in spread(column):
            out[:, :2, column, lane] = w
    for j in range(blocks):
        for p, column in ((2, -2), (3, -1), (HALF + QW, width), (HALF + QW + 1, width + 1)):
            for held in (p, p + 2) if column in (-1, width) else (p,):
                for to, w in spread(column):
                    out[j, 2, j * SEG + held, to] = w
    return out.reshape(blocks, 3 * width, 2 * width).astype(jnp.bfloat16)


def high(x):
    return x.astype(BF16).astype(F32)


def gather_sources(sa, sb, ra, rb):
    even = lax.axis_index("blk") % 2 == 0
    sa, sb, ra, rb = (x[...].astype(F32) for x in (sa, sb, ra, rb))
    own_left, own_right = jnp.where(even, sb, sa), jnp.where(even, sa, sb)
    left, right = jnp.where(even, rb, ra), jnp.where(even, ra, rb)
    turned = []
    for f in range(FIELDS):
        s = slice(f * SLOT, (f + 1) * SLOT)
        g = jnp.concatenate([left[s], own_left[s], own_right[s], right[s]], axis=0)
        turned.append(g.T.astype(BF16))
    return left, right, turned


def spread_selection(tiled, big):
    blocks = big.shape[0] // (4 * SLOT)
    lane_block = lax.broadcasted_iota(jnp.int32, tiled.shape, 1) % (blocks * SEG) // SEG
    for j in range(blocks):
        big[j * 4 * SLOT : (j + 1) * 4 * SLOT, :] = jnp.where(
            lane_block == j, tiled[...].astype(F32), 0.0
        ).astype(BF16)


def in_segments(sets, big, step):
    blocks = big.shape[0] // (4 * SLOT)
    width = blocks * SEG
    pieces = []
    for x in sets:
        for f in range(FIELDS):
            mine = x[:, f * 4 * SLOT : (f + 1) * 4 * SLOT]
            pieces.append(
                jnp.concatenate([mine[j * step : (j + 1) * step] for j in range(blocks)], axis=1)
            )
    y = mm(jnp.concatenate(pieces, axis=0), big)

    def part(i, f, which):
        start = (i * FIELDS + f) * step
        return y[start : start + step, which * width : (which + 1) * width]

    return part


def left_lanes(step, width):
    return lax.broadcasted_iota(jnp.int32, (step, width), 1) & (SEG - 1) < HALF


def halo_forcing_kernel(
    cycle, fm, link, sa, sb, ra, rb, tiled, edge, forcing, v0, q0, q1, q2,
    y_ref, fe_ref, hot_ref, bs, coef0, coef1, weighted, heavy, z_ref, big, fmc,
):
    rows, width = link.shape[1], edge.shape[1]
    step = rows // (width // SEG)
    left, right, turned = gather_sources(sa, sb, ra, rb)
    hot = jnp.concatenate(
        [
            one_hot(left[LINK_ROW : LINK_ROW + 1], rows),
            one_hot(link[...].astype(F32), rows),
            one_hot(right[LINK_ROW : LINK_ROW + 1], rows),
        ],
        axis=0,
    )
    hot_ref[...] = hot
    k_wide = 4 * SLOT
    source = lax.broadcasted_iota(jnp.int32, (rows, FIELDS * k_wide), 1) % k_wide // SLOT

    def permuted(x):
        y = mm(hot, x)
        by_left, by_right = y[:rows], y[2 * rows :]
        outer = jnp.where(source == 0, by_left, by_right)
        by_tile = jnp.where((source == 1) | (source == 2), y[rows : 2 * rows], outer)
        return by_left.astype(BF16), by_right.astype(BF16), by_tile.astype(BF16)

    fe = mm(jnp.concatenate(turned, axis=0), edge[...])
    for f in range(FIELDS):
        fe_ref[f] = fe[f * rows : (f + 1) * rows]
    g = jnp.concatenate(turned, axis=1)
    by_left, by_right, by_tile = permuted(g)
    spread_selection(tiled, big)
    part = in_segments((g, by_left, by_right), big[...], step)
    linked = in_segments((by_tile, permuted(by_tile)[2]), big[:, 2 * width : 3 * width], step)
    is_left = left_lanes(step, width)

    def at(linked, f, which):
        if linked:
            return jnp.where(is_left, part(1, f, which), part(2, f, which))
        return part(0, f, which)

    for i in range(2):
        shifted = [[at(i, f, d) for f in range(FIELDS)] for d in range(5)]
        for f in range(FIELDS):
            minus = sum(fm[e, f] * CM * shifted[1][e] for e in range(FIELDS))
            plus = sum(fm[e, f] * CM * shifted[3][e] for e in range(FIELDS))
            b = (
                C2 * shifted[0][f],
                C1 * shifted[1][f] - minus,
                (C0 + 1.0) * shifted[2][f] + CP * linked(i, f, 0),
                C1 * shifted[3][f] + plus,
                C2 * shifted[4][f],
                shifted[1][f],
                shifted[3][f],
                shifted[2][f],
            )
            for d, value in enumerate(b):
                y_ref[i * 8 + d, f] = value

    scaled_matrix(fm, fmc)
    total = cycle * width
    start = lax.axis_index("blk") * width
    lane = lax.broadcasted_iota(jnp.int32, (8, width), 1)
    weight = {d: column_weight(lane + (start + d), total) for d in range(-2, 3)}

    def dense(i, z):
        rs = pl.ds(pl.multiple_of(i * 16, 16), 16)
        for q_ref, coef in ((q0, coef0), (q1, coef1)):
            q = [q_ref[f, rs, :].astype(F32) for f in range(FIELDS)]
            u = CU * q[1]
            for e in range(FIELDS):
                coef[e, rs, :] = (u if e != 1 else u + u) + fmc[e, e]
            for j, f in enumerate((0, 2, 3, 4)):
                coef[FIELDS + j, rs, :] = CU * q[f] + fmc[f, 1]
        both_q = [[q[f, rs, :].astype(F32) for f in range(FIELDS)] for q in (q0, q2)]
        for half in range(2):
            r8 = pl.ds(pl.multiple_of(i * 16 + half * 8, 8), 8)
            mine, last = [[x[half * 8 : half * 8 + 8] for x in q] for q in both_q]
            near, w = [], []
            for f in range(FIELDS):
                x, beside = forcing[f, r8, :], fe_ref[f, r8, :]
                near.append(
                    (
                        *shift_edges(x, beside, lane, width),
                        pltpu.roll(jnp.where(lane >= width - 2, beside, x), 2, 1),
                        pltpu.roll(jnp.where(lane < 2, beside, x), width - 2, 1),
                    )
                )
                w.append(x * weight[0])
            minus = flux(fmc, last, [a[0] for a in near])
            plus = flux(fmc, last, [a[1] for a in near])
            for f in range(FIELDS):
                m1, p1, m2, p2 = near[f]
                bs[0, f, r8, :] = C2 * m2
                bs[1, f, r8, :] = C1 * m1 - minus[f]
                bs[2, f, r8, :] = C1 * p1 + plus[f]
                bs[3, f, r8, :] = C2 * p2
                weighted[f, r8, :] = w[f]
                z = z + w[f] * forcing[f, r8, :]
                x = CU * (mine[1] * w[f] + mine[f] * w[1])
                for e in range(FIELDS):
                    x = x + fmc[f, e] * w[e]
                before = jnp.where(lane == 0, 0.0, pltpu.roll(x, 1, 1))
                after = jnp.where(lane == width - 1, 0.0, pltpu.roll(x, width - 1, 1))
                turned = v0[f, r8, :] + C1 * (m1 * weight[-1] + p1 * weight[1])
                turned = turned + C2 * (m2 * weight[-2] + p2 * weight[2])
                heavy[f, r8, :] = w[f] + turned + (before - after)
        return z

    z_ref[...] = lax.fori_loop(0, rows // 16, dense, jnp.zeros((8, width), F32), unroll=2)


def halo_kernel(
    fm, sa, sb, ra, rb, tiled, edge, kp_ref, hot, y_in,
    e1_ref, e2_ref, qe_ref, y_ref, big, q_ref, fmc,
):
    for i in (1, 3, 9, 11):
        y_ref[i] = y_in[i]
    rows, width = hot.shape[1], kp_ref.shape[2]
    step = rows // (width // SEG)
    for f in range(FIELDS):
        for e in range(FIELDS):
            fmc[f, e] = fm[f, e] * CM
    _, _, turned = gather_sources(sa, sb, ra, rb)
    g = jnp.concatenate(turned, axis=1)
    qe = mm(jnp.concatenate(turned, axis=0), edge[...])
    for f in range(FIELDS):
        qe_ref[f] = qe[f * rows : (f + 1) * rows]
    y = mm(hot[...], g).astype(BF16)
    spread_selection(tiled, big)
    part = in_segments((g, y[:rows], y[2 * rows :]), big[...], step)
    is_left = left_lanes(step, width)
    for i in range(2):
        if i:
            q2 = [jnp.where(is_left, part(1, f, 0), part(2, f, 0)) for f in range(FIELDS)]
        else:
            q2 = [part(0, f, 0) for f in range(FIELDS)]
        u = CU * q2[1]
        for d, near, sign in ((1, 5, -1.0), (3, 6, 1.0)):
            inner = sum(q2[f] * y_in[i * 8 + near, f] for f in range(FIELDS))
            for f in range(FIELDS):
                value = u * y_in[i * 8 + near, f]
                if f == 1:
                    value = value + CU * inner
                y_ref[i * 8 + d, f] = y_ref[i * 8 + d, f] + sign * value
    for f in range(FIELDS):
        q_ref[f] = part(0, f, 1)
    kp = [kp_ref[i] for i in range(5)]
    p = lax.broadcasted_iota(jnp.int32, (8, width), 1) & (SEG - 1)
    holds_high = (p != 5) & (p != 14)

    def both_halves(x):
        top = high(x)
        return jnp.where(holds_high, top, pltpu.roll(x - top, 2, 1))


    def body(r, c):
        def row(ref, index):
            return jnp.broadcast_to(ref[(*index, pl.ds(r, 1), slice(None))], (8, width))

        mu, linked, d, base = [], [], [], []
        for f in range(FIELDS):
            for i, out in ((0, mu), (8, linked)):
                value = row(y_in, (i, f)) * kp[0]
                for n in range(1, 5):
                    value = value + row(y_ref if n % 2 else y_in, (i + n, f)) * kp[n]
                out.append(value)
            x = mu[f]
            m1, p1 = pltpu.roll(x, 1, 1), pltpu.roll(x, width - 1, 1)
            m2, p2 = pltpu.roll(x, 2, 1), pltpu.roll(x, width - 2, 1)
            d.append(m1 - p1)
            base.append(
                C0 * x + C1 * (m1 + p1) + C2 * (m2 + p2) + CP * linked[f]
                + row(y_in, (7, f)) * kp[2]
            )
        moved = flux(fmc, [row(q_ref, (f,)) for f in range(FIELDS)], d)
        at = pl.ds(pl.multiple_of(r * (FIELDS * 8), 8), FIELDS * 8)
        e1_ref[at, :] = jnp.concatenate([both_halves(x) for x in mu], axis=0)
        e2_ref[at, :] = jnp.concatenate(
            [both_halves(b - m) for b, m in zip(base, moved)], axis=0
        )
        return c

    lax.fori_loop(0, step, body, 0, unroll=16)


def shift_edges(x, edge, lane, width):
    return (
        pltpu.roll(jnp.where(lane == width - 1, edge, x), 1, 1),
        pltpu.roll(jnp.where(lane == 0, edge, x), width - 1, 1),
    )


def spread(ref, index, r):
    return jnp.broadcast_to(ref[(*index, pl.ds(r, 1), slice(None))], (8, ref.shape[-1]))


def place(r, f):
    return pl.ds(pl.multiple_of((r * FIELDS + f) * 8, 8), 8)


def scaled_matrix(fm, fmc):
    for f in range(FIELDS):
        for e in range(FIELDS):
            fmc[f, e] = fm[f, e] * CM


def matrix_rows(fmc, width):
    return [[jnp.full((8, width), fmc[f, e]) for e in range(FIELDS)] for f in range(FIELDS)]


def stencil_products(dz, source, edges, products):
    count = edges.shape[0]
    outside = edges[...].astype(BF16)
    for j in range(products.shape[0]):
        x = source[j * count : (j + 1) * count, :]
        top = x.astype(BF16)
        rest = (x - top.astype(F32)).astype(BF16)
        dz[j * count : (j + 1) * count, :] = mm(
            jnp.concatenate([top, rest, outside], axis=1), products[j]
        )


def step_row(source, dz, coef, fmv, linked, r):
    width = source.shape[1]

    d = [dz[place(r, f), :width] for f in range(FIELDS)]
    out = []
    for e in range(FIELDS):
        value = C0 * source[place(r, e), :] + UNIT * dz[place(r, e), width:]
        value = value + CP * source[place(linked, e), :]
        for f in range(FIELDS):
            if f == e:
                m = spread(coef, (e,), r)
            elif e == 1:
                m = spread(coef, (FIELDS + (0, 2, 3, 4).index(f),), r)
            else:
                m = fmv[f][e]
            value = value - m * d[f]
        out.append(value)
    return out


def first_steps_kernel(
    cycle, fm, inv, forcing, fe, b0, qe, k_ref, products, e1, bs, coef1, weighted, heavy_in, z_ref,
    mu2, sens_ref,
    mu1, dz, heavy, fmc,
):
    rows, width = forcing.shape[1], forcing.shape[2]
    total = cycle * width
    blocks = width // SEG
    size = rows // blocks
    scaled_matrix(fm, fmc)
    lane = lax.broadcasted_iota(jnp.int32, (8, width), 1)
    start = lax.axis_index("blk") * width
    norm = 1.0 / math.sqrt(FIELDS * rows * total)
    beside = column_weight(jnp.where(lane < width // 2, lane + width, lane - width) + start, total)

    def finish(i, c):
        r8 = pl.ds(pl.multiple_of(i * 8, 8), 8)
        w = [fe[f, r8, :] * beside for f in range(FIELDS)]
        q = [qe[f, r8, :] for f in range(FIELDS)]
        for f in range(FIELDS):
            x = CU * (q[1] * w[f] + q[f] * w[1])
            for e in range(FIELDS):
                x = x + fmc[f, e] * w[e]
            before = jnp.where(lane == 0, pltpu.roll(x, 1, 1), 0.0)
            after = jnp.where(lane == width - 1, pltpu.roll(x, width - 1, 1), 0.0)
            heavy[f, r8, :] = heavy_in[f, r8, :] + (before - after)
        return c

    zero = jnp.zeros((8, width), F32)
    lax.fori_loop(0, rows // 8, finish, 0, unroll=8)
    z = z_ref[...]
    k = [k_ref[i] for i in range(5)]

    def first(j, acc):
        acc = list(acc)
        for i in range(size):
            r = j * size + i
            for f in range(FIELDS):
                value = spread(bs, (0, f), r) * k[0] + spread(bs, (1, f), r) * k[1]
                value = value + spread(b0, (f,), r) * k[2] + spread(bs, (2, f), r) * k[3]
                value = value + spread(bs, (3, f), r) * k[4]
                mu1[place(r, f), :] = value
                acc[f] = acc[f] + value * spread(weighted, (f,), r)
        return tuple(acc)

    acc = lax.fori_loop(0, blocks, first, (zero,) * FIELDS)
    fmv = matrix_rows(fmc, width)
    stencil_products(dz, mu1, e1, products)

    def second(j, acc):
        acc = list(acc)
        for i in range(size):
            r = j * size + i
            made = step_row(mu1, dz, coef1, fmv, inv[r], r)
            for f, value in enumerate(made):
                value = value + spread(forcing, (f,), r) * k[2]
                mu2[place(r, f), :] = value
                acc[f] = acc[f] + value * spread(heavy, (f,), r)
        return tuple(acc)

    acc = lax.fori_loop(0, blocks, second, acc)
    source_part = jnp.sum(z, axis=0, keepdims=True) * k[2]
    acc = (sum(acc) - 2.0 * source_part) * norm
    acc = jnp.broadcast_to(jnp.sum(acc, axis=1, keepdims=True), (8, width))
    sub = lax.broadcasted_iota(jnp.int32, (8, width), 0)
    for group in range(GRP_DEV):
        mine = jnp.where(sub == group * AMP + lane, acc, 0.0)
        sens_ref[group : group + 1, :] = jnp.sum(mine, axis=0, keepdims=True)[:, :AMP]


def last_step_kernel(fm, inv, mu2, coef0, e2, products, out_hbm, dz, stage, fmc, out_sems):
    rows, width = coef0.shape[1:]
    blocks = width // SEG
    size = rows // blocks
    scaled_matrix(fm, fmc)
    fmv = matrix_rows(fmc, width)
    stencil_products(dz, mu2, e2, products)

    def send(j):
        at = pl.ds(pl.multiple_of(j * 8, 8), 8)
        return pltpu.make_async_copy(stage.at[:, at, :], out_hbm.at[:, at, :], out_sems.at[j])

    def third(j, c):
        for half in range(size // 8):
            r0 = j * size + half * 8
            made = [step_row(mu2, dz, coef0, fmv, inv[r0 + i], r0 + i) for i in range(8)]
            at = pl.ds(pl.multiple_of(r0, 8), 8)
            for e in range(FIELDS):
                turned = jnp.swapaxes(jnp.stack([x[e] for x in made]), 0, 1)
                for pair in range(PAIRS):
                    stage[pair * FIELDS + e, at, :] = turned[pair]
            send(j * (size // 8) + half).start()
        return c

    lax.fori_loop(0, blocks, third, 0)
    for j in range(rows // 8):
        send(j).wait()


def shift_pairs(devices, k):
    return [(i, (i + k) % devices) for i in range(devices)]


def round_over(x, axis, bit):
    return x + lax.ppermute(x, axis, [(i, i ^ bit) for i in range(lax.axis_size(axis))])


def to_neighbours(send_a, send_b, cycle):
    return (
        lax.ppermute(send_a, "blk", [(i, i ^ 1) for i in range(cycle)]),
        lax.ppermute(
            send_b,
            "blk",
            [(i, (i + 1) % cycle if i % 2 else (i - 1) % cycle) for i in range(cycle)],
        ),
    )


def on_device(checkpoints, owner, flux_matrix, row_link, blade_group, forcing):
    n_out = lax.axis_size("out")
    cycle = lax.axis_size("blk")
    rows, width = forcing.shape[1], forcing.shape[2]
    blocks = width // SEG
    step_rows = rows // blocks
    slot = checkpoints[0]

    def struct(shape, kind=F32):
        return jax.ShapeDtypeStruct(shape, kind)

    sems = pltpu.SemaphoreType.DMA
    field = struct((FIELDS, rows, width))
    strip = struct((FIELDS * SLOT, rows), BF16)
    factors = struct((5, PAIRS, width))
    slots = [slot] + [lax.ppermute(slot, "out", shift_pairs(n_out, k)) for k in range(1, n_out)]

    def stay(x):
        return pltpu.with_memory_space_constraint(x, pltpu.HBM)

    def call(kernel, out_shape, smem, hbm, vmem, scratch, limit, flops, name, out_specs=None):
        return pl.pallas_call(
            kernel,
            out_shape=out_shape,
            in_specs=[SMEM] * len(smem) + [HBM] * len(hbm) + [VMEM] * len(vmem),
            out_specs=out_specs or (VMEM,) * len(out_shape),
            scratch_shapes=scratch,
            compiler_params=pltpu.CompilerParams(vmem_limit_bytes=limit),
            cost_estimate=cost(flops, 10**6),
            name=name,
        )(*map(stay, smem), *map(stay, hbm), *vmem)

    kept = (
        forcing, row_link, forcing_select(width), slot, state_select(width),
        *halo_selects(width), stencil_selects(width),
    )
    made = (
        factors, factors, field, field, strip, strip,
        struct((rows,), jnp.int32), struct(owner.shape, jnp.int32), struct(flux_matrix.shape),
    )
    made += tuple(struct(x.shape, x.dtype) for x in kept)
    k, kp, b0, v0, f_a, f_b, inv, owner_s, fm_s, *held = call(
        functools.partial(prepare_kernel, cycle),
        made,
        (blade_group, row_link[0], owner, flux_matrix),
        kept,
        (),
        [sems((len(kept),))],
        SMALL_LIMIT,
        10**8,
        "prepare",
        (VMEM,) * 6 + (SMEM,) * 3 + (VMEM,) * len(kept),
    )
    forcing_v, link, _, slot_v, state_sel, *held = held
    forcing_tiled, state_tiled, edge, state_edge, products = held
    f_sent = (f_a, f_b, *to_neighbours(f_a, f_b, cycle))

    q_a, q_b, *chosen = call(
        functools.partial(strips_kernel, n_out),
        (strip, strip) + (struct(slot.shape, slot.dtype),) * STEPS,
        (owner_s,),
        (),
        (slot_v, *slots[1:], state_sel),
        [],
        SMALL_LIMIT,
        10**7,
        "strips",
    )
    q_sent = (q_a, q_b, *to_neighbours(q_a, q_b, cycle))

    coefficients = struct((2 * FIELDS - 1, rows, width))
    y, fe, hot, bs, coef0, coef1, weighted, heavy, z = call(
        functools.partial(halo_forcing_kernel, cycle),
        (
            struct((16, FIELDS, step_rows, width)), field, struct((3 * rows, rows), BF16),
            struct((4, FIELDS, rows, width)), coefficients, coefficients, field, field,
            struct((PAIRS, width)),
        ),
        (fm_s,),
        (),
        (link, *f_sent, forcing_tiled, edge, forcing_v, v0, *chosen),
        [
            pltpu.VMEM((blocks * 4 * SLOT, forcing_tiled.shape[1]), BF16),
            pltpu.SMEM((FIELDS, FIELDS), F32),
        ],
        SMALL_LIMIT,
        10**8,
        "halo_forcing",
    )
    flat = rows * FIELDS * PAIRS
    edges = (step_rows * FIELDS * 8, width)
    halo_operands = (*q_sent, state_tiled, state_edge, kp, hot, y)
    halo_scratch = [
        pltpu.VMEM(edges, F32),
        pltpu.VMEM((FIELDS, rows, width), F32),
        like(y),
        pltpu.VMEM((blocks * 4 * SLOT, state_tiled.shape[1]), BF16),
        pltpu.VMEM((FIELDS, step_rows, width), F32),
        pltpu.SMEM((FIELDS, FIELDS), F32),
    ]

    def halo_and_first_steps(fm, inv, *refs):
        halo_in, refs = refs[: len(halo_operands)], refs[len(halo_operands) :]
        forcing, fe, b0, k_ref, products, *ready = refs[:10]
        mu2, sens, e2, e1, qe, *work = refs[10 : 13 + len(halo_scratch)]
        halo_kernel(fm, *halo_in, e1, e2, qe, *work)
        first_steps_kernel(
            cycle, fm, inv, forcing, fe, b0, qe, k_ref, products, e1, *ready,
            mu2, sens, *refs[13 + len(halo_scratch) :],
        )

    mu2, sens, e2 = call(
        halo_and_first_steps,
        (struct((flat, width)), struct((GRP_DEV, AMP)), struct(edges)),
        (fm_s, inv),
        (),
        (*halo_operands, forcing_v, fe, b0, k, products, bs, coef1, weighted, heavy, z),
        halo_scratch
        + [
            pltpu.VMEM((flat, width), F32),
            pltpu.VMEM((flat, 2 * width), F32),
            pltpu.VMEM((FIELDS, rows, width), F32),
            pltpu.SMEM((FIELDS, FIELDS), F32),
        ],
        VMEM_LIMIT,
        10**9,
        "first_steps",
    )

    pairs_fields = PAIRS * FIELDS
    bits = [1 << i for i in reversed(range(cycle.bit_length() - 1))]
    exact = 1 << len(bits) == cycle
    if not exact:
        sens = lax.psum(sens, "blk")
    if exact and bits:
        sens = round_over(sens, "blk", bits.pop(0))
    (adjoint,) = call(
        last_step_kernel,
        (struct((pairs_fields, rows, width)),),
        (fm_s, inv),
        (),
        (mu2, coef0, e2, products),
        [
            pltpu.VMEM((flat, 2 * width), F32),
            pltpu.VMEM((pairs_fields, rows, width), F32),
            pltpu.SMEM((FIELDS, FIELDS), F32),
            sems((rows // 8,)),
        ],
        VMEM_LIMIT,
        10**9,
        "last_step",
        (HBM,),
    )
    for bit in bits if exact else ():
        sens = round_over(sens, "blk", bit)
    return adjoint.reshape(GRP_DEV, AMP, FIELDS, rows, width), sens


def solution(mesh):
    return jax.shard_map(
        on_device,
        mesh=mesh,
        in_specs=(P("out", None, None, "blk"), P(), P(), P("blk", None), P(), P(None, None, "blk")),
        out_specs=(P("out", None, None, None, "blk"), P("out", None)),
        check_vma=False,
    )
```
